32 devices in a mesh: dp: 8 (over y, x, core), expert: 4 (over z).
Axes of the slice: x: 2, y: 2, z: 4, core: 2. Of those that a mesh axis runs over, the one named last changes fastest.
Arguments:
- tokens: bfloat16 [10240, 2048], P(('dp', 'expert')), may hold values from -6 to 6
- cotangent: bfloat16 [10240, 2048], P(('dp', 'expert')), may hold values from -6 to 6
- norm_gains: bfloat16 [2, 2048], P(None, ('dp', 'expert')), may hold values from 0.25 to 1.75
- qkv_weight: bfloat16 [2048, 6144], P(('dp', 'expert')), may hold values from -0.125 to 0.125
- out_weight: bfloat16 [2048, 2048], P(('dp', 'expert')), may hold values from -1.5 to 1.5
- router_weight: bfloat16 [2048, 16], P(('dp', 'expert')), may hold values from -0.046875 to 0.046875
- adapter_down: bfloat16 [2048, 8, 3, 16], P(('dp', 'expert')), may hold values from -0.125 to 0.125
- adapter_qkv: bfloat16 [8, 16, 6144], P(None, None, ('dp', 'expert')), may hold values from -1.5 to 1.5
- adapter_out: bfloat16 [8, 16, 2048], P(None, None, ('dp', 'expert')), may hold values from -6 to 6
- adapter_router: bfloat16 [128, 16], P(('dp', 'expert')), may hold values from -0.5 to 0.5
- expert_input: bfloat16 [16, 2048, 2048], P('expert', 'dp'), may hold values from -0.125 to 0.125
- expert_output: bfloat16 [16, 1024, 2048], P('expert', 'dp'), may hold values from -5 to 5
- expert_down: bfloat16 [16, 2048, 8, 16], P('expert', 'dp'), may hold values from -0.125 to 0.125
- expert_lift: bfloat16 [16, 8, 16, 2048], P('expert', None, None, 'dp'), may hold values from -1.5 to 1.5
- routes: int32 [10240, 8], P(('dp', 'expert')), may hold values from 0 to 15, all different within a row; in each aligned block of 320 rows (0 to 319, 320 to 639, ...) at most 240 rows name the same one
- adapter_ids: int32 [8], P('dp'), may hold values from 0 to 7
- cont_lengths: int32 [8, 8], P('dp'), may hold values from 1 to 64, 256 in all within a row
Outputs:
- layer_output: bfloat16 [10240, 2048], P(('dp', 'expert'))
- input_grad: bfloat16 [10240, 2048], P(('dp', 'expert'))
- down_grad: float32 [2048, 8, 3, 16], P(('dp', 'expert'))
- qkv_grad: float32 [8, 16, 6144], P(None, None, ('dp', 'expert'))
- proj_grad: float32 [8, 16, 2048], P(None, None, ('dp', 'expert'))
- router_grad: float32 [128, 16], P(('dp', 'expert'))
- expdown_grad: float32 [16, 2048, 8, 16], P('expert', 'dp')
- explift_grad: float32 [16, 8, 16, 2048], P('expert', None, None, 'dp')
The draws below stay inside these ranges and needn't reach their ends.
Inputs may be any that keep to these rules, and one draw needn't show every extreme that they name: `routes`: each row names 8 different experts; among the rows of one device no expert is named more than 240 times, a bound that some block reaches. `cont_lengths`: each group's lengths sum to 256, the longest exactly 64.
All inputs are finite; a program needn't handle non-finite values.
Results may differ from the reference program's by a relative error of at most 0.022.
Values may be sent and summed in bfloat16 or wider, within the bound.
A program may use at most 448 MiB of HBM per device.

```python
import math
import jax
import jax.numpy as jnp
import numpy as np
from jax import lax

D = 2048
HEADS = 16
HEAD = 128
FF = 1024
TOPK = 8
RANK = 16
ADAPTERS = 8
PROMPT = 1024
NCONT = 8
CONT = 32
EXPERTS = 16
GROUP_TOK = 1280
TOK = 320
GROUPS = 8
TOKENS = 10240
CAP = 240


def set_ends(drawn, key, low, top_value):
    index_at = [jax.random.randint(jax.random.fold_in(key, axis), (), 0, length) for axis, length in enumerate(drawn.shape)]
    widest = drawn.shape.index(max(drawn.shape))
    neighbour = index_at[:widest] + [(index_at[widest] + 1) % drawn.shape[widest]] + index_at[widest + 1:]
    return drawn.at[tuple(index_at)].set(low).at[tuple(neighbour)].set(top_value)


def shard_levels(key, shape, pieces, low, high):
    factor_of = 1.0
    for position, blocks in pieces:
        heights = jax.random.uniform(jax.random.fold_in(jax.random.fold_in(key, 6), position), (blocks,), jnp.float32, low / len(pieces), high / len(pieces))
        factor_of = factor_of * jnp.repeat(jnp.exp(heights), shape[position] // blocks).reshape((-1,) + (1,) * (len(shape) - 1 - position))
    return factor_of


def split_up(amount, total, bound, skew):
    loads = [(1 << 20) // math.isqrt(rank ** skew) + 1 for rank in range(2, amount + 1)]
    rest, counts = total - bound - (amount - 1), [1] * (amount - 1)
    while rest > 0:
        candidates = [i for i in range(amount - 1) if counts[i] < bound]
        mass, remaining = sum([loads[i] for i in candidates]), rest
        for i in candidates:
            more = min(bound - counts[i], max(1, remaining * loads[i] // mass), rest)
            counts[i] = counts[i] + more
            rest = rest - more
    return np.array([bound] + counts)


def ragged_sizes(rng, number_of, total, most, slope):
    if number_of == 2:
        one = jax.random.randint(rng, (), max(1, total - most), min(most, total - 1) + 1)
        return jnp.stack([one, total - one])
    tallies = jnp.asarray(split_up(number_of, total, most, slope), jnp.int32)
    twos = (number_of - 1) // 2
    giver, receiver = tallies[1:1 + 2 * twos:2], tallies[2:2 + 2 * twos:2]
    room = jnp.minimum(giver - 1, most - receiver)
    moved = jax.random.randint(jax.random.fold_in(rng, 1), (twos,), 0, 1 << 20) % (room + 1)
    tallies = tallies.at[1:1 + 2 * twos:2].set(giver - moved).at[2:2 + 2 * twos:2].set(receiver + moved)
    return tallies[jax.random.permutation(jax.random.fold_in(rng, 2), number_of)]


def routed_block(stream_key, own, number, rows, amount, top, bound, skew):
    ranking = jax.random.permutation(stream_key, amount)
    crowded, ordinary = shares(amount, rows * top, bound, skew, True), shares(amount, rows * top, bound, skew, False)
    places = jnp.arange(amount)

    def named(sizes, rotation):
        used = int((sizes > 0).sum())
        fixed = max(1, used // 4)
        moved = fixed + (places - fixed + rotation * (used - fixed)) % max(1, amount - fixed)
        return jnp.zeros((amount,), jnp.int32).at[ranking[jnp.where(places < fixed, places, moved)]].set(jnp.asarray(sizes, jnp.int32))

    sizes = jnp.where(number % 4 == 0, named(crowded, number // 4), named(ordinary, number - number // 4 - 1))
    mixed = jax.random.permutation(jax.random.fold_in(own, 3), amount)
    donor, taker = mixed[0:amount // 2 * 2:2], mixed[1:amount // 2 * 2:2]
    room = jnp.minimum(sizes[donor] - 1, bound - sizes[taker]) // 2
    room = jnp.where((donor == ranking[0]) | (taker == ranking[0]) | (sizes[taker] == 0), 0, jnp.maximum(room, 0))
    moved = jax.random.randint(jax.random.fold_in(own, 4), (amount // 2,), 0, 1 << 20) % (room + 1)
    sizes = sizes.at[donor].add(-moved).at[taker].add(moved)
    members = jnp.searchsorted(jnp.cumsum(sizes), jnp.arange(rows * top), side="right").astype(jnp.int32)
    listing = members.reshape(top, rows).T
    listing = listing[jax.random.permutation(jax.random.fold_in(own, 1), rows)]
    rotation = jax.random.randint(jax.random.fold_in(own, 2), (rows, 1), 0, top)
    return jnp.take_along_axis(listing, (jnp.arange(top)[None, :] + rotation) % top, axis=1)


def shares(count, total, limit, lean, full):
    portions = [(1 << 20) // math.isqrt(rank ** lean) + 1 for rank in range(1, count + 1)]
    largest = limit if full else min(limit, max(-(-total // count), total * portions[0] // sum(portions)))
    least = 1 if total - largest >= count - 1 else 0
    counts, surplus = [largest] + [least] * (count - 1), total - largest - least * (count - 1)
    while surplus > 0:
        movable = [i for i in range(1, count) if counts[i] < largest] or [i for i in range(1, count) if counts[i] < limit]
        pool, budget = sum([portions[i] for i in movable]), surplus
        for i in movable:
            extra = min(limit - counts[i], max(1, budget * portions[i] // pool), surplus)
            counts[i] = counts[i] + extra
            surplus = surplus - extra
    return np.array(counts)


def gaussian(rng, dims, deviation, limit, split=(), kind=jnp.bfloat16):
    entries = jax.random.normal(rng, dims, jnp.float32) * deviation
    if len(split) > 0:
        entries = shard_levels(rng, dims, split, -0.22, 0.18) * entries
    return jnp.clip(entries, min=-limit, max=limit).astype(kind)


def setup_inputs(seed: int = 0) -> dict:
    arg_keys = jax.random.split(jax.random.key(seed), 18)
    tokens = gaussian(arg_keys[0], (TOKENS, D), 1.0, 6.0, ((0, 32),))
    cotangent = gaussian(arg_keys[1], (TOKENS, D), 1.0, 6.0, ((0, 32),))
    norm_gains = jnp.clip(1.0 + 0.15 * jax.random.normal(arg_keys[2], (2, D), jnp.float32), 0.25, 1.75).astype(jnp.bfloat16)
    qkv_weight = gaussian(arg_keys[3], (D, 3 * D), D ** -0.5, 0.125, ((0, 32),))
    out_weight = gaussian(arg_keys[4], (D, D), 16 ** -0.5, 1.5, ((0, 32),))
    router_weight = gaussian(arg_keys[5], (D, EXPERTS), (8 * D) ** -0.5, 0.046875, ((0, 32),))
    adapter_down = gaussian(arg_keys[6], (D, ADAPTERS, 3, RANK), D ** -0.5, 0.125, ((0, 32),))
    adapter_qkv = gaussian(arg_keys[7], (ADAPTERS, RANK, 3 * D), RANK ** -0.5, 1.5, ((2, 32),))
    adapter_out = gaussian(arg_keys[8], (ADAPTERS, RANK, D), 1.25, 6.0, ((2, 32),))
    adapter_router = gaussian(arg_keys[9], (ADAPTERS * RANK, EXPERTS), (8 * RANK) ** -0.5, 0.5, ((0, 32),))
    expert_input = gaussian(arg_keys[10], (EXPERTS, D, 2 * FF), D ** -0.5, 0.125, ((0, 4), (1, 8)))
    expert_output = gaussian(arg_keys[11], (EXPERTS, FF, D), 0.35, 5.0, ((0, 4), (1, 8)))
    expert_down = gaussian(arg_keys[12], (EXPERTS, D, ADAPTERS, RANK), D ** -0.5, 0.125, ((0, 4), (1, 8)))
    expert_lift = gaussian(arg_keys[13], (EXPERTS, ADAPTERS, RANK, 2 * FF), RANK ** -0.5, 1.5, ((0, 4), (3, 8)))
    routes_keys = jax.random.split(jax.random.fold_in(arg_keys[14], 1), TOKENS // TOK)
    routes_turns = jax.random.permutation(jax.random.fold_in(arg_keys[14], 3), TOKENS // TOK)
    routes = jax.vmap(lambda own, number: routed_block(jax.random.fold_in(arg_keys[14], 2), own, number, TOK, EXPERTS, TOPK, CAP, 2))(routes_keys, routes_turns).reshape((TOKENS, TOPK))
    adapter_ids = set_ends(jax.random.randint(arg_keys[15], (GROUPS,), 0, ADAPTERS), jax.random.fold_in(arg_keys[15], 1), 0, ADAPTERS - 1).astype(jnp.int32)
    cont_lengths = jax.vmap(lambda own: ragged_sizes(own, NCONT, NCONT * CONT, 2 * CONT, 2))(jax.random.split(arg_keys[16], GROUPS)).reshape((GROUPS, NCONT)).astype(jnp.int32)
    return dict(tokens=tokens, cotangent=cotangent, norm_gains=norm_gains, qkv_weight=qkv_weight, out_weight=out_weight, router_weight=router_weight, adapter_down=adapter_down, adapter_qkv=adapter_qkv, adapter_out=adapter_out, adapter_router=adapter_router, expert_input=expert_input, expert_output=expert_output, expert_down=expert_down, expert_lift=expert_lift, routes=routes, adapter_ids=adapter_ids, cont_lengths=cont_lengths)


EPSILON = 1e-05
MASKED = -1e+30
HIGHEST = lax.Precision.HIGHEST

@jax.custom_vjp
def low(v):
    return lax.optimization_barrier(v.astype(jnp.bfloat16)).astype(jnp.float32)

@jax.custom_vjp
def low_back(v):
    return v

def low_keep(v):
    return (low(v), None)

def low_pass(kept, grad):
    return (grad,)

def back_keep(v):
    return (v, None)

def back_low(kept, grad):
    return (low(grad),)
low.defvjp(low_keep, low_pass)
low_back.defvjp(back_keep, back_low)

def matmul(left, right):
    return jnp.dot(left, right, precision=HIGHEST)

def rms_norm(values, gain_row):
    return values * lax.rsqrt(lax.optimization_barrier(jnp.mean(values * values, axis=-1, keepdims=True)) + EPSILON) * gain_row

def softmax_last(scores):
    top = lax.optimization_barrier(jnp.max(scores, axis=-1, keepdims=True))
    expd = jnp.exp(scores - top)
    return expd / lax.optimization_barrier(jnp.sum(expd, axis=-1, keepdims=True))

def segment_of(lengths):
    places = jnp.arange(GROUP_TOK, dtype=jnp.int32)
    limits = PROMPT + jnp.cumsum(lengths, dtype=jnp.int32)
    passed = lax.optimization_barrier(jnp.sum((places[:, None] >= limits[None, :]).astype(jnp.int32), axis=1, dtype=jnp.int32))
    return (jnp.where(places < PROMPT, 0, 1 + passed).astype(jnp.int32), places)

def group_forward(inputs, route_rows, lengths, adapter, weights):
    gain_rows, qkv_matrix, out_matrix, router_matrix, adapt_down, adapt_qkv, adapt_out, adapt_router, input_matrix, output_matrix, expert_down, expert_lift = weights
    picked = adapt_down[:, adapter]
    normed = low(rms_norm(inputs, gain_rows[0]))
    rank_query = low(low_back(matmul(normed, picked[:, 0])))
    qkv = low(low_back(matmul(normed, qkv_matrix) + matmul(rank_query, adapt_qkv[adapter])))
    queries = qkv[:, :D].reshape(GROUP_TOK, HEADS, HEAD)
    keys = qkv[:, D:2 * D].reshape(GROUP_TOK, HEADS, HEAD)
    values = qkv[:, 2 * D:].reshape(GROUP_TOK, HEADS, HEAD)
    segments, places = segment_of(lengths)
    from_prompt = (segments[None, :] == 0) & (segments[:, None] != 0)
    own_causal = (segments[None, :] == segments[:, None]) & (places[None, :] <= places[:, None])
    allowed = from_prompt | own_causal
    scores = low_back(jnp.einsum('thd,shd->hts', queries, keys, precision=HIGHEST) * HEAD ** (-0.5))
    scores = jnp.where(allowed[None], scores, MASKED)
    probs = low(softmax_last(scores))
    mixed = low(low_back(jnp.einsum('hts,shd->thd', probs, values, precision=HIGHEST).reshape(GROUP_TOK, D)))
    rank_mix = low(low_back(matmul(mixed, picked[:, 1])))
    branch = low_back(matmul(mixed, out_matrix) + matmul(rank_mix, adapt_out[adapter]))
    middle = inputs + branch
    second = low(rms_norm(middle, gain_rows[1]))
    rank_route = low(low_back(matmul(second, picked[:, 2])))
    lift_route = adapt_router.reshape(ADAPTERS, RANK, EXPERTS)[adapter]
    logits = low_back(matmul(second, router_matrix) + matmul(rank_route, lift_route))
    router_probs = softmax_last(logits)
    gates = jnp.take_along_axis(router_probs, route_rows, axis=1)

    def expert_term(expert):
        rows_in = low_back(second)
        rank_expert = low(low_back(matmul(rows_in, expert_down[expert, :, adapter])))
        gate_up = low_back(matmul(rows_in, input_matrix[expert]) + matmul(rank_expert, expert_lift[expert, adapter]))
        gate_part = gate_up[:, :FF]
        hidden = low(gate_part * jax.nn.sigmoid(gate_part) * gate_up[:, FF:])
        expert_out = low(low_back(matmul(hidden, output_matrix[expert])))
        weight_col = lax.optimization_barrier(jnp.sum(jnp.where(route_rows == expert, gates, 0.0), axis=1))
        return weight_col[:, None] * expert_out
    terms = lax.map(jax.checkpoint(expert_term), jnp.arange(EXPERTS, dtype=jnp.int32))
    return middle + lax.optimization_barrier(jnp.sum(terms, axis=0))

def reference(tokens, cotangent, norm_gains, qkv_weight, out_weight, router_weight, adapter_down, adapter_qkv, adapter_out, adapter_router, expert_input, expert_output, expert_down, expert_lift, routes, adapter_ids, cont_lengths):

    def widen(array):
        return array.astype(jnp.float32)
    fixed = (widen(norm_gains), widen(qkv_weight), widen(out_weight), widen(router_weight))
    frozen = (widen(expert_input), widen(expert_output))

    def forward(inputs, adapt_down, adapt_qkv, adapt_out, adapt_router, exp_down, exp_lift):
        weights = fixed + (adapt_down, adapt_qkv, adapt_out, adapt_router) + frozen + (exp_down, exp_lift)

        def one_group(packed):
            group_rows, route_rows, lengths, adapter = packed
            return group_forward(group_rows, route_rows, lengths, adapter, weights)
        outputs = lax.map(jax.checkpoint(one_group), (inputs.reshape(GROUPS, GROUP_TOK, D), routes.reshape(GROUPS, GROUP_TOK, TOPK), cont_lengths, adapter_ids))
        return outputs.reshape(TOKENS, D)
    result, pullback = jax.vjp(forward, widen(tokens), widen(adapter_down), widen(adapter_qkv), widen(adapter_out), widen(adapter_router), widen(expert_down), widen(expert_lift))
    grads = pullback(widen(cotangent))
    return (result.astype(jnp.bfloat16), grads[0].astype(jnp.bfloat16), grads[1], grads[2], grads[3], grads[4], grads[5], grads[6])
```

```python
import functools
import jax
import jax.numpy as jnp
from jax import lax
from jax.experimental import pallas as pl
from jax.experimental.pallas import tpu as pltpu
from jax.sharding import PartitionSpec as P

D = 2048
HEAD = 128
FF = 1024
RANK = 16
ADAPTERS = 8
EXP_DEV = 4
PROMPT = 1024
EPSILON = 1e-05
MASKED = -1e30

MESH = pl.DeviceIdType.MESH
ANY = pl.BlockSpec(memory_space=pl.ANY)
VMEM = pl.BlockSpec(memory_space=pltpu.VMEM)


def greet_line(me, parts):
    barrier = pltpu.get_barrier_semaphore()

    @pl.when(me > 0)
    def _():
        pl.semaphore_signal(barrier, inc=1, device_id={"expert": me - 1}, device_id_type=MESH)

    @pl.when(me < parts - 1)
    def _():
        pl.semaphore_signal(barrier, inc=1, device_id={"expert": me + 1}, device_id_type=MESH)

    pl.semaphore_wait(barrier, jnp.where((me > 0) & (me < parts - 1), 2, 1))


def greet_all(me, parts):
    barrier = pltpu.get_barrier_semaphore()
    for k in range(1, parts):
        pl.semaphore_signal(
            barrier, inc=1, device_id={"expert": lax.rem(me + k, parts)}, device_id_type=MESH
        )
    pl.semaphore_wait(barrier, parts - 1)


def gather_kernel(parts, count, *refs):
    srcs, dsts = refs[:count], refs[count : 2 * count]
    own_sem, send_up, recv_up, send_down, recv_down = refs[2 * count :]
    me = lax.axis_index("expert")
    greet_line(me, parts)

    def block(i, origin):
        rows = srcs[i].shape[0]
        return dsts[i].at[pl.ds(pl.multiple_of(origin * rows, rows), rows)]

    def hop(i, src, origin, to, send, recv):
        return pltpu.make_async_remote_copy(
            src_ref=src,
            dst_ref=block(i, origin),
            send_sem=send,
            recv_sem=recv,
            device_id={"expert": to},
            device_id_type=MESH,
        )

    for step in range(parts - 1):
        for up in (True, False):
            origin = me - step if up else me + step
            to = me + 1 if up else me - 1
            send, recv = (send_up, recv_up) if up else (send_down, recv_down)
            has = (origin >= 0) & (origin < parts)
            for i in range(count):
                if step > 0:

                    @pl.when(has)
                    def _(i=i, origin=origin, send=send, recv=recv, step=step):
                        hop(i, block(i, origin), origin, me, send.at[i, step], recv.at[i, step - 1]).wait_recv()

                @pl.when(has & (to >= 0) & (to < parts))
                def _(i=i, origin=origin, to=to, send=send, recv=recv, step=step):
                    src = srcs[i] if step == 0 else block(i, origin)
                    hop(i, src, origin, to, send.at[i, step], recv.at[i, step]).start()

    for i in range(count):
        own = pltpu.make_async_copy(srcs[i], block(i, me), own_sem.at[i])
        own.start()
        own.wait()
    for up in (True, False):
        send, recv = (send_up, recv_up) if up else (send_down, recv_down)
        to = me + 1 if up else me - 1
        last = me - (parts - 1) if up else me + (parts - 1)
        for i in range(count):

            @pl.when((last >= 0) & (last < parts))
            def _(i=i, last=last, send=send, recv=recv):
                hop(i, block(i, last), last, me, send.at[i, 0], recv.at[i, parts - 2]).wait_recv()

            for step in range(parts - 1):
                origin = me - step if up else me + step

                @pl.when((origin >= 0) & (origin < parts) & (to >= 0) & (to < parts))
                def _(i=i, origin=origin, send=send, recv=recv, step=step):
                    hop(i, block(i, origin), origin, me, send.at[i, step], recv.at[i, step]).wait_send()


def line_gather(arrays, cid):
    parts = lax.axis_size("expert")
    n = len(arrays)
    sem = pltpu.SemaphoreType.DMA
    return pl.pallas_call(
        functools.partial(gather_kernel, parts, n),
        out_shape=[jax.ShapeDtypeStruct((parts * a.shape[0],) + a.shape[1:], a.dtype) for a in arrays],
        in_specs=[ANY] * n,
        out_specs=[ANY] * n,
        scratch_shapes=[sem((n,))] + [sem((n, parts - 1))] * 4,
        compiler_params=pltpu.CompilerParams(collective_id=cid, has_side_effects=True),
        name="line_gather_%d" % cid,
    )(*arrays)


def exchange_kernel(parts, count, stack, *refs):
    srcs, dsts = refs[:count], refs[count : 2 * count]
    own_sem, send, recv = refs[2 * count :]
    me = lax.axis_index("expert")
    greet_all(me, parts)

    def piece(i, owner):
        rows = srcs[i].shape[0] // parts
        return srcs[i].at[pl.ds(pl.multiple_of(owner * rows, rows), rows)]

    def place(i, origin):
        rows, cols = srcs[i].shape[0] // parts, srcs[i].shape[1]
        if stack:
            return dsts[i].at[pl.ds(pl.multiple_of(origin * rows, rows), rows)]
        return dsts[i].at[:, pl.ds(pl.multiple_of(origin * cols, cols), cols)]

    copies = []
    for k in list(range(parts - 1, 0, -1)):
        to = lax.rem(me + k, parts)
        for i in range(count):
            copy = pltpu.make_async_remote_copy(
                src_ref=piece(i, to),
                dst_ref=place(i, me),
                send_sem=send.at[i, k - 1],
                recv_sem=recv.at[i, k - 1],
                device_id={"expert": to},
                device_id_type=MESH,
            )
            copy.start()
            copies.append(copy)
    for i in range(count):
        own = pltpu.make_async_copy(piece(i, me), place(i, me), own_sem.at[i])
        own.start()
        own.wait()
    for copy in copies:
        copy.wait_send()
    for k in list(range(parts - 1, 0, -1)):
        origin = lax.rem(me + parts - k, parts)
        for i in range(count):
            pltpu.make_async_remote_copy(
                src_ref=piece(i, me),
                dst_ref=place(i, origin),
                send_sem=send.at[i, k - 1],
                recv_sem=recv.at[i, k - 1],
                device_id={"expert": origin},
                device_id_type=MESH,
            ).wait_recv()


def exchange(arrays, cid, stack=False):
    parts = lax.axis_size("expert")
    n = len(arrays)
    sem = pltpu.SemaphoreType.DMA
    return pl.pallas_call(
        functools.partial(exchange_kernel, parts, n, stack),
        out_shape=[
            jax.ShapeDtypeStruct(
                a.shape if stack else (a.shape[0] // parts, a.shape[1] * parts), a.dtype
            )
            for a in arrays
        ],
        in_specs=[ANY] * n,
        out_specs=[ANY] * n,
        scratch_shapes=[sem((n,)), sem((n, parts - 1)), sem((n, parts - 1))],
        compiler_params=pltpu.CompilerParams(collective_id=cid, has_side_effects=True),
        name="exchange_%d" % cid,
    )(*arrays)


def reduce_kernel(parts, src, out, slot_up, slot_down, send_up, recv_up, send_down, recv_down):
    me = lax.axis_index("expert")
    greet_line(me, parts)
    rows = out.shape[0]
    step_rows = 16

    def term(dest):
        return src.at[pl.ds(pl.multiple_of(dest * rows, rows), rows)]

    def add(into, dest):
        @pl.loop(0, rows // step_rows)
        def _(r):
            here = pl.ds(pl.multiple_of(r * step_rows, step_rows), step_rows)
            there = pl.ds(pl.multiple_of(dest * rows + r * step_rows, step_rows), step_rows)
            total = into[here, :].astype(jnp.float32) + src[there, :].astype(jnp.float32)
            into[here, :] = total.astype(jnp.bfloat16)

    def hop(ref, slot, step, to, send, recv):
        return pltpu.make_async_remote_copy(
            src_ref=ref,
            dst_ref=slot.at[step],
            send_sem=send.at[step],
            recv_sem=recv.at[step],
            device_id={"expert": to},
            device_id_type=MESH,
        )

    streams = ((True, slot_up, send_up, recv_up), (False, slot_down, send_down, recv_down))
    for step in range(parts - 1):
        for up, slot, send, recv in streams:
            line = me if up else parts - 1 - me
            dest_line = parts - 1 - step + line
            dest = dest_line if up else parts - 1 - dest_line
            to = me + 1 if up else me - 1

            @pl.when(line == 0)
            def _(dest=dest, slot=slot, step=step, to=to, send=send, recv=recv):
                hop(term(dest), slot, step, to, send, recv).start()

            if step > 0:

                @pl.when((line > 0) & (step >= line) & (line < parts - 1))
                def _(dest=dest, slot=slot, step=step, to=to, send=send, recv=recv):
                    hop(slot.at[step - 1], slot, step - 1, me, send, recv).wait_recv()
                    add(slot.at[step - 1], dest)
                    hop(slot.at[step - 1], slot, step, to, send, recv).start()

    @pl.loop(0, rows // step_rows)
    def _(r):
        here = pl.ds(pl.multiple_of(r * step_rows, step_rows), step_rows)
        there = pl.ds(pl.multiple_of(me * rows + r * step_rows, step_rows), step_rows)
        out[here, :] = src[there, :].astype(jnp.float32)

    last = parts - 2
    for up, slot, send, recv in streams:
        line = me if up else parts - 1 - me

        @pl.when(line > 0)
        def _(slot=slot, send=send, recv=recv):
            hop(slot.at[last], slot, last, me, send, recv).wait_recv()

            @pl.loop(0, rows // step_rows)
            def _(r):
                here = pl.ds(pl.multiple_of(r * step_rows, step_rows), step_rows)
                out[here, :] = out[here, :] + slot[last, here, :].astype(jnp.float32)

    for up, slot, send, recv in streams:
        line = me if up else parts - 1 - me
        for step in range(parts - 1):

            @pl.when((step >= line) & (line < parts - 1))
            def _(slot=slot, step=step, send=send, recv=recv):
                hop(slot.at[step], slot, step, me, send, recv).wait_send()


def line_reduce(terms, cid):
    parts = lax.axis_size("expert")
    rows, cols = terms.shape[0] // parts, terms.shape[1]
    sem = pltpu.SemaphoreType.DMA
    return pl.pallas_call(
        functools.partial(reduce_kernel, parts),
        out_shape=jax.ShapeDtypeStruct((rows, cols), jnp.float32),
        in_specs=[VMEM],
        out_specs=VMEM,
        scratch_shapes=[pltpu.VMEM((parts - 1, rows, cols), jnp.bfloat16)] * 2 + [sem((parts - 1,))] * 4,
        compiler_params=pltpu.CompilerParams(
            collective_id=cid, has_side_effects=True, vmem_limit_bytes=48 * 1024 * 1024
        ),
        name="line_reduce_%d" % cid,
    )(terms)


def dot_plain(left, right):
    return jnp.dot(left, right, preferred_element_type=jnp.float32)


def dot_left(left, right):
    return lax.dot_general(
        left, right, (((0,), (0,)), ((), ())), preferred_element_type=jnp.float32
    )


def dot_right(left, right):
    return lax.dot_general(
        left, right, (((1,), (1,)), ((), ())), preferred_element_type=jnp.float32
    )


def norm_inverse(values):
    return lax.rsqrt(jnp.mean(values * values, axis=-1, keepdims=True) + EPSILON)


def norm_backward(values, inverse, gain_row, upstream):
    scaled = upstream * gain_row
    return inverse * scaled - values * inverse**3 * jnp.mean(
        scaled * values, axis=-1, keepdims=True
    )


def segments_of(lengths, places):
    upto = jnp.arange(lengths.shape[0])
    limits = PROMPT + jnp.sum(
        jnp.where(upto[:, None] <= upto[None, :], lengths[:, None], 0), axis=0
    )
    passed = jnp.sum((places[:, None] >= limits[None, :]).astype(jnp.int32), axis=1)
    return jnp.where(places < PROMPT, 0, 1 + passed)


def pack_rows(arrays, lanes):
    flat = jnp.concatenate([a.reshape(-1) for a in arrays])
    rows = -(-flat.shape[0] // (16 * lanes)) * 16
    return jnp.pad(flat, (0, rows * lanes - flat.shape[0])).reshape(rows, lanes)


def body(
    tokens,
    cotangent,
    norm_gains,
    qkv_weight,
    out_weight,
    router_weight,
    adapter_down,
    adapter_qkv,
    adapter_out,
    adapter_router,
    expert_input,
    expert_output,
    expert_down,
    expert_lift,
    routes,
    adapter_ids,
    cont_lengths,
):
    low = jnp.bfloat16
    piece = tokens.shape[0]
    parts = lax.axis_size("expert")
    groups = lax.axis_size("dp")
    ways = parts * groups
    me = lax.axis_index("expert")
    total = parts * piece
    experts = EXP_DEV * parts
    width = D // parts
    heads = width // HEAD
    scale = HEAD ** (-0.5)
    share = D // ways
    first = me * piece
    adapter = adapter_ids[0]
    own_hot = (jnp.arange(ADAPTERS, dtype=jnp.int32) == adapter).astype(low)

    qkv_blocks = (
        qkv_weight.reshape(share, 3, parts, width).transpose(2, 0, 1, 3).reshape(parts * share, 3 * width)
    )
    smalls = (
        norm_gains.T,
        router_weight,
        adapter_down,
        adapter_qkv.transpose(2, 0, 1),
        adapter_out.transpose(2, 0, 1),
        adapter_router,
        own_hot,
    )
    small = pack_rows(smalls, 128)
    (qkv_line,) = exchange([qkv_blocks], 0, stack=True)
    small_line, out_line = line_gather([small, out_weight], 1)
    qkv_matrix = lax.all_gather(qkv_line, "dp", axis=0, tiled=True)
    small_all = lax.all_gather(small_line, "dp", axis=0, tiled=True).reshape(ways, -1)
    out_matrix = lax.all_gather(out_line, "dp", axis=0, tiled=True)
    down_rows = expert_down.reshape(EXP_DEV * expert_down.shape[1], ADAPTERS * RANK)
    lift_rows = expert_lift.reshape(EXP_DEV * ADAPTERS * RANK, expert_lift.shape[3])
    down_gathered = lax.all_gather(down_rows, "dp", axis=0, tiled=False)
    lift_gathered = lax.all_gather(lift_rows, "dp", axis=0, tiled=False)
    matrices = [
        (
            lax.all_gather(expert_input[j], "dp", axis=0, tiled=True),
            lax.all_gather(expert_output[j], "dp", axis=0, tiled=True),
        )
        for j in range(EXP_DEV)
    ]

    at = 0
    taken = []
    for a in smalls:
        taken.append(small_all[:, at : at + a.size])
        at += a.size
    gain_rows = taken[0].reshape(D, 2).T.astype(jnp.float32)
    router_matrix = taken[1].reshape(D, experts)
    down_pick = lax.dynamic_index_in_dim(
        taken[2].reshape(D, ADAPTERS, 3, RANK), adapter, 1, keepdims=False
    )
    lift_pick = lax.dynamic_index_in_dim(
        taken[3].reshape(3 * D, ADAPTERS, RANK), adapter, 1, keepdims=False
    )
    lift_own = (
        lax.dynamic_index_in_dim(lift_pick.reshape(3, parts, width, RANK), me, 1, keepdims=False)
        .reshape(3 * width, RANK)
    )
    lift_mix = lax.dynamic_index_in_dim(
        taken[4].reshape(D, ADAPTERS, RANK), adapter, 1, keepdims=False
    )
    lift_route = lax.dynamic_index_in_dim(
        taken[5].reshape(ADAPTERS, RANK, experts), adapter, 0, keepdims=False
    )
    group_hot = taken[6].reshape(groups, parts, ADAPTERS)[:, 0].astype(jnp.float32)
    down_query, down_mix, down_route = down_pick[:, 0], down_pick[:, 1], down_pick[:, 2]
    down_expert = (
        lax.dynamic_slice_in_dim(down_gathered, adapter * RANK, RANK, 2)
        .reshape(groups, EXP_DEV, -1, RANK)
        .transpose(1, 0, 2, 3)
        .reshape(EXP_DEV, D, RANK)
    )
    lift_expert = (
        lax.dynamic_index_in_dim(
            lift_gathered.reshape(groups, EXP_DEV, ADAPTERS, RANK, -1), adapter, 2, keepdims=False
        )
        .transpose(1, 2, 0, 3)
        .reshape(EXP_DEV, RANK, 2 * FF)
    )

    expert_ids = jnp.arange(128, dtype=jnp.int32)
    routed = jnp.any(routes[:, :, None] == expert_ids[None, None, :], axis=1).astype(low)
    tokens_all, routed_all = line_gather([tokens, routed], 2)
    inputs_all = tokens_all.astype(jnp.float32)
    normed_low = (inputs_all * norm_inverse(inputs_all) * gain_rows[0]).astype(low)
    rank_query = dot_plain(normed_low, down_query).astype(low)
    qkv_low = (dot_plain(normed_low, qkv_matrix) + dot_right(rank_query, lift_own)).astype(low)
    queries = qkv_low[:, :width].reshape(total, heads, HEAD)
    key_heads = qkv_low[:, width : 2 * width].reshape(total, heads, HEAD)
    value_heads = qkv_low[:, 2 * width :].reshape(total, heads, HEAD)
    places = jnp.arange(total, dtype=jnp.int32)
    segments = segments_of(cont_lengths[0], places)
    allowed = ((segments[None, :] == 0) & (segments[:, None] != 0)) | (
        (segments[None, :] == segments[:, None]) & (places[None, :] <= places[:, None])
    )
    scores = jnp.einsum("thd,shd->hts", queries, key_heads, preferred_element_type=jnp.float32)
    scores = jnp.where(allowed[None], scores * scale, MASKED)
    top_score = jnp.max(scores, axis=-1, keepdims=True)
    expd = jnp.exp(scores - top_score)
    total_exp = jnp.sum(expd, axis=-1, keepdims=True)
    log_total = top_score + jnp.log(total_exp)
    probs_low = (expd / total_exp).astype(low)
    mixed_heads = (
        jnp.einsum("hts,shd->thd", probs_low, value_heads, preferred_element_type=jnp.float32)
        .reshape(total, width)
        .astype(low)
    )
    (mixed_low,) = exchange([mixed_heads], 3)

    inputs = tokens.astype(jnp.float32)
    upstream = cotangent.astype(jnp.float32)
    rank_mix = dot_plain(mixed_low, down_mix).astype(low)
    middle = inputs + dot_plain(mixed_low, out_matrix) + dot_right(rank_mix, lift_mix)
    inverse_second = norm_inverse(middle)
    second_low = (middle * inverse_second * gain_rows[1]).astype(low)
    second_all, upstream_all = line_gather([second_low, cotangent], 4)

    rank_route_all = dot_plain(second_all, down_route).astype(low)
    logits = dot_plain(second_all, router_matrix) + dot_plain(rank_route_all, lift_route)
    logit_exp = jnp.exp(logits - jnp.max(logits, axis=-1, keepdims=True))
    probs_all = logit_exp / jnp.sum(logit_exp, axis=-1, keepdims=True)
    gates_all = probs_all * routed_all[:, :experts].astype(jnp.float32)
    gates_own = lax.dynamic_slice_in_dim(gates_all, me * EXP_DEV, EXP_DEV, 1)

    output_terms = 0.0
    slot_terms = 0.0
    gate_grads, lift_terms, down_terms = [], [], []
    for j in range(EXP_DEV):
        input_matrix, output_matrix = matrices[j]
        gate_column = gates_own[:, j : j + 1]
        rank_expert = dot_plain(second_all, down_expert[j]).astype(low)
        gate_up = dot_plain(second_all, input_matrix) + dot_plain(rank_expert, lift_expert[j])
        gate_part, up_part = gate_up[:, :FF], gate_up[:, FF:]
        sigma = jax.nn.sigmoid(gate_part)
        hidden = gate_part * sigma * up_part
        output_terms = output_terms + dot_plain((gate_column * hidden).astype(low), output_matrix)
        hidden_grad = dot_right(upstream_all, output_matrix)
        gate_grads.append(jnp.sum(hidden_grad * hidden, axis=1, keepdims=True))
        hidden_grad = hidden_grad * gate_column
        gate_up_grad = jnp.concatenate(
            [
                hidden_grad * up_part * sigma * (1.0 + gate_part * (1.0 - sigma)),
                hidden_grad * gate_part * sigma,
            ],
            axis=-1,
        ).astype(low)
        rank_expert_grad = dot_right(gate_up_grad, lift_expert[j]).astype(low)
        slot_terms = (
            slot_terms
            + dot_right(gate_up_grad, input_matrix)
            + dot_right(rank_expert_grad, down_expert[j])
        )
        lift_terms.append(dot_left(rank_expert, gate_up_grad))
        down_terms.append(dot_left(rank_expert_grad, second_all))

    gate_grad = jnp.concatenate(gate_grads, axis=1)
    gate_grad_wide = lax.dynamic_update_slice(
        jnp.zeros((total, 64), jnp.float32), gate_grad, (0, me * EXP_DEV)
    )
    gate_high = gate_grad_wide.astype(low)
    gate_rest = (gate_grad_wide - gate_high.astype(jnp.float32)).astype(low)
    slot_sum = line_reduce(
        jnp.concatenate([slot_terms.astype(low), gate_high, gate_rest], axis=1), 5
    )
    output_sum = lax.psum_scatter(
        output_terms.astype(low), "expert", scatter_dimension=0, tiled=True
    )
    layer_output = (middle + output_sum.astype(jnp.float32)).astype(low)

    lift_sent = jnp.stack(lift_terms).astype(low).reshape(EXP_DEV * RANK, groups, -1)
    down_sent = jnp.stack(down_terms).astype(low).reshape(EXP_DEV * RANK, groups, -1)
    expert_sent = jnp.concatenate([lift_sent, down_sent], axis=0).transpose(1, 0, 2)
    expert_got = lax.all_to_all(expert_sent, "dp", split_axis=0, concat_axis=0, tiled=True)
    by_adapter = jnp.einsum(
        "ga,gkc->akc", group_hot, expert_got.astype(jnp.float32), precision=lax.Precision.HIGHEST
    ).reshape(ADAPTERS, 2, EXP_DEV, RANK, -1)
    explift_grad = by_adapter[:, 0].transpose(1, 0, 2, 3)
    expdown_grad = by_adapter[:, 1].transpose(1, 3, 0, 2)

    expert_part = slot_sum[:, :D]
    prob_grad = slot_sum[:, D : D + experts] + slot_sum[:, D + 64 : D + 64 + experts]
    router_probs = lax.dynamic_slice_in_dim(probs_all, first, piece, 0)
    rank_route = lax.dynamic_slice_in_dim(rank_route_all, first, piece, 0)
    prob_grad = jnp.where(routed[:, :experts] > 0, prob_grad, 0.0)
    logit_grad = (
        router_probs * (prob_grad - jnp.sum(router_probs * prob_grad, axis=1, keepdims=True))
    ).astype(low)
    rank_route_grad = dot_right(logit_grad, lift_route).astype(low)
    second_grad = (
        expert_part + dot_right(logit_grad, router_matrix) + dot_right(rank_route_grad, down_route)
    )
    lift_route_grad = dot_left(rank_route, logit_grad)
    down_route_grad = dot_left(rank_route_grad, second_low)
    middle_grad = upstream + norm_backward(middle, inverse_second, gain_rows[1], second_grad)
    branch_grad = middle_grad.astype(low)
    rank_mix_grad = dot_plain(branch_grad, lift_mix).astype(low)
    mixed_grad = (dot_right(branch_grad, out_matrix) + dot_right(rank_mix_grad, down_mix)).astype(
        low
    )
    lift_mix_grad = dot_left(rank_mix, branch_grad)
    down_mix_grad = dot_left(rank_mix_grad, mixed_low)

    (mixed_back,) = exchange(
        [mixed_grad.reshape(piece, parts, width).transpose(1, 0, 2).reshape(parts * piece, width)],
        6,
        stack=True,
    )
    grad_heads = mixed_back.reshape(total, heads, HEAD)
    scores = jnp.einsum("thd,shd->hts", queries, key_heads, preferred_element_type=jnp.float32)
    probs = jnp.exp(jnp.where(allowed[None], scores * scale, MASKED) - log_total)
    prob_back = jnp.einsum(
        "thd,shd->hts", grad_heads, value_heads, preferred_element_type=jnp.float32
    )
    delta = jnp.sum(probs * prob_back, axis=-1, keepdims=True)
    score_grad = (probs * (prob_back - delta)).astype(low)
    query_grad = jnp.einsum("hts,shd->thd", score_grad, key_heads, preferred_element_type=jnp.float32)
    key_grad = jnp.einsum("hts,thd->shd", score_grad, queries, preferred_element_type=jnp.float32)
    value_grad = jnp.einsum(
        "hts,thd->shd", probs.astype(low), grad_heads, preferred_element_type=jnp.float32
    )
    qkv_back = jnp.concatenate(
        [
            (query_grad * scale).reshape(total, width),
            (key_grad * scale).reshape(total, width),
            value_grad.reshape(total, width),
        ],
        axis=1,
    ).astype(low)
    rank_query_grad = dot_plain(qkv_back, lift_own).astype(low)
    first_terms = dot_right(qkv_back, qkv_matrix) + dot_right(rank_query_grad, down_query)
    lift_query_grad = dot_left(rank_query, qkv_back)
    down_query_grad = dot_left(rank_query_grad, normed_low)

    lift_query_wide = lax.dynamic_update_slice(
        jnp.zeros((RANK, 3, parts, width), jnp.float32),
        lift_query_grad.reshape(RANK, 3, 1, width),
        (0, 0, me, 0),
    ).reshape(RANK, groups, parts, 3 * share)

    def by_owner(grad):
        return grad.reshape(grad.shape[0], groups, parts, -1)

    def flat_owner(grad):
        return grad.transpose(2, 1, 0, 3).reshape(parts, groups, -1)

    route_flat = jnp.broadcast_to(
        lift_route_grad.reshape(1, 1, RANK * experts), (parts, groups, RANK * experts)
    )
    down_owner = flat_owner(
        by_owner(jnp.concatenate([down_query_grad, down_mix_grad, down_route_grad, lift_mix_grad]))
    )
    owned = jnp.concatenate([down_owner, flat_owner(lift_query_wide), route_flat], axis=2)
    per_group = owned.shape[2]
    owned = owned.reshape(parts, groups * per_group)
    rows = -(-owned.shape[1] // (16 * D)) * 16
    owned = jnp.pad(owned, ((0, 0), (0, rows * D - owned.shape[1]))).reshape(parts, rows, D)
    terms = jnp.concatenate(
        [first_terms.astype(low).reshape(parts, piece, D), owned.astype(low)], axis=1
    ).reshape(parts * (piece + rows), D)
    first_sum = line_reduce(terms, 7)
    first_grad = first_sum[:piece]
    inverse_first = norm_inverse(inputs)
    input_grad = (
        middle_grad + norm_backward(inputs, inverse_first, gain_rows[0], first_grad)
    ).astype(low)

    sent = first_sum[piece:].reshape(-1)[: groups * per_group].reshape(groups, per_group)
    got = lax.all_to_all(sent, "dp", split_axis=0, concat_axis=0, tiled=True)
    summed = jnp.einsum("ga,gk->ak", group_hot, got, precision=lax.Precision.HIGHEST)
    n_down = 4 * RANK * share
    downs = summed[:, :n_down].reshape(ADAPTERS, 4, RANK, share)
    down_grad = downs[:, :3].transpose(3, 0, 1, 2)
    proj_grad = downs[:, 3]
    n_qkv = RANK * 3 * share
    qkv_grad = summed[:, n_down : n_down + n_qkv].reshape(ADAPTERS, RANK, 3 * share)
    router_rows = summed[:, n_down + n_qkv :].reshape(ADAPTERS * RANK, experts)
    own_rows = ADAPTERS * RANK // ways
    router_grad = lax.dynamic_slice_in_dim(
        router_rows, (lax.axis_index("dp") * parts + me) * own_rows, own_rows, 0
    )
    return (
        layer_output,
        input_grad,
        down_grad,
        qkv_grad,
        proj_grad,
        router_grad,
        expdown_grad,
        explift_grad,
    )


def solution(mesh):
    placed = (
        P(("dp", "expert"), None),
        P(("dp", "expert"), None),
        P(None, ("dp", "expert")),
        P(("dp", "expert"), None),
        P(("dp", "expert"), None),
        P(("dp", "expert"), None),
        P(("dp", "expert"), None, None, None),
        P(None, None, ("dp", "expert")),
        P(None, None, ("dp", "expert")),
        P(("dp", "expert"), None),
        P("expert", "dp", None),
        P("expert", "dp", None),
        P("expert", "dp", None, None),
        P("expert", None, None, "dp"),
        P(("dp", "expert"), None),
        P("dp"),
        P("dp", None),
    )
    return jax.shard_map(
        body,
        mesh=mesh,
        in_specs=placed,
        out_specs=(
            P(("dp", "expert"), None),
            P(("dp", "expert"), None),
            P(("dp", "expert"), None, None, None),
            P(None, None, ("dp", "expert")),
            P(None, None, ("dp", "expert")),
            P(("dp", "expert"), None),
            P("expert", "dp", None, None),
            P("expert", None, None, "dp"),
        ),
        check_vma=False,
    )
```

```python
import functools

import jax
import jax.numpy as jnp
from jax import lax
from jax.experimental import pallas as pl
from jax.experimental.pallas import tpu as pltpu
from jax.sharding import PartitionSpec as P

D = 2048
HEAD = 128
FF = 1024
RANK = 16
ADAPTERS = 8
EXP_DEV = 4
PROMPT = 1024
EPSILON = 1e-05
MASKED = -1e30
LANES = 128
BLOCK = 256
ROWS = 1280
TILE = 512
SMALL = 1024

MESH = pl.DeviceIdType.MESH
ANY = pl.BlockSpec(memory_space=pl.ANY)
VMEM = pl.BlockSpec(memory_space=pltpu.VMEM)


def dot_plain(left, right):
    return jnp.dot(left, right, preferred_element_type=jnp.float32)


def dot_left(left, right):
    return lax.dot_general(
        left, right, (((0,), (0,)), ((), ())), preferred_element_type=jnp.float32
    )


def dot_right(left, right):
    return lax.dot_general(
        left, right, (((1,), (1,)), ((), ())), preferred_element_type=jnp.float32
    )


def transfer_cost(elements):
    return pl.CostEstimate(flops=0, bytes_accessed=140 * elements, transcendentals=0)


def greet_line(me, parts):
    barrier = pltpu.get_barrier_semaphore()

    @pl.when(me > 0)
    def _():
        pl.semaphore_signal(barrier, inc=1, device_id={"expert": me - 1}, device_id_type=MESH)

    @pl.when(me < parts - 1)
    def _():
        pl.semaphore_signal(barrier, inc=1, device_id={"expert": me + 1}, device_id_type=MESH)

    pl.semaphore_wait(barrier, jnp.where((me > 0) & (me < parts - 1), 2, 1))


def greet_all(me, parts):
    barrier = pltpu.get_barrier_semaphore()
    for k in range(1, parts):
        pl.semaphore_signal(
            barrier, inc=1, device_id={"expert": lax.rem(me + k, parts)}, device_id_type=MESH
        )
    pl.semaphore_wait(barrier, parts - 1)


def gather_kernel(parts, count, *refs):
    srcs, dsts = refs[:count], refs[count : 2 * count]
    own_sem, send_up, recv_up, send_down, recv_down = refs[2 * count :]
    me = lax.axis_index("expert")
    greet_line(me, parts)

    def block(i, origin):
        rows = srcs[i].shape[0]
        return dsts[i].at[pl.ds(pl.multiple_of(origin * rows, rows), rows)]

    def hop(i, src, origin, to, send, recv):
        return pltpu.make_async_remote_copy(
            src_ref=src,
            dst_ref=block(i, origin),
            send_sem=send,
            recv_sem=recv,
            device_id={"expert": to},
            device_id_type=MESH,
        )

    for step in range(parts - 1):
        for up in (True, False):
            origin = me - step if up else me + step
            to = me + 1 if up else me - 1
            send, recv = (send_up, recv_up) if up else (send_down, recv_down)
            has = (origin >= 0) & (origin < parts)
            for i in range(count):
                if step > 0:

                    @pl.when(has)
                    def _(i=i, origin=origin, send=send, recv=recv, step=step):
                        hop(i, block(i, origin), origin, me, send.at[i, step], recv.at[i, step - 1]).wait_recv()

                @pl.when(has & (to >= 0) & (to < parts))
                def _(i=i, origin=origin, to=to, send=send, recv=recv, step=step):
                    src = srcs[i] if step == 0 else block(i, origin)
                    hop(i, src, origin, to, send.at[i, step], recv.at[i, step]).start()

    for i in range(count):
        own = pltpu.make_async_copy(srcs[i], block(i, me), own_sem.at[i])
        own.start()
        own.wait()
    for up in (True, False):
        send, recv = (send_up, recv_up) if up else (send_down, recv_down)
        to = me + 1 if up else me - 1
        last = me - (parts - 1) if up else me + (parts - 1)
        for i in range(count):

            @pl.when((last >= 0) & (last < parts))
            def _(i=i, last=last, send=send, recv=recv):
                hop(i, block(i, last), last, me, send.at[i, 0], recv.at[i, parts - 2]).wait_recv()

            for step in range(parts - 1):
                origin = me - step if up else me + step

                @pl.when((origin >= 0) & (origin < parts) & (to >= 0) & (to < parts))
                def _(i=i, origin=origin, send=send, recv=recv, step=step):
                    hop(i, block(i, origin), origin, me, send.at[i, step], recv.at[i, step]).wait_send()


def line_gather(arrays, cid):
    parts = lax.axis_size("expert")
    n = len(arrays)
    sem = pltpu.SemaphoreType.DMA
    return pl.pallas_call(
        functools.partial(gather_kernel, parts, n),
        out_shape=[jax.ShapeDtypeStruct((parts * a.shape[0],) + a.shape[1:], a.dtype) for a in arrays],
        in_specs=[ANY] * n,
        out_specs=[ANY] * n,
        scratch_shapes=[sem((n,))] + [sem((n, parts - 1))] * 4,
        cost_estimate=transfer_cost(parts * sum(a.size for a in arrays)),
        compiler_params=pltpu.CompilerParams(collective_id=cid, has_side_effects=True),
        name="line_gather_%d" % cid,
    )(*arrays)


def exchange_kernel(parts, count, stack, *refs):
    srcs, dsts = refs[:count], refs[count : 2 * count]
    own_sem, send, recv = refs[2 * count :]
    me = lax.axis_index("expert")
    greet_all(me, parts)

    def piece(i, owner):
        rows = srcs[i].shape[0] // parts
        return srcs[i].at[pl.ds(pl.multiple_of(owner * rows, rows), rows)]

    def place(i, origin):
        rows, cols = srcs[i].shape[0] // parts, srcs[i].shape[1]
        if stack:
            return dsts[i].at[pl.ds(pl.multiple_of(origin * rows, rows), rows)]
        return dsts[i].at[:, pl.ds(pl.multiple_of(origin * cols, cols), cols)]

    copies = []
    for k in list(range(parts - 1, 0, -1)):
        to = lax.rem(me + k, parts)
        for i in range(count):
            copy = pltpu.make_async_remote_copy(
                src_ref=piece(i, to),
                dst_ref=place(i, me),
                send_sem=send.at[i, k - 1],
                recv_sem=recv.at[i, k - 1],
                device_id={"expert": to},
                device_id_type=MESH,
            )
            copy.start()
            copies.append(copy)
    for i in range(count):
        own = pltpu.make_async_copy(piece(i, me), place(i, me), own_sem.at[i])
        own.start()
        own.wait()
    for copy in copies:
        copy.wait_send()
    for k in list(range(parts - 1, 0, -1)):
        origin = lax.rem(me + parts - k, parts)
        for i in range(count):
            pltpu.make_async_remote_copy(
                src_ref=piece(i, me),
                dst_ref=place(i, origin),
                send_sem=send.at[i, k - 1],
                recv_sem=recv.at[i, k - 1],
                device_id={"expert": origin},
                device_id_type=MESH,
            ).wait_recv()


def exchange(arrays, cid, stack=False):
    parts = lax.axis_size("expert")
    n = len(arrays)
    sem = pltpu.SemaphoreType.DMA
    return pl.pallas_call(
        functools.partial(exchange_kernel, parts, n, stack),
        out_shape=[
            jax.ShapeDtypeStruct(
                a.shape if stack else (a.shape[0] // parts, a.shape[1] * parts), a.dtype
            )
            for a in arrays
        ],
        in_specs=[ANY] * n,
        out_specs=[ANY] * n,
        scratch_shapes=[sem((n,)), sem((n, parts - 1)), sem((n, parts - 1))],
        cost_estimate=transfer_cost(sum(a.size for a in arrays)),
        compiler_params=pltpu.CompilerParams(collective_id=cid, has_side_effects=True),
        name="exchange_%d" % cid,
    )(*arrays)


def reduce_kernel(parts, src, out, slot_up, slot_down, send_up, recv_up, send_down, recv_down):
    me = lax.axis_index("expert")
    greet_line(me, parts)
    rows = out.shape[0]
    step_rows = 16

    def term(dest):
        return src.at[pl.ds(pl.multiple_of(dest * rows, rows), rows)]

    def add(into, dest):
        @pl.loop(0, rows // step_rows)
        def _(r):
            here = pl.ds(pl.multiple_of(r * step_rows, step_rows), step_rows)
            there = pl.ds(pl.multiple_of(dest * rows + r * step_rows, step_rows), step_rows)
            total = into[here, :].astype(jnp.float32) + src[there, :].astype(jnp.float32)
            into[here, :] = total.astype(jnp.bfloat16)

    def hop(ref, slot, step, to, send, recv):
        return pltpu.make_async_remote_copy(
            src_ref=ref,
            dst_ref=slot.at[step],
            send_sem=send.at[step],
            recv_sem=recv.at[step],
            device_id={"expert": to},
            device_id_type=MESH,
        )

    streams = ((True, slot_up, send_up, recv_up), (False, slot_down, send_down, recv_down))
    for step in range(parts - 1):
        for up, slot, send, recv in streams:
            line = me if up else parts - 1 - me
            dest_line = parts - 1 - step + line
            dest = dest_line if up else parts - 1 - dest_line
            to = me + 1 if up else me - 1

            @pl.when(line == 0)
            def _(dest=dest, slot=slot, step=step, to=to, send=send, recv=recv):
                hop(term(dest), slot, step, to, send, recv).start()

            if step > 0:

                @pl.when((line > 0) & (step >= line) & (line < parts - 1))
                def _(dest=dest, slot=slot, step=step, to=to, send=send, recv=recv):
                    hop(slot.at[step - 1], slot, step - 1, me, send, recv).wait_recv()
                    add(slot.at[step - 1], dest)
                    hop(slot.at[step - 1], slot, step, to, send, recv).start()

    @pl.loop(0, rows // step_rows)
    def _(r):
        here = pl.ds(pl.multiple_of(r * step_rows, step_rows), step_rows)
        there = pl.ds(pl.multiple_of(me * rows + r * step_rows, step_rows), step_rows)
        out[here, :] = src[there, :].astype(jnp.float32)

    last = parts - 2
    for up, slot, send, recv in streams:
        line = me if up else parts - 1 - me

        @pl.when(line > 0)
        def _(slot=slot, send=send, recv=recv):
            hop(slot.at[last], slot, last, me, send, recv).wait_recv()

            @pl.loop(0, rows // step_rows)
            def _(r):
                here = pl.ds(pl.multiple_of(r * step_rows, step_rows), step_rows)
                out[here, :] = out[here, :] + slot[last, here, :].astype(jnp.float32)

    for up, slot, send, recv in streams:
        line = me if up else parts - 1 - me
        for step in range(parts - 1):

            @pl.when((step >= line) & (line < parts - 1))
            def _(slot=slot, step=step, send=send, recv=recv):
                hop(slot.at[step], slot, step, me, send, recv).wait_send()


def line_reduce(terms, cid):
    parts = lax.axis_size("expert")
    rows, cols = terms.shape[0] // parts, terms.shape[1]
    sem = pltpu.SemaphoreType.DMA
    return pl.pallas_call(
        functools.partial(reduce_kernel, parts),
        out_shape=jax.ShapeDtypeStruct((rows, cols), jnp.float32),
        in_specs=[VMEM],
        out_specs=VMEM,
        scratch_shapes=[pltpu.VMEM((parts - 1, rows, cols), jnp.bfloat16)] * 2 + [sem((parts - 1,))] * 4,
        cost_estimate=transfer_cost(terms.size),
        compiler_params=pltpu.CompilerParams(
            collective_id=cid, has_side_effects=True, vmem_limit_bytes=48 * 1024 * 1024
        ),
        name="line_reduce_%d" % cid,
    )(terms)


def weights_kernel(parts, blocks, out, small, dst, own_sem, send, recv, send_up, recv_up, send_down, recv_down):
    me = lax.axis_index("expert")
    share = out.shape[0]
    wide = blocks.shape[1]
    greet_all(me, parts)

    def rows(origin):
        return pl.ds(pl.multiple_of(origin * share, share), share)

    def exchanged(k, to, origin):
        return pltpu.make_async_remote_copy(
            src_ref=blocks.at[rows(to)],
            dst_ref=dst.at[rows(origin), :wide],
            send_sem=send.at[k - 1],
            recv_sem=recv.at[k - 1],
            device_id={"expert": to},
            device_id_type=MESH,
        )

    shared = ((out, wide), (small, wide + out.shape[1]))

    def place(i, origin):
        src, at = shared[i]
        return dst.at[rows(origin), at : at + src.shape[1]]

    def hop(i, src, origin, to, send_sem, recv_sem):
        return pltpu.make_async_remote_copy(
            src_ref=src,
            dst_ref=place(i, origin),
            send_sem=send_sem,
            recv_sem=recv_sem,
            device_id={"expert": to},
            device_id_type=MESH,
        )

    streams = ((1, send_up, recv_up), (-1, send_down, recv_down))
    for step in range(parts - 1):
        for way, sends, recvs in streams:
            origin, to = me - way * step, me + way
            has = (origin >= 0) & (origin < parts)
            for i in range(2):
                if step > 0:

                    @pl.when(has)
                    def _(i=i, origin=origin, sends=sends, recvs=recvs, step=step):
                        hop(i, place(i, origin), origin, me, sends.at[i, step], recvs.at[i, step - 1]).wait_recv()

                @pl.when(has & (to >= 0) & (to < parts))
                def _(i=i, origin=origin, to=to, sends=sends, recvs=recvs, step=step):
                    src = shared[i][0] if step == 0 else place(i, origin)
                    hop(i, src, origin, to, sends.at[i, step], recvs.at[i, step]).start()

        if step == 0:
            for k in range(parts - 1, 0, -1):
                to = lax.rem(me + k, parts)
                exchanged(k, to, me).start()

    for i in range(3):
        src, target = (
            (blocks.at[rows(me)], dst.at[rows(me), :wide]) if i == 2 else (shared[i][0], place(i, me))
        )
        own = pltpu.make_async_copy(src, target, own_sem.at[i])
        own.start()
        own.wait()
    for way, sends, recvs in streams:
        to, last = me + way, me - way * (parts - 1)
        for i in range(2):

            @pl.when((last >= 0) & (last < parts))
            def _(i=i, last=last, sends=sends, recvs=recvs):
                hop(i, place(i, last), last, me, sends.at[i, 0], recvs.at[i, parts - 2]).wait_recv()

            for step in range(parts - 1):
                origin = me - way * step

                @pl.when((origin >= 0) & (origin < parts) & (to >= 0) & (to < parts))
                def _(i=i, origin=origin, sends=sends, recvs=recvs, step=step):
                    hop(i, place(i, origin), origin, me, sends.at[i, step], recvs.at[i, step]).wait_send()

    for k in range(parts - 1, 0, -1):
        exchanged(k, lax.rem(me + k, parts), me).wait_send()
        exchanged(k, me, lax.rem(me + parts - k, parts)).wait_recv()


def gather_weights(blocks, out, small, cid):
    parts = lax.axis_size("expert")
    sem = pltpu.SemaphoreType.DMA
    cols = blocks.shape[1] + out.shape[1] + small.shape[1]
    return pl.pallas_call(
        functools.partial(weights_kernel, parts),
        out_shape=jax.ShapeDtypeStruct((blocks.shape[0], cols), blocks.dtype),
        in_specs=[ANY] * 3,
        out_specs=ANY,
        scratch_shapes=[sem((3,)), sem((parts - 1,)), sem((parts - 1,))] + [sem((2, parts - 1))] * 4,
        cost_estimate=transfer_cost(blocks.shape[0] * cols),
        compiler_params=pltpu.CompilerParams(collective_id=cid, has_side_effects=True),
        name="gather_weights",
    )(blocks, out, small)


def diagonal_mask(column_ref, row_ref, block):
    here = pl.ds(block * BLOCK, BLOCK)
    seg_query = column_ref[here, :]
    seg_key = row_ref[:, here]
    shape = (BLOCK, BLOCK)
    causal = lax.broadcasted_iota(jnp.int32, shape, 1) <= lax.broadcasted_iota(jnp.int32, shape, 0)
    same = (seg_query == seg_key) & causal
    return same | ((seg_key == 0) & (seg_query != 0))


def masked_scores(query, key_ref, column_ref, row_ref, block):
    scale = HEAD ** (-0.5)
    here = pl.ds(block * BLOCK, BLOCK)
    own = dot_right(query, key_ref[here, :]) * scale
    own = jnp.where(diagonal_mask(column_ref, row_ref, block), own, MASKED)
    if block == 0:
        return own
    ahead = dot_right(query, key_ref[: block * BLOCK, :]) * scale
    return jnp.concatenate([ahead, own], axis=1)


def attention_kernel(column_ref, row_ref, query_ref, key_ref, value_ref, mixed_ref, lse_ref):
    total = query_ref.shape[0]
    for block in range(total // BLOCK):
        here = pl.ds(block * BLOCK, BLOCK)
        scores = masked_scores(query_ref[here, :], key_ref, column_ref, row_ref, block)
        top = jnp.max(scores, axis=1, keepdims=True)
        expd = jnp.exp(scores - top)
        mass = jnp.sum(expd, axis=1, keepdims=True)
        probs = (expd / mass).astype(jnp.bfloat16)
        mixed = dot_plain(probs, value_ref[: (block + 1) * BLOCK, :])
        mixed_ref[here, :] = mixed.astype(jnp.bfloat16)
        lse_ref[0, here, :] = top + jnp.log(mass)


def head_specs(total, heads):
    return [
        pl.BlockSpec((total, HEAD), lambda h, part=part: (0, part * heads + h)) for part in range(3)
    ]


def run_attention(column, row, qkv):
    total, heads = qkv.shape[0], qkv.shape[1] // (3 * HEAD)
    whole = pl.BlockSpec(memory_space=pltpu.VMEM)
    return pl.pallas_call(
        attention_kernel,
        grid=(heads,),
        in_specs=[whole, whole] + head_specs(total, heads),
        out_specs=[
            pl.BlockSpec((total, HEAD), lambda h: (0, h)),
            pl.BlockSpec((1, total, 1), lambda h: (h, 0, 0)),
        ],
        out_shape=[
            jax.ShapeDtypeStruct((total, heads * HEAD), jnp.bfloat16),
            jax.ShapeDtypeStruct((heads, total, 1), jnp.float32),
        ],
        compiler_params=pltpu.CompilerParams(
            dimension_semantics=("arbitrary",), vmem_limit_bytes=48 * 1024 * 1024
        ),
        cost_estimate=pl.CostEstimate(
            flops=3 * heads * total * total * HEAD,
            bytes_accessed=8 * total * heads * HEAD,
            transcendentals=heads * total * total // 2,
        ),
        name="attention",
    )(column, row, qkv, qkv, qkv)


def attention_back_kernel(
    column_ref, row_ref, query_ref, key_ref, value_ref, grad_ref, lse_ref, back_query_ref, back_key_ref, back_value_ref, key_acc, value_acc
):
    scale = HEAD ** (-0.5)
    total = query_ref.shape[0]
    key_acc[...] = jnp.zeros_like(key_acc)
    value_acc[...] = jnp.zeros_like(value_acc)
    for block in range(total // BLOCK):
        here = pl.ds(block * BLOCK, BLOCK)
        upto = pl.ds(0, (block + 1) * BLOCK)
        query, grad = query_ref[here, :], grad_ref[here, :]
        scores = masked_scores(query, key_ref, column_ref, row_ref, block)
        probs = jnp.exp(scores - lse_ref[0, here, :])
        prob_back = dot_right(grad, value_ref[upto, :])
        delta = jnp.sum(probs * prob_back, axis=1, keepdims=True)
        score_grad = (probs * (prob_back - delta)).astype(jnp.bfloat16)
        back_query_ref[here, :] = (dot_plain(score_grad, key_ref[upto, :]) * scale).astype(jnp.bfloat16)
        key_acc[upto, :] += dot_left(score_grad, query)
        value_acc[upto, :] += dot_left(probs.astype(jnp.bfloat16), grad)
    back_key_ref[...] = (key_acc[...] * scale).astype(jnp.bfloat16)
    back_value_ref[...] = value_acc[...].astype(jnp.bfloat16)


def run_attention_back(column, row, qkv, grad, lse):
    total, heads = qkv.shape[0], qkv.shape[1] // (3 * HEAD)
    whole = pl.BlockSpec(memory_space=pltpu.VMEM)
    head = pl.BlockSpec((total, HEAD), lambda h: (0, h))
    return pl.pallas_call(
        attention_back_kernel,
        grid=(heads,),
        in_specs=[whole, whole]
        + head_specs(total, heads)
        + [head, pl.BlockSpec((1, total, 1), lambda h: (h, 0, 0))],
        out_specs=[head] * 3,
        out_shape=[jax.ShapeDtypeStruct((total, heads * HEAD), jnp.bfloat16)] * 3,
        scratch_shapes=[pltpu.VMEM((total, HEAD), jnp.float32)] * 2,
        compiler_params=pltpu.CompilerParams(
            dimension_semantics=("arbitrary",), vmem_limit_bytes=48 * 1024 * 1024
        ),
        cost_estimate=pl.CostEstimate(
            flops=8 * heads * total * total * HEAD,
            bytes_accessed=16 * total * heads * HEAD,
            transcendentals=heads * total * total // 2,
        ),
        name="attention_back",
    )(column, row, qkv, qkv, qkv, grad, lse)


def own_lift(lift_ref, j):
    row = lax.broadcasted_iota(jnp.int32, (LANES, TILE), 0)
    own = (row >= j * RANK) & (row < (j + 1) * RANK)
    return jnp.where(own, lift_ref[...].astype(jnp.float32), 0.0).astype(jnp.bfloat16)


def gate_column(gates_ref, here, j):
    shape = (ROWS, LANES)
    mine = lax.broadcasted_iota(jnp.int32, shape, 1) == lax.axis_index("expert") * EXP_DEV + j
    return mine, jnp.sum(
        jnp.where(mine, gates_ref[here, :].astype(jnp.float32), 0.0), axis=1, keepdims=True
    )


def row_chunk(b, rows=None):
    rows = rows or ROWS
    return pl.ds(pl.multiple_of(b * rows, rows), rows)


def forward_kernel(
    rows_ref,
    gates_ref,
    down_ref,
    lift_gate_ref,
    lift_up_ref,
    in_gate_ref,
    in_up_ref,
    out_ref,
    output_ref,
    ranks_ref,
    gate_ref,
    up_ref,
    output_acc,
    stage,
    sem,
):
    j, f = pl.program_id(0), pl.program_id(1)
    total = rows_ref.shape[0]

    @pl.when((j == 0) & (f == 0))
    def _():
        @pl.loop(0, total // ROWS)
        def _(b):
            here = row_chunk(b)
            ranks_ref[here, :] = dot_right(rows_ref[here, :], down_ref[...]).astype(jnp.bfloat16)
            output_acc[here, :] = jnp.zeros((ROWS, D), jnp.float32)

    lift_gate, lift_up = own_lift(lift_gate_ref, j), own_lift(lift_up_ref, j)

    @pl.loop(0, total // ROWS)
    def _(b):
        here = row_chunk(b)
        rows = rows_ref[here, :]
        _, column = gate_column(gates_ref, here, j)
        gate = dot_plain(rows, in_gate_ref[0]) + dot_plain(ranks_ref[here, :], lift_gate)
        up = dot_plain(rows, in_up_ref[0]) + dot_plain(ranks_ref[here, :], lift_up)
        gate_ref[0, here, :] = gate.astype(jnp.bfloat16)
        up_ref[0, here, :] = up.astype(jnp.bfloat16)
        hidden = (column * (gate * jax.nn.sigmoid(gate) * up)).astype(jnp.bfloat16)
        output_acc[here, :] += dot_plain(hidden, out_ref[0])

    @pl.when((j == EXP_DEV - 1) & (f == FF // TILE - 1))
    def _():
        @pl.loop(0, total // stage.shape[0])
        def _(b):
            here = row_chunk(b, stage.shape[0])
            stage[...] = output_acc[here, :].astype(jnp.bfloat16)
            copy = pltpu.make_async_copy(stage, output_ref.at[here], sem)
            copy.start()
            copy.wait()


def weight_specs():
    tiles = FF // TILE
    return [
        pl.BlockSpec((LANES, TILE), lambda j, f: (0, f)),
        pl.BlockSpec((LANES, TILE), lambda j, f: (0, f + tiles)),
        pl.BlockSpec((1, D, TILE), lambda j, f: (j, 0, f)),
        pl.BlockSpec((1, D, TILE), lambda j, f: (j, 0, f + tiles)),
        pl.BlockSpec((1, TILE, D), lambda j, f: (j, f, 0)),
    ]


EXPERT_PARAMS = pltpu.CompilerParams(
    dimension_semantics=("arbitrary", "arbitrary"), vmem_limit_bytes=60 * 1024 * 1024
)


def experts_forward(rows, gates, down, lift, matrix_in, matrix_out):
    total = rows.shape[0]
    kept = pl.BlockSpec((1, total, TILE), lambda j, f: (j, 0, f))
    return pl.pallas_call(
        forward_kernel,
        grid=(EXP_DEV, FF // TILE),
        in_specs=[VMEM] * 3 + weight_specs(),
        out_specs=[
            ANY,
            pl.BlockSpec((total, LANES), lambda j, f: (0, 0), pipeline_mode=pl.Buffered(1)),
            kept,
            kept,
        ],
        out_shape=[
            jax.ShapeDtypeStruct((total, D), jnp.bfloat16),
            jax.ShapeDtypeStruct((total, LANES), jnp.bfloat16),
            jax.ShapeDtypeStruct((EXP_DEV, total, FF), jnp.bfloat16),
            jax.ShapeDtypeStruct((EXP_DEV, total, FF), jnp.bfloat16),
        ],
        scratch_shapes=[
            pltpu.VMEM((total, D), jnp.float32),
            pltpu.VMEM((320, D), jnp.bfloat16),
            pltpu.SemaphoreType.DMA,
        ],
        compiler_params=EXPERT_PARAMS,
        cost_estimate=pl.CostEstimate(
            flops=6 * EXP_DEV * total * D * FF,
            bytes_accessed=EXP_DEV * 6 * D * FF + 8 * total * D,
            transcendentals=EXP_DEV * total * FF,
        ),
        name="experts_forward",
    )(rows, gates, down, lift, lift, matrix_in, matrix_in, matrix_out)


def backward_kernel(
    parts,
    gates_ref,
    ranks_ref,
    down_ref,
    lift_gate_ref,
    lift_up_ref,
    in_gate_ref,
    in_up_ref,
    out_ref,
    gate_ref,
    up_ref,
    *refs,
):
    blocks, refs = refs[:parts], refs[parts:]
    slot_ref, rank_ref, lift_grad_gate_ref, lift_grad_up_ref, upstream, slot_acc, rank_acc, gate_acc, lift_acc, stage, sems = refs
    j, f = pl.program_id(0), pl.program_id(1)
    total = upstream.shape[0]

    @pl.when((j == 0) & (f == 0))
    def _():
        piece = total // parts
        copies = []
        for shift in range(parts):
            owner = lax.rem(lax.axis_index("expert") + parts - shift, parts)
            there = row_chunk(owner, piece)
            copies.append(pltpu.make_async_copy(blocks[shift], upstream.at[there], sems.at[shift]))
        for copy in copies:
            copy.start()

        @pl.loop(0, total // ROWS)
        def _(b):
            here = row_chunk(b)
            slot_acc[here, :] = jnp.zeros((ROWS, D), jnp.float32)
            rank_acc[here, :] = jnp.zeros((ROWS, LANES), jnp.float32)
            gate_acc[here, :] = jnp.zeros((ROWS, LANES), jnp.float32)

        for copy in copies:
            copy.wait()

    lift_acc[...] = jnp.zeros_like(lift_acc)
    lift_gate, lift_up = own_lift(lift_gate_ref, j), own_lift(lift_up_ref, j)

    @pl.loop(0, total // ROWS)
    def _(b):
        here = row_chunk(b)
        mine, column = gate_column(gates_ref, here, j)
        raw = dot_right(upstream[here, :], out_ref[0])
        gate = gate_ref[0, here, :].astype(jnp.float32)
        up = up_ref[0, here, :].astype(jnp.float32)
        sigma = jax.nn.sigmoid(gate)
        silu = gate * sigma
        gate_grad = jnp.sum(raw * (silu * up), axis=1, keepdims=True)
        back = raw * column
        to_gate = (back * up * (sigma + silu * (1.0 - sigma))).astype(jnp.bfloat16)
        to_up = (back * silu).astype(jnp.bfloat16)
        slot_acc[here, :] += dot_right(to_gate, in_gate_ref[0]) + dot_right(to_up, in_up_ref[0])
        rank_acc[here, :] += dot_right(to_gate, lift_gate) + dot_right(to_up, lift_up)
        gate_acc[here, :] += jnp.where(mine, gate_grad, 0.0)
        lift_acc[0] += dot_left(ranks_ref[here, :], to_gate)
        lift_acc[1] += dot_left(ranks_ref[here, :], to_up)

    own = row_chunk(j, RANK)
    lift_grad_gate_ref[0] = lift_acc[0, own, :]
    lift_grad_up_ref[0] = lift_acc[1, own, :]

    @pl.when((j == EXP_DEV - 1) & (f == FF // TILE - 1))
    def _():
        @pl.loop(0, total // stage.shape[0])
        def _(b):
            here = row_chunk(b, stage.shape[0])
            rank_low = rank_acc[here, :].astype(jnp.bfloat16)
            rank_ref[here, :] = rank_low
            slot = slot_acc[here, :] + dot_plain(rank_low, down_ref[...])
            stage[:, :D] = slot.astype(jnp.bfloat16)
            wide = gate_acc[here, :]
            high = wide.astype(jnp.bfloat16).astype(jnp.float32)
            both = high + pltpu.roll(wide - high, LANES // 2, 1)
            stage[:, D:] = both.astype(jnp.bfloat16)
            copy = pltpu.make_async_copy(stage, slot_ref.at[here], sems.at[0])
            copy.start()
            copy.wait()


def experts_backward(blocks, gates, ranks, down, lift, matrix_in, matrix_out, gate, up):
    total, parts = gates.shape[0], len(blocks)
    grad = pl.BlockSpec((1, RANK, TILE), lambda j, f: (j, 0, f))
    kept = pl.BlockSpec((1, total, TILE), lambda j, f: (j, 0, f))
    return pl.pallas_call(
        functools.partial(backward_kernel, parts),
        grid=(EXP_DEV, FF // TILE),
        in_specs=[VMEM] * 3 + weight_specs() + [kept, kept] + [ANY] * parts,
        out_specs=[
            ANY,
            pl.BlockSpec((total, LANES), lambda j, f: (0, 0), pipeline_mode=pl.Buffered(1)),
            grad,
            grad,
        ],
        out_shape=[
            jax.ShapeDtypeStruct((total, D + LANES), jnp.bfloat16),
            jax.ShapeDtypeStruct((total, LANES), jnp.bfloat16),
            jax.ShapeDtypeStruct((EXP_DEV, RANK, FF), jnp.float32),
            jax.ShapeDtypeStruct((EXP_DEV, RANK, FF), jnp.float32),
        ],
        scratch_shapes=[
            pltpu.VMEM((total, D), jnp.bfloat16),
            pltpu.VMEM((total, D), jnp.float32),
            pltpu.VMEM((total, LANES), jnp.float32),
            pltpu.VMEM((total, LANES), jnp.float32),
            pltpu.VMEM((2, LANES, TILE), jnp.float32),
            pltpu.VMEM((320, D + LANES), jnp.bfloat16),
            pltpu.SemaphoreType.DMA((parts,)),
        ],
        compiler_params=EXPERT_PARAMS,
        cost_estimate=pl.CostEstimate(
            flops=8 * EXP_DEV * total * D * FF,
            bytes_accessed=EXP_DEV * 6 * D * FF + 8 * total * D,
            transcendentals=EXP_DEV * total * FF,
        ),
        name="experts_backward",
    )(gates, ranks, down, lift, lift, matrix_in, matrix_in, matrix_out, gate, up, *blocks)


def norm_inverse(values):
    return lax.rsqrt(jnp.mean(values * values, axis=-1, keepdims=True) + EPSILON)


def norm_backward(values, inverse, gain_row, upstream):
    scaled = upstream * gain_row
    return inverse * scaled - values * inverse**3 * jnp.mean(
        scaled * values, axis=-1, keepdims=True
    )


def segments_of(lengths, places):
    upto = jnp.arange(lengths.shape[0])
    limits = PROMPT + jnp.sum(
        jnp.where(upto[:, None] <= upto[None, :], lengths[:, None], 0), axis=0
    )
    passed = jnp.sum((places[:, None] >= limits[None, :]).astype(jnp.int32), axis=1)
    return jnp.where(places < PROMPT, 0, 1 + passed)


def body(
    tokens,
    cotangent,
    norm_gains,
    qkv_weight,
    out_weight,
    router_weight,
    adapter_down,
    adapter_qkv,
    adapter_out,
    adapter_router,
    expert_input,
    expert_output,
    expert_down,
    expert_lift,
    routes,
    adapter_ids,
    cont_lengths,
):
    low = jnp.bfloat16
    piece = tokens.shape[0]
    parts = lax.axis_size("expert")
    groups = lax.axis_size("dp")
    ways = parts * groups
    me = lax.axis_index("expert")
    total = parts * piece
    experts = EXP_DEV * parts
    width = D // parts
    share = D // ways
    route_rows = ADAPTERS * RANK // ways
    adapter = adapter_ids[0]

    adapter_cols = expert_lift.shape[3]
    expert_pairs = jnp.concatenate([expert_down.transpose(0, 2, 3, 1), expert_lift]).reshape(
        2 * EXP_DEV * ADAPTERS * RANK, adapter_cols
    )
    matrix_out = lax.all_gather(expert_output, "dp", axis=1, tiled=True)

    qkv_blocks = (
        qkv_weight.reshape(share, 3, parts, width).transpose(2, 0, 1, 3).reshape(parts * share, 3 * width)
    )

    def columns(array, upto):
        return jnp.pad(array, ((0, share - array.shape[0]), (0, upto - array.shape[1])))

    own_hot = (jnp.arange(ADAPTERS, dtype=jnp.int32) == adapter).astype(low)
    small = jnp.concatenate(
        [
            adapter_down.reshape(share, ADAPTERS * 3 * RANK),
            adapter_out.reshape(ADAPTERS * RANK, share).T,
            columns(router_weight, 32),
            columns(adapter_router, 32),
            columns(norm_gains.T, 8),
            columns(jnp.broadcast_to(own_hot, (share, ADAPTERS)), 56),
            adapter_qkv.reshape(ADAPTERS * RANK, 3, share).transpose(2, 1, 0).reshape(share, 3 * LANES),
        ],
        axis=1,
    )
    dense_line = gather_weights(qkv_blocks, out_weight, small, 0)
    dense_line, matrix_out = lax.optimization_barrier((dense_line, matrix_out))
    dense_all = lax.all_gather(dense_line, "dp", axis=0, tiled=True)
    (tokens_all,) = line_gather([tokens], 1)
    expert_input, expert_pairs, dense_all, tokens_all = lax.optimization_barrier(
        (expert_input, expert_pairs, dense_all, tokens_all)
    )
    pairs_all = lax.all_gather(expert_pairs, "dp", axis=0, tiled=False)
    matrix_in = lax.all_gather(expert_input, "dp", axis=1, tiled=True)
    qkv_matrix = dense_all[:, : 3 * width]
    out_matrix = dense_all[:, 3 * width : 3 * width + D]
    small_at = 3 * width + D

    row = jnp.arange(152, dtype=jnp.int32)[:, None]
    at = jnp.arange(small_at + SMALL, dtype=jnp.int32)[None, :]
    wanted = jnp.where(
        row < 48,
        adapter * 48 + row,
        jnp.where(
            row < 64,
            384 + adapter * RANK + row - 48,
            jnp.where(
                row < 112,
                640 + LANES * ((row - 64) // RANK) + adapter * RANK + (row - 64) % RANK,
                jnp.where(row < 120, 576 + row - 112, 512 + row - 120),
            ),
        ),
    )
    picked = dot_right((at == small_at + wanted).astype(low), dense_all)
    gain_rows = picked[112:114]
    picked = picked.astype(low)
    down_query, down_mix, down_route = picked[:16], picked[16:32], picked[32:48]
    lift_mix = picked[48:64]
    router_rows = picked[120 : 120 + experts]
    lift_query = (
        picked[64:112].reshape(3, RANK, ways, share).transpose(1, 2, 0, 3).reshape(RANK, 3, parts, width)
    )
    lift_query = lax.dynamic_index_in_dim(lift_query, me, 2, keepdims=False).reshape(RANK, 3 * width)
    by_owner = dense_all[:, small_at + 512 : small_at + 512 + LANES].reshape(ways, share, LANES)
    lift_route = lax.dynamic_slice_in_dim(
        by_owner[:, :route_rows, 32 : 32 + experts].reshape(ADAPTERS * RANK, experts),
        adapter * RANK,
        RANK,
        0,
    )
    group_hot = by_owner.reshape(groups, parts, share, LANES)[:, 0, 0, 72 : 72 + ADAPTERS].astype(
        jnp.float32
    )
    pairs = lax.dynamic_index_in_dim(
        pairs_all.reshape(groups, 2, EXP_DEV, ADAPTERS, RANK, adapter_cols), adapter, 3, keepdims=False
    )
    pairs = pairs.transpose(1, 2, 3, 0, 4).reshape(2, EXP_DEV * RANK, D)
    pairs = jnp.pad(pairs, ((0, 0), (0, LANES - EXP_DEV * RANK), (0, 0)))

    def shifted(array, by):
        return lax.ppermute(array, "expert", [(i, (i + by) % parts) for i in range(parts)])

    early, tokens_all = lax.optimization_barrier((cotangent, tokens_all))
    next_cotangent = shifted(early, 1)

    inputs_all = tokens_all.astype(jnp.float32)
    normed_low = (inputs_all * norm_inverse(inputs_all) * gain_rows[0:1]).astype(low)
    rank_query = dot_right(normed_low, down_query).astype(low)
    qkv_low = (dot_plain(normed_low, qkv_matrix) + dot_plain(rank_query, lift_query)).astype(low)
    segments = segments_of(cont_lengths[0], jnp.arange(total, dtype=jnp.int32))
    segment_column, segment_row = segments[:, None], segments[None, :]
    mixed_heads, log_mass = run_attention(segment_column, segment_row, qkv_low)
    (mixed_low,) = exchange([mixed_heads], 3)

    inputs = tokens.astype(jnp.float32)
    upstream = cotangent.astype(jnp.float32)
    rank_mix = dot_right(mixed_low, down_mix).astype(low)
    middle = inputs + dot_plain(mixed_low, out_matrix) + dot_plain(rank_mix, lift_mix)
    inverse_second = norm_inverse(middle)
    second_low = (middle * inverse_second * gain_rows[1:2]).astype(low)
    rank_route = dot_right(second_low, down_route).astype(low)
    logits = dot_right(second_low, router_rows) + dot_plain(rank_route, lift_route)
    logit_exp = jnp.exp(logits - jnp.max(logits, axis=-1, keepdims=True))
    router_probs = logit_exp / jnp.sum(logit_exp, axis=-1, keepdims=True)
    expert_ids = jnp.arange(experts, dtype=jnp.int32)
    routed = jnp.any(routes[:, :, None] == expert_ids[None, None, :], axis=1)
    gates = jnp.where(routed, router_probs, 0.0).astype(low)
    gates = jnp.pad(gates, ((0, 0), (0, LANES - experts)))
    second_low, next_cotangent = lax.optimization_barrier((second_low, next_cotangent))
    second_all, gates_all = line_gather([second_low, gates], 4)

    late, second_all = lax.optimization_barrier((cotangent, second_all))
    cotangents = [cotangent, next_cotangent] + [shifted(late, s) for s in range(2, parts)]
    output_terms, ranks, gate, up = experts_forward(
        second_all, gates_all, pairs[0], pairs[1], matrix_in, matrix_out
    )
    output_sum = lax.psum_scatter(output_terms, "expert", scatter_dimension=0, tiled=True)
    slot_terms, rank_expert_grad, lift_gate_grad, lift_up_grad = experts_backward(
        cotangents, gates_all, ranks, pairs[0], pairs[1], matrix_in, matrix_out, gate, up
    )
    slot_sum = line_reduce(slot_terms, 5)
    layer_output = (middle + output_sum.astype(jnp.float32)).astype(low)

    lift_sent = jnp.concatenate([lift_gate_grad, lift_up_grad], axis=2).reshape(EXP_DEV * RANK, D)
    down_sent = dot_left(rank_expert_grad[:, : EXP_DEV * RANK], second_all)
    expert_sent = (
        jnp.concatenate([lift_sent, down_sent], axis=0)
        .astype(low)
        .reshape(2 * EXP_DEV * RANK, groups, -1)
        .transpose(1, 0, 2)
    )
    expert_got = lax.all_to_all(expert_sent, "dp", split_axis=0, concat_axis=0, tiled=True)
    by_adapter = jnp.einsum(
        "ga,gkc->akc", group_hot, expert_got.astype(jnp.float32), precision=lax.Precision.HIGHEST
    ).reshape(ADAPTERS, 2, EXP_DEV, RANK, -1)
    explift_grad = by_adapter[:, 0].transpose(1, 0, 2, 3)
    expdown_grad = by_adapter[:, 1].transpose(1, 3, 0, 2)

    prob_grad = slot_sum[:, D : D + experts] + slot_sum[:, D + 64 : D + 64 + experts]
    prob_grad = jnp.where(routed, prob_grad, 0.0)
    logit_grad = (
        router_probs * (prob_grad - jnp.sum(router_probs * prob_grad, axis=1, keepdims=True))
    ).astype(low)
    rank_route_grad = dot_right(logit_grad, lift_route).astype(low)
    second_grad = (
        slot_sum[:, :D] + dot_plain(logit_grad, router_rows) + dot_plain(rank_route_grad, down_route)
    )
    middle_grad = upstream + norm_backward(middle, inverse_second, gain_rows[1:2], second_grad)
    branch_grad = middle_grad.astype(low)
    rank_mix_grad = dot_right(branch_grad, lift_mix).astype(low)
    mixed_grad = (dot_right(branch_grad, out_matrix) + dot_plain(rank_mix_grad, down_mix)).astype(low)

    (mixed_back,) = exchange(
        [mixed_grad.reshape(piece, parts, width).transpose(1, 0, 2).reshape(total, width)], 6, stack=True
    )
    back_query, back_key, back_value = run_attention_back(
        segment_column, segment_row, qkv_low, mixed_back, log_mass
    )
    qkv_back = jnp.concatenate([back_query, back_key, back_value], axis=1)
    rank_query_grad = dot_right(qkv_back, lift_query).astype(low)
    first_terms = (dot_right(qkv_back, qkv_matrix) + dot_plain(rank_query_grad, down_query)).astype(low)
    lift_query_grad = lax.dynamic_update_slice(
        jnp.zeros((RANK, 3, parts, width), jnp.float32),
        dot_left(rank_query, qkv_back).reshape(RANK, 3, 1, width),
        (0, 0, me, 0),
    )
    downs = jnp.concatenate(
        [
            dot_left(rank_query_grad, normed_low),
            dot_left(rank_mix_grad, mixed_low),
            dot_left(rank_route_grad, second_low),
            dot_left(rank_mix, branch_grad),
        ]
    )
    owned = jnp.concatenate(
        [
            downs.reshape(4 * RANK, ways, share).transpose(1, 0, 2).reshape(ways, -1),
            lift_query_grad.reshape(RANK, ways, 3 * share).transpose(1, 0, 2).reshape(ways, -1),
            jnp.broadcast_to(dot_left(rank_route, logit_grad).reshape(1, -1), (ways, RANK * experts)),
        ],
        axis=1,
    ).astype(low)
    owned, first_terms = lax.optimization_barrier((owned, first_terms))
    first_grad = line_reduce(first_terms, 7)
    got = lax.all_to_all(owned, ("dp", "expert"), split_axis=0, concat_axis=0, tiled=True)
    got, first_grad = lax.optimization_barrier((got, first_grad))
    inverse_first = norm_inverse(inputs)
    input_grad = (
        middle_grad + norm_backward(inputs, inverse_first, gain_rows[0:1], first_grad)
    ).astype(low)
    summed = jnp.einsum(
        "ga,gek->ak",
        group_hot,
        got.astype(jnp.float32).reshape(groups, parts, -1),
        precision=lax.Precision.HIGHEST,
    )
    n_down, n_qkv = 4 * RANK * share, 3 * RANK * share
    downs = summed[:, :n_down].reshape(ADAPTERS, 4, RANK, share)
    down_grad = downs[:, :3].transpose(3, 0, 1, 2)
    proj_grad = downs[:, 3]
    qkv_grad = summed[:, n_down : n_down + n_qkv].reshape(ADAPTERS, RANK, 3 * share)
    router_grad = lax.dynamic_slice_in_dim(
        summed[:, n_down + n_qkv :].reshape(ADAPTERS * RANK, experts),
        (lax.axis_index("dp") * parts + me) * route_rows,
        route_rows,
        0,
    )
    return (
        layer_output,
        input_grad,
        down_grad,
        qkv_grad,
        proj_grad,
        router_grad,
        expdown_grad,
        explift_grad,
    )


def solution(mesh):
    placed = (
        P(("dp", "expert"), None),
        P(("dp", "expert"), None),
        P(None, ("dp", "expert")),
        P(("dp", "expert"), None),
        P(("dp", "expert"), None),
        P(("dp", "expert"), None),
        P(("dp", "expert"), None, None, None),
        P(None, None, ("dp", "expert")),
        P(None, None, ("dp", "expert")),
        P(("dp", "expert"), None),
        P("expert", "dp", None),
        P("expert", "dp", None),
        P("expert", "dp", None, None),
        P("expert", None, None, "dp"),
        P(("dp", "expert"), None),
        P("dp"),
        P("dp", None),
    )
    return jax.shard_map(
        body,
        mesh=mesh,
        in_specs=placed,
        out_specs=(
            P(("dp", "expert"), None),
            P(("dp", "expert"), None),
            P(("dp", "expert"), None, None, None),
            P(None, None, ("dp", "expert")),
            P(None, None, ("dp", "expert")),
            P(("dp", "expert"), None),
            P("expert", "dp", None, None),
            P("expert", None, None, "dp"),
        ),
        check_vma=False,
    )
```

```python
import functools

import jax
import jax.numpy as jnp
from jax import lax
from jax.experimental import pallas as pl
from jax.experimental.pallas import tpu as pltpu
from jax.sharding import PartitionSpec as P

D = 2048
HEAD = 128
FF = 1024
RANK = 16
ADAPTERS = 8
EXP_DEV = 4
PROMPT = 1024
EPSILON = 1e-05
MASKED = -1e30
LANES = 128
BLOCK = 256
ROWS = 1280
TILE = 512
SMALL = 1024

MESH = pl.DeviceIdType.MESH
ANY = pl.BlockSpec(memory_space=pl.ANY)
VMEM = pl.BlockSpec(memory_space=pltpu.VMEM)


def dot_plain(left, right):
    return jnp.dot(left, right, preferred_element_type=jnp.float32)


def dot_left(left, right):
    return lax.dot_general(
        left, right, (((0,), (0,)), ((), ())), preferred_element_type=jnp.float32
    )


def dot_right(left, right):
    return lax.dot_general(
        left, right, (((1,), (1,)), ((), ())), preferred_element_type=jnp.float32
    )


def transfer_cost(elements):
    return pl.CostEstimate(flops=0, bytes_accessed=140 * elements, transcendentals=0)


def greet_line(me, parts):
    barrier = pltpu.get_barrier_semaphore()

    @pl.when(me > 0)
    def _():
        pl.semaphore_signal(barrier, inc=1, device_id={"expert": me - 1}, device_id_type=MESH)

    @pl.when(me < parts - 1)
    def _():
        pl.semaphore_signal(barrier, inc=1, device_id={"expert": me + 1}, device_id_type=MESH)

    pl.semaphore_wait(barrier, jnp.where((me > 0) & (me < parts - 1), 2, 1))


def greet_all(me, parts):
    barrier = pltpu.get_barrier_semaphore()
    for k in range(1, parts):
        pl.semaphore_signal(
            barrier, inc=1, device_id={"expert": lax.rem(me + k, parts)}, device_id_type=MESH
        )
    pl.semaphore_wait(barrier, parts - 1)


def gather_kernel(parts, pieces, count, *refs):
    srcs, dsts = refs[:count], refs[count : 2 * count]
    own_sem, send_up, recv_up, send_down, recv_down = refs[2 * count :]
    me = lax.axis_index("expert")
    greet_line(me, parts)

    def block(i, origin, piece):
        rows = srcs[i].shape[0] // pieces
        at = origin * srcs[i].shape[0] + piece * rows
        return dsts[i].at[pl.ds(pl.multiple_of(at, rows), rows)]

    def hop(i, src, origin, piece, to, send, recv, step, got):
        n = i * pieces + piece
        return pltpu.make_async_remote_copy(
            src_ref=src,
            dst_ref=block(i, origin, piece),
            send_sem=send.at[n, step],
            recv_sem=recv.at[n, got],
            device_id={"expert": to},
            device_id_type=MESH,
        )

    streams = ((1, send_up, recv_up), (-1, send_down, recv_down))
    for step in range(parts - 1):
        for piece in range(pieces):
            for i in range(count):
                for way, send, recv in streams:
                    origin, to = me - way * step, me + way
                    has = (origin >= 0) & (origin < parts)
                    if step > 0:

                        @pl.when(has)
                        def _(i=i, origin=origin, piece=piece, send=send, recv=recv, step=step):
                            here = block(i, origin, piece)
                            hop(i, here, origin, piece, me, send, recv, step, step - 1).wait_recv()

                    @pl.when(has & (to >= 0) & (to < parts))
                    def _(i=i, origin=origin, piece=piece, to=to, send=send, recv=recv, step=step):
                        rows = srcs[i].shape[0] // pieces
                        src = srcs[i].at[piece * rows : (piece + 1) * rows] if step == 0 else block(i, origin, piece)
                        hop(i, src, origin, piece, to, send, recv, step, step).start()

        if step == 0:
            for i in range(count):
                rows = srcs[i].shape[0]
                there = dsts[i].at[pl.ds(pl.multiple_of(me * rows, rows), rows)]
                pltpu.make_async_copy(srcs[i], there, own_sem.at[i]).start()
    for i in range(count):
        rows = srcs[i].shape[0]
        there = dsts[i].at[pl.ds(pl.multiple_of(me * rows, rows), rows)]
        pltpu.make_async_copy(srcs[i], there, own_sem.at[i]).wait()
    for way, send, recv in streams:
        to, last = me + way, me - way * (parts - 1)
        for i in range(count):
            for piece in range(pieces):

                @pl.when((last >= 0) & (last < parts))
                def _(i=i, piece=piece, last=last, send=send, recv=recv):
                    here = block(i, last, piece)
                    hop(i, here, last, piece, me, send, recv, 0, parts - 2).wait_recv()

                for step in range(parts - 1):
                    origin = me - way * step

                    @pl.when((origin >= 0) & (origin < parts) & (to >= 0) & (to < parts))
                    def _(i=i, piece=piece, origin=origin, send=send, recv=recv, step=step):
                        here = block(i, origin, piece)
                        hop(i, here, origin, piece, me, send, recv, step, step).wait_send()


def line_gather(arrays, cid, pieces=1):
    parts = lax.axis_size("expert")
    n = len(arrays)
    sem = pltpu.SemaphoreType.DMA
    return pl.pallas_call(
        functools.partial(gather_kernel, parts, pieces, n),
        out_shape=[jax.ShapeDtypeStruct((parts * a.shape[0],) + a.shape[1:], a.dtype) for a in arrays],
        in_specs=[ANY] * n,
        out_specs=[ANY] * n,
        scratch_shapes=[sem((n,))] + [sem((n * pieces, parts - 1))] * 4,
        cost_estimate=transfer_cost(parts * sum(a.size for a in arrays)),
        compiler_params=pltpu.CompilerParams(collective_id=cid, has_side_effects=True),
        name="line_gather_%d" % cid,
    )(*arrays)


def exchange_kernel(parts, count, stack, *refs):
    srcs, dsts = refs[:count], refs[count : 2 * count]
    own_sem, send, recv = refs[2 * count :]
    me = lax.axis_index("expert")
    greet_all(me, parts)

    def piece(i, owner):
        rows = srcs[i].shape[0] // parts
        return srcs[i].at[pl.ds(pl.multiple_of(owner * rows, rows), rows)]

    def place(i, origin):
        rows, cols = srcs[i].shape[0] // parts, srcs[i].shape[1]
        if stack:
            return dsts[i].at[pl.ds(pl.multiple_of(origin * rows, rows), rows)]
        return dsts[i].at[:, pl.ds(pl.multiple_of(origin * cols, cols), cols)]

    copies = []
    for k in list(range(parts - 1, 0, -1)):
        to = lax.rem(me + k, parts)
        for i in range(count):
            copy = pltpu.make_async_remote_copy(
                src_ref=piece(i, to),
                dst_ref=place(i, me),
                send_sem=send.at[i, k - 1],
                recv_sem=recv.at[i, k - 1],
                device_id={"expert": to},
                device_id_type=MESH,
            )
            copy.start()
            copies.append(copy)
    for i in range(count):
        own = pltpu.make_async_copy(piece(i, me), place(i, me), own_sem.at[i])
        own.start()
        own.wait()
    for copy in copies:
        copy.wait_send()
    for k in list(range(parts - 1, 0, -1)):
        origin = lax.rem(me + parts - k, parts)
        for i in range(count):
            pltpu.make_async_remote_copy(
                src_ref=piece(i, me),
                dst_ref=place(i, origin),
                send_sem=send.at[i, k - 1],
                recv_sem=recv.at[i, k - 1],
                device_id={"expert": origin},
                device_id_type=MESH,
            ).wait_recv()


def exchange(arrays, cid, stack=False):
    parts = lax.axis_size("expert")
    n = len(arrays)
    sem = pltpu.SemaphoreType.DMA
    return pl.pallas_call(
        functools.partial(exchange_kernel, parts, n, stack),
        out_shape=[
            jax.ShapeDtypeStruct(
                a.shape if stack else (a.shape[0] // parts, a.shape[1] * parts), a.dtype
            )
            for a in arrays
        ],
        in_specs=[ANY] * n,
        out_specs=[ANY] * n,
        scratch_shapes=[sem((n,)), sem((n, parts - 1)), sem((n, parts - 1))],
        cost_estimate=transfer_cost(sum(a.size for a in arrays)),
        compiler_params=pltpu.CompilerParams(collective_id=cid, has_side_effects=True),
        name="exchange_%d" % cid,
    )(*arrays)


def reduce_kernel(parts, pieces, src, out, slot_up, slot_down, send_up, recv_up, send_down, recv_down):
    me = lax.axis_index("expert")
    greet_line(me, parts)
    rows = out.shape[0]
    part = rows // pieces
    step_rows = 16

    def hop(ref, slot, step, piece, to, send, recv):
        return pltpu.make_async_remote_copy(
            src_ref=ref,
            dst_ref=slot.at[step, piece * part : (piece + 1) * part],
            send_sem=send.at[step, piece],
            recv_sem=recv.at[step, piece],
            device_id={"expert": to},
            device_id_type=MESH,
        )

    def landed(slot, step, piece, send, recv):
        return hop(slot.at[step, piece * part : (piece + 1) * part], slot, step, piece, me, send, recv)

    streams = ((True, slot_up, send_up, recv_up), (False, slot_down, send_down, recv_down))
    for step in range(parts - 1):
        for piece in range(pieces):
            for up, slot, send, recv in streams:
                line = me if up else parts - 1 - me
                dest_line = parts - 1 - step + line
                dest = dest_line if up else parts - 1 - dest_line
                to = me + 1 if up else me - 1

                @pl.when(line == 0)
                def _(dest=dest, slot=slot, step=step, piece=piece, to=to, send=send, recv=recv):
                    there = pl.ds(pl.multiple_of(dest * rows + piece * part, part), part)
                    hop(src.at[there], slot, step, piece, to, send, recv).start()

                if step > 0:

                    @pl.when((line > 0) & (step >= line) & (line < parts - 1))
                    def _(dest=dest, slot=slot, step=step, piece=piece, to=to, send=send, recv=recv):
                        landed(slot, step - 1, piece, send, recv).wait_recv()

                        @pl.loop(0, part // step_rows)
                        def _(r):
                            at = piece * part + r * step_rows
                            here = pl.ds(pl.multiple_of(at, step_rows), step_rows)
                            there = pl.ds(pl.multiple_of(dest * rows + at, step_rows), step_rows)
                            both = slot[step - 1, here, :].astype(jnp.float32) + src[there, :].astype(jnp.float32)
                            slot[step - 1, here, :] = both.astype(jnp.bfloat16)

                        sent = slot.at[step - 1, piece * part : (piece + 1) * part]
                        hop(sent, slot, step, piece, to, send, recv).start()

    @pl.loop(0, rows // step_rows)
    def _(r):
        here = pl.ds(pl.multiple_of(r * step_rows, step_rows), step_rows)
        there = pl.ds(pl.multiple_of(me * rows + r * step_rows, step_rows), step_rows)
        out[here, :] = src[there, :].astype(jnp.float32)

    last = parts - 2
    for piece in range(pieces):
        for up, slot, send, recv in streams:
            line = me if up else parts - 1 - me

            @pl.when(line > 0)
            def _(slot=slot, piece=piece, send=send, recv=recv):
                landed(slot, last, piece, send, recv).wait_recv()

                @pl.loop(0, part // step_rows)
                def _(r):
                    here = pl.ds(pl.multiple_of(piece * part + r * step_rows, step_rows), step_rows)
                    out[here, :] = out[here, :] + slot[last, here, :].astype(jnp.float32)

    for up, slot, send, recv in streams:
        line = me if up else parts - 1 - me
        for step in range(parts - 1):
            for piece in range(pieces):

                @pl.when((step >= line) & (line < parts - 1))
                def _(slot=slot, step=step, piece=piece, send=send, recv=recv):
                    landed(slot, step, piece, send, recv).wait_send()


def line_reduce(terms, cid, pieces=1):
    parts = lax.axis_size("expert")
    rows, cols = terms.shape[0] // parts, terms.shape[1]
    sem = pltpu.SemaphoreType.DMA
    return pl.pallas_call(
        functools.partial(reduce_kernel, parts, pieces),
        out_shape=jax.ShapeDtypeStruct((rows, cols), jnp.float32),
        in_specs=[VMEM],
        out_specs=VMEM,
        scratch_shapes=[pltpu.VMEM((parts - 1, rows, cols), jnp.bfloat16)] * 2
        + [sem((parts - 1, pieces))] * 4,
        cost_estimate=transfer_cost(terms.size),
        compiler_params=pltpu.CompilerParams(
            collective_id=cid, has_side_effects=True, vmem_limit_bytes=48 * 1024 * 1024
        ),
        name="line_reduce_%d" % cid,
    )(terms)


def weights_kernel(parts, blocks, out, small, dst, dst_out, own_sem, send, recv, send_up, recv_up, send_down, recv_down):
    me = lax.axis_index("expert")
    share = out.shape[0]
    wide = blocks.shape[1]
    greet_all(me, parts)

    def rows(origin):
        return pl.ds(pl.multiple_of(origin * share, share), share)

    def exchanged(k, to, origin):
        return pltpu.make_async_remote_copy(
            src_ref=blocks.at[rows(to)],
            dst_ref=dst.at[rows(origin), :wide],
            send_sem=send.at[k - 1],
            recv_sem=recv.at[k - 1],
            device_id={"expert": to},
            device_id_type=MESH,
        )

    shared = ((out, dst_out, 0), (small, dst, wide))

    def place(i, origin):
        src, into, at = shared[i]
        return into.at[rows(origin), at : at + src.shape[1]]

    def hop(i, src, origin, to, send_sem, recv_sem):
        return pltpu.make_async_remote_copy(
            src_ref=src,
            dst_ref=place(i, origin),
            send_sem=send_sem,
            recv_sem=recv_sem,
            device_id={"expert": to},
            device_id_type=MESH,
        )

    streams = ((1, send_up, recv_up), (-1, send_down, recv_down))
    for step in range(parts - 1):
        for way, sends, recvs in streams:
            origin, to = me - way * step, me + way
            has = (origin >= 0) & (origin < parts)
            for i in range(2):
                if step > 0:

                    @pl.when(has)
                    def _(i=i, origin=origin, sends=sends, recvs=recvs, step=step):
                        hop(i, place(i, origin), origin, me, sends.at[i, step], recvs.at[i, step - 1]).wait_recv()

                @pl.when(has & (to >= 0) & (to < parts))
                def _(i=i, origin=origin, to=to, sends=sends, recvs=recvs, step=step):
                    src = shared[i][0] if step == 0 else place(i, origin)
                    hop(i, src, origin, to, sends.at[i, step], recvs.at[i, step]).start()

        if step == 0:
            for k in range(parts - 1, 0, -1):
                to = lax.rem(me + k, parts)
                exchanged(k, to, me).start()
            owns = [
                pltpu.make_async_copy(src, target, own_sem.at[i])
                for i, (src, target) in enumerate(
                    (
                        (blocks.at[rows(me)], dst.at[rows(me), :wide]),
                        (out, place(0, me)),
                        (small, place(1, me)),
                    )
                )
            ]
            for copy in owns:
                copy.start()

    for copy in owns:
        copy.wait()
    for way, sends, recvs in streams:
        to, last = me + way, me - way * (parts - 1)
        for i in range(2):

            @pl.when((last >= 0) & (last < parts))
            def _(i=i, last=last, sends=sends, recvs=recvs):
                hop(i, place(i, last), last, me, sends.at[i, 0], recvs.at[i, parts - 2]).wait_recv()

            for step in range(parts - 1):
                origin = me - way * step

                @pl.when((origin >= 0) & (origin < parts) & (to >= 0) & (to < parts))
                def _(i=i, origin=origin, sends=sends, recvs=recvs, step=step):
                    hop(i, place(i, origin), origin, me, sends.at[i, step], recvs.at[i, step]).wait_send()

    for k in range(parts - 1, 0, -1):
        exchanged(k, lax.rem(me + k, parts), me).wait_send()
        exchanged(k, me, lax.rem(me + parts - k, parts)).wait_recv()


def gather_weights(blocks, out, small, cid):
    parts = lax.axis_size("expert")
    sem = pltpu.SemaphoreType.DMA
    rows, cols = blocks.shape[0], blocks.shape[1] + small.shape[1]
    return pl.pallas_call(
        functools.partial(weights_kernel, parts),
        out_shape=[
            jax.ShapeDtypeStruct((rows, cols), blocks.dtype),
            jax.ShapeDtypeStruct((rows, out.shape[1]), blocks.dtype),
        ],
        in_specs=[ANY] * 3,
        out_specs=[ANY] * 2,
        scratch_shapes=[sem((3,)), sem((parts - 1,)), sem((parts - 1,))] + [sem((2, parts - 1))] * 4,
        cost_estimate=transfer_cost(rows * (cols + out.shape[1])),
        compiler_params=pltpu.CompilerParams(collective_id=cid, has_side_effects=True),
        name="gather_weights",
    )(blocks, out, small)


def diagonal_mask(column_ref, row_ref, block):
    here = pl.ds(block * BLOCK, BLOCK)
    seg_query = column_ref[here, :]
    seg_key = row_ref[:, here]
    shape = (BLOCK, BLOCK)
    causal = lax.broadcasted_iota(jnp.int32, shape, 1) <= lax.broadcasted_iota(jnp.int32, shape, 0)
    same = (seg_query == seg_key) & causal
    return same | ((seg_key == 0) & (seg_query != 0))


def masked_scores(query, key_ref, column_ref, row_ref, block):
    scale = HEAD ** (-0.5)
    here = pl.ds(block * BLOCK, BLOCK)
    own = dot_right(query, key_ref[here, :]) * scale
    own = jnp.where(diagonal_mask(column_ref, row_ref, block), own, MASKED)
    if block == 0:
        return own
    ahead = dot_right(query, key_ref[: block * BLOCK, :]) * scale
    return jnp.concatenate([ahead, own], axis=1)


def attention_kernel(column_ref, row_ref, query_ref, key_ref, value_ref, mixed_ref, lse_ref):
    total = query_ref.shape[0]
    for block in range(total // BLOCK):
        here = pl.ds(block * BLOCK, BLOCK)
        scores = masked_scores(query_ref[here, :], key_ref, column_ref, row_ref, block)
        top = jnp.max(scores, axis=1, keepdims=True)
        expd = jnp.exp(scores - top)
        mass = jnp.sum(expd, axis=1, keepdims=True)
        probs = (expd / mass).astype(jnp.bfloat16)
        mixed = dot_plain(probs, value_ref[: (block + 1) * BLOCK, :])
        mixed_ref[here, :] = mixed.astype(jnp.bfloat16)
        lse_ref[0, here, :] = top + jnp.log(mass)


def head_specs(total, heads):
    return [
        pl.BlockSpec((total, HEAD), lambda h, part=part: (0, part * heads + h)) for part in range(3)
    ]


def run_attention(column, row, qkv):
    total, heads = qkv.shape[0], qkv.shape[1] // (3 * HEAD)
    whole = pl.BlockSpec(memory_space=pltpu.VMEM)
    return pl.pallas_call(
        attention_kernel,
        grid=(heads,),
        in_specs=[whole, whole] + head_specs(total, heads),
        out_specs=[
            pl.BlockSpec((total, HEAD), lambda h: (0, h)),
            pl.BlockSpec((1, total, 1), lambda h: (h, 0, 0)),
        ],
        out_shape=[
            jax.ShapeDtypeStruct((total, heads * HEAD), jnp.bfloat16),
            jax.ShapeDtypeStruct((heads, total, 1), jnp.float32),
        ],
        compiler_params=pltpu.CompilerParams(
            dimension_semantics=("arbitrary",), vmem_limit_bytes=48 * 1024 * 1024
        ),
        cost_estimate=pl.CostEstimate(
            flops=3 * heads * total * total * HEAD,
            bytes_accessed=8 * total * heads * HEAD,
            transcendentals=heads * total * total // 2,
        ),
        name="attention",
    )(column, row, qkv, qkv, qkv)


def attention_back_kernel(
    column_ref, row_ref, query_ref, key_ref, value_ref, grad_ref, lse_ref, back_query_ref, back_key_ref, back_value_ref, key_acc, value_acc
):
    scale = HEAD ** (-0.5)
    total = query_ref.shape[0]
    key_acc[...] = jnp.zeros_like(key_acc)
    value_acc[...] = jnp.zeros_like(value_acc)
    for block in range(total // BLOCK):
        here = pl.ds(block * BLOCK, BLOCK)
        upto = pl.ds(0, (block + 1) * BLOCK)
        query, grad = query_ref[here, :], grad_ref[here, :]
        scores = masked_scores(query, key_ref, column_ref, row_ref, block)
        probs = jnp.exp(scores - lse_ref[0, here, :])
        prob_back = dot_right(grad, value_ref[upto, :])
        delta = jnp.sum(probs * prob_back, axis=1, keepdims=True)
        score_grad = (probs * (prob_back - delta)).astype(jnp.bfloat16)
        back_query_ref[here, :] = (dot_plain(score_grad, key_ref[upto, :]) * scale).astype(jnp.bfloat16)
        key_acc[upto, :] += dot_left(score_grad, query)
        value_acc[upto, :] += dot_left(probs.astype(jnp.bfloat16), grad)
    back_key_ref[...] = (key_acc[...] * scale).astype(jnp.bfloat16)
    back_value_ref[...] = value_acc[...].astype(jnp.bfloat16)


def run_attention_back(column, row, qkv, grad, lse):
    total, heads = qkv.shape[0], qkv.shape[1] // (3 * HEAD)
    whole = pl.BlockSpec(memory_space=pltpu.VMEM)
    head = pl.BlockSpec((total, HEAD), lambda h: (0, h))
    return pl.pallas_call(
        attention_back_kernel,
        grid=(heads,),
        in_specs=[whole, whole]
        + head_specs(total, heads)
        + [head, pl.BlockSpec((1, total, 1), lambda h: (h, 0, 0))],
        out_specs=[head] * 3,
        out_shape=[jax.ShapeDtypeStruct((total, heads * HEAD), jnp.bfloat16)] * 3,
        scratch_shapes=[pltpu.VMEM((total, HEAD), jnp.float32)] * 2,
        compiler_params=pltpu.CompilerParams(
            dimension_semantics=("arbitrary",), vmem_limit_bytes=48 * 1024 * 1024
        ),
        cost_estimate=pl.CostEstimate(
            flops=8 * heads * total * total * HEAD,
            bytes_accessed=16 * total * heads * HEAD,
            transcendentals=heads * total * total // 2,
        ),
        name="attention_back",
    )(column, row, qkv, qkv, qkv, grad, lse)


def own_lift(lift_ref, j):
    row = lax.broadcasted_iota(jnp.int32, (LANES, TILE), 0)
    own = (row >= j * RANK) & (row < (j + 1) * RANK)
    return jnp.where(own, lift_ref[...].astype(jnp.float32), 0.0).astype(jnp.bfloat16)


def gate_column(gates_ref, here, j):
    shape = (ROWS, LANES)
    mine = lax.broadcasted_iota(jnp.int32, shape, 1) == lax.axis_index("expert") * EXP_DEV + j
    return mine, jnp.sum(
        jnp.where(mine, gates_ref[here, :].astype(jnp.float32), 0.0), axis=1, keepdims=True
    )


def row_chunk(b, rows=None):
    rows = rows or ROWS
    return pl.ds(pl.multiple_of(b * rows, rows), rows)


def forward_kernel(
    rows_ref,
    gates_ref,
    down_ref,
    lift_gate_ref,
    lift_up_ref,
    in_gate_ref,
    in_up_ref,
    out_ref,
    *refs,
):
    output_ref, ranks_ref, gate_ref, up_ref, output_acc, stage, sems = refs
    j, f = pl.program_id(0), pl.program_id(1)
    total = rows_ref.shape[0]

    @pl.when((j == 0) & (f == 0))
    def _():
        @pl.loop(0, total // ROWS)
        def _(b):
            here = row_chunk(b)
            ranks_ref[here, :] = dot_right(rows_ref[here, :], down_ref[...]).astype(jnp.bfloat16)
            output_acc[here, :] = jnp.zeros((ROWS, D), jnp.float32)

    lift_gate, lift_up = own_lift(lift_gate_ref, j), own_lift(lift_up_ref, j)

    @pl.loop(0, total // ROWS)
    def _(b):
        here = row_chunk(b)
        rows = rows_ref[here, :]
        _, column = gate_column(gates_ref, here, j)
        gate = dot_plain(rows, in_gate_ref[0].reshape(D, TILE)) + dot_plain(ranks_ref[here, :], lift_gate)
        up = dot_plain(rows, in_up_ref[0].reshape(D, TILE)) + dot_plain(ranks_ref[here, :], lift_up)
        gate_ref[0, here, :] = gate.astype(jnp.bfloat16)
        up_ref[0, here, :] = up.astype(jnp.bfloat16)
        hidden = (column * (gate * jax.nn.sigmoid(gate) * up)).astype(jnp.bfloat16)
        output_acc[here, :] += dot_plain(hidden, out_ref[0])

    @pl.when((j == EXP_DEV - 1) & (f == FF // TILE - 1))
    def _():
        def copy(b):
            slot = lax.rem(b, 2)
            here = row_chunk(b, stage.shape[1])
            return pltpu.make_async_copy(stage.at[slot], output_ref.at[here], sems.at[slot])

        steps = total // stage.shape[1]

        @pl.loop(0, steps)
        def _(b):
            @pl.when(b >= 2)
            def _():
                copy(b - 2).wait()

            here = row_chunk(b, stage.shape[1])
            stage[lax.rem(b, 2)] = output_acc[here, :].astype(jnp.bfloat16)
            copy(b).start()

        for b in range(steps - 2, steps):
            copy(b).wait()


def weight_specs(ring, share):
    tiles = FF // TILE
    return [
        pl.BlockSpec((LANES, TILE), lambda j, f: (0, f)),
        pl.BlockSpec((LANES, TILE), lambda j, f: (0, f + tiles)),
        pl.BlockSpec((1, ring, share, TILE), lambda j, f: (j, 0, 0, f)),
        pl.BlockSpec((1, ring, share, TILE), lambda j, f: (j, 0, 0, f + tiles)),
        pl.BlockSpec((1, TILE, D), lambda j, f: (j, f, 0)),
    ]


EXPERT_PARAMS = pltpu.CompilerParams(
    dimension_semantics=("arbitrary", "arbitrary"), vmem_limit_bytes=60 * 1024 * 1024
)


def experts_forward(rows, gates, down, lift, matrix_in, matrix_out):
    total = rows.shape[0]
    kept = pl.BlockSpec((1, total, TILE), lambda j, f: (j, 0, f))
    return pl.pallas_call(
        forward_kernel,
        grid=(EXP_DEV, FF // TILE),
        in_specs=[VMEM] * 3 + weight_specs(*matrix_in.shape[1:2], D // matrix_in.shape[1]),
        out_specs=[
            ANY,
            pl.BlockSpec((total, LANES), lambda j, f: (0, 0), pipeline_mode=pl.Buffered(1)),
            kept,
            kept,
        ],
        out_shape=[
            jax.ShapeDtypeStruct((total, D), jnp.bfloat16),
            jax.ShapeDtypeStruct((total, LANES), jnp.bfloat16),
            jax.ShapeDtypeStruct((EXP_DEV, total, FF), jnp.bfloat16),
            jax.ShapeDtypeStruct((EXP_DEV, total, FF), jnp.bfloat16),
        ],
        scratch_shapes=[
            pltpu.VMEM((total, D), jnp.float32),
            pltpu.VMEM((2, 160, D), jnp.bfloat16),
            pltpu.SemaphoreType.DMA((2,)),
        ],
        compiler_params=EXPERT_PARAMS,
        cost_estimate=pl.CostEstimate(
            flops=6 * EXP_DEV * total * D * FF,
            bytes_accessed=EXP_DEV * 6 * D * FF + 8 * total * D,
            transcendentals=EXP_DEV * total * FF,
        ),
        name="experts_forward",
    )(rows, gates, down, lift, lift, matrix_in, matrix_in, matrix_out)


def backward_kernel(
    parts,
    gates_ref,
    ranks_ref,
    down_ref,
    lift_gate_ref,
    lift_up_ref,
    in_gate_ref,
    in_up_ref,
    out_ref,
    gate_ref,
    up_ref,
    *refs,
):
    blocks, refs = refs[:parts], refs[parts:]
    slot_ref, rank_ref, lift_grad_gate_ref, lift_grad_up_ref, upstream, slot_acc, rank_acc, gate_acc, lift_acc, stage, sems = refs
    j, f = pl.program_id(0), pl.program_id(1)
    total = upstream.shape[0]

    @pl.when((j == 0) & (f == 0))
    def _():
        piece = total // parts
        copies = []
        for shift in range(parts):
            owner = lax.rem(lax.axis_index("expert") + parts - shift, parts)
            there = row_chunk(owner, piece)
            copies.append(pltpu.make_async_copy(blocks[shift], upstream.at[there], sems.at[shift]))
        for copy in copies:
            copy.start()

        @pl.loop(0, total // ROWS)
        def _(b):
            here = row_chunk(b)
            slot_acc[here, :] = jnp.zeros((ROWS, D), jnp.float32)
            rank_acc[here, :] = jnp.zeros((ROWS, LANES), jnp.float32)
            gate_acc[here, :] = jnp.zeros((ROWS, LANES), jnp.float32)

        for copy in copies:
            copy.wait()

    lift_acc[...] = jnp.zeros_like(lift_acc)
    lift_gate, lift_up = own_lift(lift_gate_ref, j), own_lift(lift_up_ref, j)

    @pl.loop(0, total // ROWS)
    def _(b):
        here = row_chunk(b)
        mine, column = gate_column(gates_ref, here, j)
        raw = dot_right(upstream[here, :], out_ref[0])
        gate = gate_ref[0, here, :].astype(jnp.float32)
        up = up_ref[0, here, :].astype(jnp.float32)
        sigma = jax.nn.sigmoid(gate)
        silu = gate * sigma
        gate_grad = jnp.sum(raw * (silu * up), axis=1, keepdims=True)
        back = raw * column
        to_gate = (back * up * (sigma + silu * (1.0 - sigma))).astype(jnp.bfloat16)
        to_up = (back * silu).astype(jnp.bfloat16)
        slot_acc[here, :] += dot_right(to_gate, in_gate_ref[0].reshape(D, TILE)) + dot_right(
            to_up, in_up_ref[0].reshape(D, TILE)
        )
        rank_acc[here, :] += dot_right(to_gate, lift_gate) + dot_right(to_up, lift_up)
        gate_acc[here, :] += jnp.where(mine, gate_grad, 0.0)
        lift_acc[0] += dot_left(ranks_ref[here, :], to_gate)
        lift_acc[1] += dot_left(ranks_ref[here, :], to_up)

    own = row_chunk(j, RANK)
    lift_grad_gate_ref[0] = lift_acc[0, own, :]
    lift_grad_up_ref[0] = lift_acc[1, own, :]

    @pl.when((j == EXP_DEV - 1) & (f == FF // TILE - 1))
    def _():
        def copy(b):
            slot = lax.rem(b, 2)
            here = row_chunk(b, stage.shape[1])
            return pltpu.make_async_copy(stage.at[slot], slot_ref.at[here], sems.at[slot])

        steps = total // stage.shape[1]

        @pl.loop(0, steps)
        def _(b):
            @pl.when(b >= 2)
            def _():
                copy(b - 2).wait()

            here = row_chunk(b, stage.shape[1])
            rank_low = rank_acc[here, :].astype(jnp.bfloat16)
            rank_ref[here, :] = rank_low
            slot = slot_acc[here, :] + dot_plain(rank_low, down_ref[...])
            wide = gate_acc[here, :]
            high = wide.astype(jnp.bfloat16).astype(jnp.float32)
            both = high + pltpu.roll(wide - high, LANES // 2, 1)
            stage[lax.rem(b, 2), :, :D] = slot.astype(jnp.bfloat16)
            stage[lax.rem(b, 2), :, D:] = both.astype(jnp.bfloat16)
            copy(b).start()

        for b in range(steps - 2, steps):
            copy(b).wait()


def experts_backward(blocks, gates, ranks, down, lift, matrix_in, matrix_out, gate, up):
    total, parts = gates.shape[0], len(blocks)
    grad = pl.BlockSpec((1, RANK, TILE), lambda j, f: (j, 0, f))
    kept = pl.BlockSpec((1, total, TILE), lambda j, f: (j, 0, f))
    return pl.pallas_call(
        functools.partial(backward_kernel, parts),
        grid=(EXP_DEV, FF // TILE),
        in_specs=[VMEM] * 3 + weight_specs(*matrix_in.shape[1:2], D // matrix_in.shape[1]) + [kept, kept] + [ANY] * parts,
        out_specs=[
            ANY,
            pl.BlockSpec((total, LANES), lambda j, f: (0, 0), pipeline_mode=pl.Buffered(1)),
            grad,
            grad,
        ],
        out_shape=[
            jax.ShapeDtypeStruct((total, D + LANES), jnp.bfloat16),
            jax.ShapeDtypeStruct((total, LANES), jnp.bfloat16),
            jax.ShapeDtypeStruct((EXP_DEV, RANK, FF), jnp.float32),
            jax.ShapeDtypeStruct((EXP_DEV, RANK, FF), jnp.float32),
        ],
        scratch_shapes=[
            pltpu.VMEM((total, D), jnp.bfloat16),
            pltpu.VMEM((total, D), jnp.float32),
            pltpu.VMEM((total, LANES), jnp.float32),
            pltpu.VMEM((total, LANES), jnp.float32),
            pltpu.VMEM((2, LANES, TILE), jnp.float32),
            pltpu.VMEM((2, 160, D + LANES), jnp.bfloat16),
            pltpu.SemaphoreType.DMA((parts,)),
        ],
        compiler_params=EXPERT_PARAMS,
        cost_estimate=pl.CostEstimate(
            flops=8 * EXP_DEV * total * D * FF,
            bytes_accessed=EXP_DEV * 6 * D * FF + 8 * total * D,
            transcendentals=EXP_DEV * total * FF,
        ),
        name="experts_backward",
    )(gates, ranks, down, lift, lift, matrix_in, matrix_in, matrix_out, gate, up, *blocks)


def pick_kernel(sel_ref, rows_ref, out_ref):
    @pl.when(pl.program_id(0) == 0)
    def _():
        out_ref[...] = jnp.zeros_like(out_ref)

    out_ref[...] += dot_right(sel_ref[...], rows_ref[...])


def pick_rows(chosen, dense, at):
    rows, cols = chosen.shape
    wide = 2 * LANES
    return pl.pallas_call(
        pick_kernel,
        grid=(cols // wide,),
        in_specs=[
            pl.BlockSpec((rows, wide), lambda i: (0, i)),
            pl.BlockSpec((dense.shape[0], wide), lambda i: (0, at // wide + i)),
        ],
        out_specs=pl.BlockSpec((rows, dense.shape[0]), lambda i: (0, 0)),
        out_shape=jax.ShapeDtypeStruct((rows, dense.shape[0]), jnp.float32),
        name="pick_rows",
    )(chosen, dense)


def first_kernel(query_ref, key_ref, value_ref, rank_ref, down_ref, *refs):
    weights, out_ref = refs[:3], refs[3]
    total = dot_right(query_ref[...], weights[0][...]) + dot_right(key_ref[...], weights[1][...])
    total = total + dot_right(value_ref[...], weights[2][...]) + dot_plain(rank_ref[...], down_ref[...])
    out_ref[...] = total.astype(jnp.bfloat16)


def first_products(backs, ranks, down, dense):
    total, width = backs[0].shape
    tile = 512
    weights = [
        pl.BlockSpec((tile, width), lambda i, part=part: (i, part)) for part in range(3)
    ]
    return pl.pallas_call(
        first_kernel,
        grid=(D // tile,),
        in_specs=[VMEM] * 4 + [pl.BlockSpec((RANK, tile), lambda i: (0, i))] + weights,
        out_specs=pl.BlockSpec((total, tile), lambda i: (0, i)),
        out_shape=jax.ShapeDtypeStruct((total, D), jnp.bfloat16),
        compiler_params=pltpu.CompilerParams(vmem_limit_bytes=48 * 1024 * 1024),
        cost_estimate=pl.CostEstimate(
            flops=6 * total * width * D, bytes_accessed=6 * width * D + 2 * total * D, transcendentals=0
        ),
        name="first_products",
    )(*backs, ranks, down, dense, dense, dense)


def norm_inverse(values):
    return lax.rsqrt(jnp.mean(values * values, axis=-1, keepdims=True) + EPSILON)


def norm_backward(values, inverse, gain_row, upstream):
    scaled = upstream * gain_row
    return inverse * scaled - values * inverse**3 * jnp.mean(
        scaled * values, axis=-1, keepdims=True
    )


def segments_of(lengths, places):
    upto = jnp.arange(lengths.shape[0])
    limits = PROMPT + jnp.sum(
        jnp.where(upto[:, None] <= upto[None, :], lengths[:, None], 0), axis=0
    )
    passed = jnp.sum((places[:, None] >= limits[None, :]).astype(jnp.int32), axis=1)
    return jnp.where(places < PROMPT, 0, 1 + passed)


def body(
    tokens,
    cotangent,
    norm_gains,
    qkv_weight,
    out_weight,
    router_weight,
    adapter_down,
    adapter_qkv,
    adapter_out,
    adapter_router,
    expert_input,
    expert_output,
    expert_down,
    expert_lift,
    routes,
    adapter_ids,
    cont_lengths,
):
    low = jnp.bfloat16
    piece = tokens.shape[0]
    parts = lax.axis_size("expert")
    groups = lax.axis_size("dp")
    ways = parts * groups
    me = lax.axis_index("expert")
    total = parts * piece
    experts = EXP_DEV * parts
    width = D // parts
    share = D // ways
    route_rows = ADAPTERS * RANK // ways
    adapter = adapter_ids[0]

    adapter_cols = expert_lift.shape[3]
    pairs_own = jnp.stack([expert_down.transpose(0, 2, 3, 1), expert_lift], axis=1)
    abreast = D // (ADAPTERS * adapter_cols)
    pair_rows = 2 * RANK // abreast
    pairs_own = (
        pairs_own.reshape(EXP_DEV, 2 // abreast, abreast, ADAPTERS, RANK, adapter_cols)
        .transpose(0, 1, 4, 2, 3, 5)
        .reshape(EXP_DEV, pair_rows, D)
    )
    expert_rows = jnp.concatenate([expert_input, pairs_own], axis=1)
    matrix_out = lax.all_gather(expert_output, "dp", axis=1, tiled=True)

    qkv_blocks = (
        qkv_weight.reshape(share, 3, parts, width).transpose(2, 0, 1, 3).reshape(parts * share, 3 * width)
    )

    def columns(array, upto):
        return jnp.pad(array, ((0, share - array.shape[0]), (0, upto - array.shape[1])))

    own_hot = (jnp.arange(ADAPTERS, dtype=jnp.int32) == adapter).astype(low)
    small = jnp.concatenate(
        [
            adapter_down.reshape(share, ADAPTERS * 3 * RANK),
            adapter_out.reshape(ADAPTERS * RANK, share).T,
            columns(router_weight, 32),
            columns(adapter_router, 32),
            columns(norm_gains.T, 8),
            columns(jnp.broadcast_to(own_hot, (share, ADAPTERS)), 56),
            adapter_qkv.reshape(ADAPTERS * RANK, 3, share).transpose(2, 1, 0).reshape(share, 3 * LANES),
        ],
        axis=1,
    )
    dense_line, out_line = gather_weights(qkv_blocks, out_weight, small, 0)
    dense_line, out_line, expert_rows, matrix_out = lax.optimization_barrier(
        (dense_line, out_line, expert_rows, matrix_out)
    )
    dense_all = lax.all_gather(dense_line, "dp", axis=0, tiled=True)
    (tokens_all,) = line_gather([tokens], 1, 2)
    out_matrix = lax.all_gather(out_line, "dp", axis=0, tiled=True)
    matrix_in = lax.all_gather(expert_rows, "dp", axis=1, tiled=True).reshape(EXP_DEV, groups, -1, D)
    qkv_matrix = dense_all[:, : 3 * width]
    small_at = 3 * width

    row = jnp.arange(160, dtype=jnp.int32)[:, None]
    at = jnp.arange(SMALL, dtype=jnp.int32)[None, :]
    wanted = jnp.where(
        row < 48,
        adapter * 48 + row,
        jnp.where(
            row < 64,
            384 + adapter * RANK + row - 48,
            jnp.where(
                row < 112,
                640 + LANES * ((row - 64) // RANK) + adapter * RANK + (row - 64) % RANK,
                jnp.where(row < 120, 576 + row - 112, 512 + row - 120),
            ),
        ),
    )
    picked = pick_rows((at == wanted).astype(low), dense_all, small_at)
    gain_rows = picked[112:114]
    picked = picked.astype(low)
    down_query, down_mix, down_route = picked[:16], picked[16:32], picked[32:48]
    lift_mix = picked[48:64]
    router_rows = picked[120 : 120 + experts]
    lift_query = (
        picked[64:112].reshape(3, RANK, ways, share).transpose(1, 2, 0, 3).reshape(RANK, 3, parts, width)
    )
    lift_query = lax.dynamic_index_in_dim(lift_query, me, 2, keepdims=False).reshape(RANK, 3 * width)
    by_owner = dense_all[:, small_at + 512 : small_at + 512 + LANES].reshape(ways, share, LANES)
    lift_route = lax.dynamic_slice_in_dim(
        by_owner[:, :route_rows, 32 : 32 + experts].reshape(ADAPTERS * RANK, experts),
        adapter * RANK,
        RANK,
        0,
    )
    group_hot = by_owner.reshape(groups, parts, share, LANES)[:, 0, 0, 72 : 72 + ADAPTERS].astype(
        jnp.float32
    )
    def shifted(array, by):
        return lax.ppermute(array, "expert", [(i, (i + by) % parts) for i in range(parts)])

    early, tokens_all = lax.optimization_barrier((cotangent, tokens_all))
    early_shifts, late_shifts = [1], list(range(2, parts))
    moved = {s: shifted(early, s) for s in early_shifts}

    inputs_all = tokens_all.astype(jnp.float32)
    normed_low = (inputs_all * norm_inverse(inputs_all) * gain_rows[0:1]).astype(low)
    rank_query = dot_right(normed_low, down_query).astype(low)
    qkv_low = (dot_plain(normed_low, qkv_matrix) + dot_plain(rank_query, lift_query)).astype(low)
    segments = segments_of(cont_lengths[0], jnp.arange(total, dtype=jnp.int32))
    segment_column, segment_row = segments[:, None], segments[None, :]
    mixed_heads, log_mass = run_attention(segment_column, segment_row, qkv_low)
    (mixed_low,) = exchange([mixed_heads], 3)

    inputs = tokens.astype(jnp.float32)
    upstream = cotangent.astype(jnp.float32)
    rank_mix = dot_right(mixed_low, down_mix).astype(low)
    middle = inputs + dot_plain(mixed_low, out_matrix) + dot_plain(rank_mix, lift_mix)
    inverse_second = norm_inverse(middle)
    second_low = (middle * inverse_second * gain_rows[1:2]).astype(low)
    rank_route = dot_right(second_low, down_route).astype(low)
    logits = dot_right(second_low, router_rows) + dot_plain(rank_route, lift_route)
    logit_exp = jnp.exp(logits - jnp.max(logits, axis=-1, keepdims=True))
    router_probs = logit_exp / jnp.sum(logit_exp, axis=-1, keepdims=True)
    expert_ids = jnp.arange(experts, dtype=jnp.int32)
    routed = jnp.any(routes[:, :, None] == expert_ids[None, None, :], axis=1)
    gates = jnp.where(routed, router_probs, 0.0).astype(low)
    gates = jnp.pad(gates, ((0, 0), (0, LANES - experts)))
    held = lax.optimization_barrier([second_low] + [moved[s] for s in early_shifts])
    second_low = held[0]
    moved.update(zip(early_shifts, held[1:]))
    second_all, gates_all = line_gather([second_low, gates], 4, 2)

    late, second_all = lax.optimization_barrier((cotangent, second_all))
    moved.update({s: shifted(late, s) for s in late_shifts})
    cotangents = [cotangent] + [moved[s] for s in range(1, parts)]
    pairs = jnp.stack(
        [
            lax.dynamic_slice_in_dim(
                matrix_in[:, :, matrix_in.shape[2] - pair_rows :],
                (beside * ADAPTERS + adapter) * adapter_cols,
                adapter_cols,
                3,
            ).reshape(EXP_DEV, groups, 2 // abreast, RANK, adapter_cols)
            for beside in range(abreast)
        ],
        axis=3,
    )
    pairs = pairs.reshape(EXP_DEV, groups, 2, RANK, adapter_cols).transpose(2, 0, 3, 1, 4)
    pairs = pairs.reshape(2, EXP_DEV * RANK, D)
    pairs = jnp.pad(pairs, ((0, 0), (0, LANES - EXP_DEV * RANK), (0, 0)))
    output_terms, ranks, gate, up = experts_forward(
        second_all, gates_all, pairs[0], pairs[1], matrix_in, matrix_out
    )
    output_sum = lax.psum_scatter(output_terms, "expert", scatter_dimension=0, tiled=True)
    slot_terms, rank_expert_grad, lift_gate_grad, lift_up_grad = experts_backward(
        cotangents, gates_all, ranks, pairs[0], pairs[1], matrix_in, matrix_out, gate, up
    )
    slot_sum = line_reduce(slot_terms, 5, 2)

    lift_sent = jnp.concatenate([lift_gate_grad, lift_up_grad], axis=2).reshape(EXP_DEV * RANK, D)
    down_sent = dot_left(rank_expert_grad[:, : EXP_DEV * RANK], second_all)
    expert_sent = (
        jnp.concatenate([lift_sent, down_sent], axis=0)
        .astype(low)
        .reshape(2 * EXP_DEV * RANK, groups, -1)
        .transpose(1, 0, 2)
    )
    expert_got = lax.all_to_all(expert_sent, "dp", split_axis=0, concat_axis=0, tiled=True)
    by_adapter = jnp.einsum(
        "ga,gkc->akc", group_hot, expert_got.astype(jnp.float32), precision=lax.Precision.HIGHEST
    ).reshape(ADAPTERS, 2, EXP_DEV, RANK, -1)
    explift_grad = by_adapter[:, 0].transpose(1, 0, 2, 3)
    expdown_grad = by_adapter[:, 1].transpose(1, 3, 0, 2)

    prob_grad = slot_sum[:, D : D + experts] + slot_sum[:, D + 64 : D + 64 + experts]
    prob_grad = jnp.where(routed, prob_grad, 0.0)
    logit_grad = (
        router_probs * (prob_grad - jnp.sum(router_probs * prob_grad, axis=1, keepdims=True))
    ).astype(low)
    rank_route_grad = dot_right(logit_grad, lift_route).astype(low)
    second_grad = (
        slot_sum[:, :D] + dot_plain(logit_grad, router_rows) + dot_plain(rank_route_grad, down_route)
    )
    middle_grad = upstream + norm_backward(middle, inverse_second, gain_rows[1:2], second_grad)
    branch_grad = middle_grad.astype(low)
    rank_mix_grad = dot_right(branch_grad, lift_mix).astype(low)
    mixed_grad = (dot_right(branch_grad, out_matrix) + dot_plain(rank_mix_grad, down_mix)).astype(low)

    (mixed_back,) = exchange(
        [mixed_grad.reshape(piece, parts, width).transpose(1, 0, 2).reshape(total, width)], 6, stack=True
    )
    back_query, back_key, back_value = run_attention_back(
        segment_column, segment_row, qkv_low, mixed_back, log_mass
    )
    qkv_back = jnp.concatenate([back_query, back_key, back_value], axis=1)
    rank_query_grad = dot_right(qkv_back, lift_query).astype(low)
    first_terms = first_products([back_query, back_key, back_value], rank_query_grad, down_query, dense_all)
    lift_query_grad = lax.dynamic_update_slice(
        jnp.zeros((RANK, 3, parts, width), jnp.float32),
        dot_left(rank_query, qkv_back).reshape(RANK, 3, 1, width),
        (0, 0, me, 0),
    )
    downs = jnp.concatenate(
        [
            dot_left(rank_query_grad, normed_low),
            dot_left(rank_mix_grad, mixed_low),
            dot_left(rank_route_grad, second_low),
            dot_left(rank_mix, branch_grad),
        ]
    )
    owned = jnp.concatenate(
        [
            downs.reshape(4 * RANK, ways, share).transpose(1, 0, 2).reshape(ways, -1),
            lift_query_grad.reshape(RANK, ways, 3 * share).transpose(1, 0, 2).reshape(ways, -1),
            jnp.broadcast_to(dot_left(rank_route, logit_grad).reshape(1, -1), (ways, RANK * experts)),
        ],
        axis=1,
    ).astype(low)
    first_grad = lax.psum_scatter(first_terms, "expert", scatter_dimension=0, tiled=True).astype(jnp.float32)
    got = lax.all_to_all(owned, ("dp", "expert"), split_axis=0, concat_axis=0, tiled=True)
    inverse_first = norm_inverse(inputs)
    input_grad = (
        middle_grad + norm_backward(inputs, inverse_first, gain_rows[0:1], first_grad)
    ).astype(low)
    summed = jnp.einsum(
        "ga,gek->ak",
        group_hot,
        got.astype(jnp.float32).reshape(groups, parts, -1),
        precision=lax.Precision.HIGHEST,
    )
    n_down, n_qkv = 4 * RANK * share, 3 * RANK * share
    downs = summed[:, :n_down].reshape(ADAPTERS, 4, RANK, share)
    down_grad = downs[:, :3].transpose(3, 0, 1, 2)
    proj_grad = downs[:, 3]
    qkv_grad = summed[:, n_down : n_down + n_qkv].reshape(ADAPTERS, RANK, 3 * share)
    router_grad = lax.dynamic_slice_in_dim(
        summed[:, n_down + n_qkv :].reshape(ADAPTERS * RANK, experts),
        (lax.axis_index("dp") * parts + me) * route_rows,
        route_rows,
        0,
    )
    layer_output = (middle + output_sum.astype(jnp.float32)).astype(low)
    return (
        layer_output,
        input_grad,
        down_grad,
        qkv_grad,
        proj_grad,
        router_grad,
        expdown_grad,
        explift_grad,
    )


def solution(mesh):
    placed = (
        P(("dp", "expert"), None),
        P(("dp", "expert"), None),
        P(None, ("dp", "expert")),
        P(("dp", "expert"), None),
        P(("dp", "expert"), None),
        P(("dp", "expert"), None),
        P(("dp", "expert"), None, None, None),
        P(None, None, ("dp", "expert")),
        P(None, None, ("dp", "expert")),
        P(("dp", "expert"), None),
        P("expert", "dp", None),
        P("expert", "dp", None),
        P("expert", "dp", None, None),
        P("expert", None, None, "dp"),
        P(("dp", "expert"), None),
        P("dp"),
        P("dp", None),
    )
    return jax.shard_map(
        body,
        mesh=mesh,
        in_specs=placed,
        out_specs=(
            P(("dp", "expert"), None),
            P(("dp", "expert"), None),
            P(("dp", "expert"), None, None, None),
            P(None, None, ("dp", "expert")),
            P(None, None, ("dp", "expert")),
            P(("dp", "expert"), None),
            P("expert", "dp", None, None),
            P("expert", None, None, "dp"),
        ),
        check_vma=False,
    )
```

```python
import functools

import jax
import jax.numpy as jnp
from jax import lax
from jax.experimental import pallas as pl
from jax.experimental.pallas import tpu as pltpu
from jax.sharding import PartitionSpec as P

D = 2048
HEAD = 128
FF = 1024
RANK = 16
ADAPTERS = 8
EXP_DEV = 4
PROMPT = 1024
EPSILON = 1e-05
MASKED = -1e30
LANES = 128
BLOCK = 256
ROWS = 1280
TILE = 512
SMALL = 1024

MESH = pl.DeviceIdType.MESH
ANY = pl.BlockSpec(memory_space=pl.ANY)
VMEM = pl.BlockSpec(memory_space=pltpu.VMEM)


def dot_plain(left, right):
    return jnp.dot(left, right, preferred_element_type=jnp.float32)


def dot_left(left, right):
    return lax.dot_general(
        left, right, (((0,), (0,)), ((), ())), preferred_element_type=jnp.float32
    )


def dot_right(left, right):
    return lax.dot_general(
        left, right, (((1,), (1,)), ((), ())), preferred_element_type=jnp.float32
    )


def transfer_cost(elements):
    return pl.CostEstimate(flops=0, bytes_accessed=140 * elements, transcendentals=0)


def greet_line(me, parts):
    barrier = pltpu.get_barrier_semaphore()

    @pl.when(me > 0)
    def _():
        pl.semaphore_signal(barrier, inc=1, device_id={"expert": me - 1}, device_id_type=MESH)

    @pl.when(me < parts - 1)
    def _():
        pl.semaphore_signal(barrier, inc=1, device_id={"expert": me + 1}, device_id_type=MESH)

    pl.semaphore_wait(barrier, jnp.where((me > 0) & (me < parts - 1), 2, 1))


def greet_all(me, parts):
    barrier = pltpu.get_barrier_semaphore()
    for k in range(1, parts):
        pl.semaphore_signal(
            barrier, inc=1, device_id={"expert": lax.rem(me + k, parts)}, device_id_type=MESH
        )
    pl.semaphore_wait(barrier, parts - 1)


def gather_kernel(parts, pieces, count, *refs):
    srcs, dsts = refs[:count], refs[count : 2 * count]
    own_sem, send_up, recv_up, send_down, recv_down = refs[2 * count :]
    me = lax.axis_index("expert")
    greet_line(me, parts)

    def block(i, origin, piece):
        rows = srcs[i].shape[0] // pieces
        at = origin * srcs[i].shape[0] + piece * rows
        return dsts[i].at[pl.ds(pl.multiple_of(at, rows), rows)]

    def hop(i, src, origin, piece, to, send, recv, step, got):
        n = i * pieces + piece
        return pltpu.make_async_remote_copy(
            src_ref=src,
            dst_ref=block(i, origin, piece),
            send_sem=send.at[n, step],
            recv_sem=recv.at[n, got],
            device_id={"expert": to},
            device_id_type=MESH,
        )

    streams = ((1, send_up, recv_up), (-1, send_down, recv_down))
    for step in range(parts - 1):
        for piece in range(pieces):
            for i in range(count):
                for way, send, recv in streams:
                    origin, to = me - way * step, me + way
                    has = (origin >= 0) & (origin < parts)
                    if step > 0:

                        @pl.when(has)
                        def _(i=i, origin=origin, piece=piece, send=send, recv=recv, step=step):
                            here = block(i, origin, piece)
                            hop(i, here, origin, piece, me, send, recv, step, step - 1).wait_recv()

                    @pl.when(has & (to >= 0) & (to < parts))
                    def _(i=i, origin=origin, piece=piece, to=to, send=send, recv=recv, step=step):
                        rows = srcs[i].shape[0] // pieces
                        src = srcs[i].at[piece * rows : (piece + 1) * rows] if step == 0 else block(i, origin, piece)
                        hop(i, src, origin, piece, to, send, recv, step, step).start()

        if step == 0:
            for i in range(count):
                rows = srcs[i].shape[0]
                there = dsts[i].at[pl.ds(pl.multiple_of(me * rows, rows), rows)]
                pltpu.make_async_copy(srcs[i], there, own_sem.at[i]).start()
    for i in range(count):
        rows = srcs[i].shape[0]
        there = dsts[i].at[pl.ds(pl.multiple_of(me * rows, rows), rows)]
        pltpu.make_async_copy(srcs[i], there, own_sem.at[i]).wait()
    for way, send, recv in streams:
        to, last = me + way, me - way * (parts - 1)
        for i in range(count):
            for piece in range(pieces):

                @pl.when((last >= 0) & (last < parts))
                def _(i=i, piece=piece, last=last, send=send, recv=recv):
                    here = block(i, last, piece)
                    hop(i, here, last, piece, me, send, recv, 0, parts - 2).wait_recv()

                for step in range(parts - 1):
                    origin = me - way * step

                    @pl.when((origin >= 0) & (origin < parts) & (to >= 0) & (to < parts))
                    def _(i=i, piece=piece, origin=origin, send=send, recv=recv, step=step):
                        here = block(i, origin, piece)
                        hop(i, here, origin, piece, me, send, recv, step, step).wait_send()


def line_gather(arrays, cid, pieces=1):
    parts = lax.axis_size("expert")
    n = len(arrays)
    sem = pltpu.SemaphoreType.DMA
    return pl.pallas_call(
        functools.partial(gather_kernel, parts, pieces, n),
        out_shape=[jax.ShapeDtypeStruct((parts * a.shape[0],) + a.shape[1:], a.dtype) for a in arrays],
        in_specs=[ANY] * n,
        out_specs=[ANY] * n,
        scratch_shapes=[sem((n,))] + [sem((n * pieces, parts - 1))] * 4,
        cost_estimate=transfer_cost(parts * sum(a.size for a in arrays)),
        compiler_params=pltpu.CompilerParams(collective_id=cid, has_side_effects=True),
        name="line_gather_%d" % cid,
    )(*arrays)


def exchange_kernel(parts, count, stack, *refs):
    srcs, dsts = refs[:count], refs[count : 2 * count]
    own_sem, send, recv = refs[2 * count :]
    me = lax.axis_index("expert")
    greet_all(me, parts)

    def piece(i, owner):
        rows = srcs[i].shape[0] // parts
        return srcs[i].at[pl.ds(pl.multiple_of(owner * rows, rows), rows)]

    def place(i, origin):
        rows, cols = srcs[i].shape[0] // parts, srcs[i].shape[1]
        if stack:
            return dsts[i].at[pl.ds(pl.multiple_of(origin * rows, rows), rows)]
        return dsts[i].at[:, pl.ds(pl.multiple_of(origin * cols, cols), cols)]

    copies = []
    for k in list(range(parts - 1, 0, -1)):
        to = lax.rem(me + k, parts)
        for i in range(count):
            copy = pltpu.make_async_remote_copy(
                src_ref=piece(i, to),
                dst_ref=place(i, me),
                send_sem=send.at[i, k - 1],
                recv_sem=recv.at[i, k - 1],
                device_id={"expert": to},
                device_id_type=MESH,
            )
            copy.start()
            copies.append(copy)
    for i in range(count):
        own = pltpu.make_async_copy(piece(i, me), place(i, me), own_sem.at[i])
        own.start()
        own.wait()
    for copy in copies:
        copy.wait_send()
    for k in list(range(parts - 1, 0, -1)):
        origin = lax.rem(me + parts - k, parts)
        for i in range(count):
            pltpu.make_async_remote_copy(
                src_ref=piece(i, me),
                dst_ref=place(i, origin),
                send_sem=send.at[i, k - 1],
                recv_sem=recv.at[i, k - 1],
                device_id={"expert": origin},
                device_id_type=MESH,
            ).wait_recv()


def exchange(arrays, cid, stack=False):
    parts = lax.axis_size("expert")
    n = len(arrays)
    sem = pltpu.SemaphoreType.DMA
    return pl.pallas_call(
        functools.partial(exchange_kernel, parts, n, stack),
        out_shape=[
            jax.ShapeDtypeStruct(
                a.shape if stack else (a.shape[0] // parts, a.shape[1] * parts), a.dtype
            )
            for a in arrays
        ],
        in_specs=[ANY] * n,
        out_specs=[ANY] * n,
        scratch_shapes=[sem((n,)), sem((n, parts - 1)), sem((n, parts - 1))],
        cost_estimate=transfer_cost(sum(a.size for a in arrays)),
        compiler_params=pltpu.CompilerParams(collective_id=cid, has_side_effects=True),
        name="exchange_%d" % cid,
    )(*arrays)


def reduce_kernel(parts, pieces, src, out, slot_up, slot_down, send_up, recv_up, send_down, recv_down):
    me = lax.axis_index("expert")
    greet_line(me, parts)
    rows = out.shape[0]
    part = rows // pieces
    step_rows = 16

    def hop(ref, slot, step, piece, to, send, recv):
        return pltpu.make_async_remote_copy(
            src_ref=ref,
            dst_ref=slot.at[step, piece * part : (piece + 1) * part],
            send_sem=send.at[step, piece],
            recv_sem=recv.at[step, piece],
            device_id={"expert": to},
            device_id_type=MESH,
        )

    def landed(slot, step, piece, send, recv):
        return hop(slot.at[step, piece * part : (piece + 1) * part], slot, step, piece, me, send, recv)

    streams = ((True, slot_up, send_up, recv_up), (False, slot_down, send_down, recv_down))
    for step in range(parts - 1):
        for piece in range(pieces):
            for up, slot, send, recv in streams:
                line = me if up else parts - 1 - me
                dest_line = parts - 1 - step + line
                dest = dest_line if up else parts - 1 - dest_line
                to = me + 1 if up else me - 1

                @pl.when(line == 0)
                def _(dest=dest, slot=slot, step=step, piece=piece, to=to, send=send, recv=recv):
                    there = pl.ds(pl.multiple_of(dest * rows + piece * part, part), part)
                    hop(src.at[there], slot, step, piece, to, send, recv).start()

                if step > 0:

                    @pl.when((line > 0) & (step >= line) & (line < parts - 1))
                    def _(dest=dest, slot=slot, step=step, piece=piece, to=to, send=send, recv=recv):
                        landed(slot, step - 1, piece, send, recv).wait_recv()

                        @pl.loop(0, part // step_rows)
                        def _(r):
                            at = piece * part + r * step_rows
                            here = pl.ds(pl.multiple_of(at, step_rows), step_rows)
                            there = pl.ds(pl.multiple_of(dest * rows + at, step_rows), step_rows)
                            both = slot[step - 1, here, :].astype(jnp.float32) + src[there, :].astype(jnp.float32)
                            slot[step - 1, here, :] = both.astype(jnp.bfloat16)

                        sent = slot.at[step - 1, piece * part : (piece + 1) * part]
                        hop(sent, slot, step, piece, to, send, recv).start()

    @pl.loop(0, rows // step_rows)
    def _(r):
        here = pl.ds(pl.multiple_of(r * step_rows, step_rows), step_rows)
        there = pl.ds(pl.multiple_of(me * rows + r * step_rows, step_rows), step_rows)
        out[here, :] = src[there, :].astype(jnp.float32)

    last = parts - 2
    for piece in range(pieces):
        for up, slot, send, recv in streams:
            line = me if up else parts - 1 - me

            @pl.when(line > 0)
            def _(slot=slot, piece=piece, send=send, recv=recv):
                landed(slot, last, piece, send, recv).wait_recv()

                @pl.loop(0, part // step_rows)
                def _(r):
                    here = pl.ds(pl.multiple_of(piece * part + r * step_rows, step_rows), step_rows)
                    out[here, :] = out[here, :] + slot[last, here, :].astype(jnp.float32)

    for up, slot, send, recv in streams:
        line = me if up else parts - 1 - me
        for step in range(parts - 1):
            for piece in range(pieces):

                @pl.when((step >= line) & (line < parts - 1))
                def _(slot=slot, step=step, piece=piece, send=send, recv=recv):
                    landed(slot, step, piece, send, recv).wait_send()


def line_reduce(terms, cid, pieces=1):
    parts = lax.axis_size("expert")
    rows, cols = terms.shape[0] // parts, terms.shape[1]
    sem = pltpu.SemaphoreType.DMA
    return pl.pallas_call(
        functools.partial(reduce_kernel, parts, pieces),
        out_shape=jax.ShapeDtypeStruct((rows, cols), jnp.float32),
        in_specs=[VMEM],
        out_specs=VMEM,
        scratch_shapes=[pltpu.VMEM((parts - 1, rows, cols), jnp.bfloat16)] * 2
        + [sem((parts - 1, pieces))] * 4,
        cost_estimate=transfer_cost(terms.size),
        compiler_params=pltpu.CompilerParams(
            collective_id=cid, has_side_effects=True, vmem_limit_bytes=48 * 1024 * 1024
        ),
        name="line_reduce_%d" % cid,
    )(terms)


def weights_kernel(parts, blocks, out, small, chosen, dst, dst_out, dst_chosen, own_sem, send, recv, send_up, recv_up, send_down, recv_down):
    me = lax.axis_index("expert")
    share = out.shape[0]
    wide = blocks.shape[1]
    greet_all(me, parts)

    def rows(origin):
        return pl.ds(pl.multiple_of(origin * share, share), share)

    def exchanged(k, to, origin):
        return pltpu.make_async_remote_copy(
            src_ref=blocks.at[rows(to)],
            dst_ref=dst.at[rows(origin), :wide],
            send_sem=send.at[k - 1],
            recv_sem=recv.at[k - 1],
            device_id={"expert": to},
            device_id_type=MESH,
        )

    shared = ((out, dst_out, 0), (small, dst, wide), (chosen, dst_chosen, 0))

    def place(i, origin):
        src, into, at = shared[i]
        return into.at[rows(origin), at : at + src.shape[1]]

    def hop(i, src, origin, to, send_sem, recv_sem):
        return pltpu.make_async_remote_copy(
            src_ref=src,
            dst_ref=place(i, origin),
            send_sem=send_sem,
            recv_sem=recv_sem,
            device_id={"expert": to},
            device_id_type=MESH,
        )

    streams = ((1, send_up, recv_up), (-1, send_down, recv_down))
    for step in range(parts - 1):
        for way, sends, recvs in streams:
            origin, to = me - way * step, me + way
            has = (origin >= 0) & (origin < parts)
            for i in range(3):
                if step > 0:

                    @pl.when(has)
                    def _(i=i, origin=origin, sends=sends, recvs=recvs, step=step):
                        hop(i, place(i, origin), origin, me, sends.at[i, step], recvs.at[i, step - 1]).wait_recv()

                @pl.when(has & (to >= 0) & (to < parts))
                def _(i=i, origin=origin, to=to, sends=sends, recvs=recvs, step=step):
                    src = shared[i][0] if step == 0 else place(i, origin)
                    hop(i, src, origin, to, sends.at[i, step], recvs.at[i, step]).start()

        if step == 0:
            for k in range(parts - 1, 0, -1):
                to = lax.rem(me + k, parts)
                exchanged(k, to, me).start()
            owns = [
                pltpu.make_async_copy(src, target, own_sem.at[i])
                for i, (src, target) in enumerate(
                    (
                        (blocks.at[rows(me)], dst.at[rows(me), :wide]),
                        (out, place(0, me)),
                        (small, place(1, me)),
                        (chosen, place(2, me)),
                    )
                )
            ]
            for copy in owns:
                copy.start()

    for copy in owns:
        copy.wait()
    for way, sends, recvs in streams:
        to, last = me + way, me - way * (parts - 1)
        for i in range(3):

            @pl.when((last >= 0) & (last < parts))
            def _(i=i, last=last, sends=sends, recvs=recvs):
                hop(i, place(i, last), last, me, sends.at[i, 0], recvs.at[i, parts - 2]).wait_recv()

            for step in range(parts - 1):
                origin = me - way * step

                @pl.when((origin >= 0) & (origin < parts) & (to >= 0) & (to < parts))
                def _(i=i, origin=origin, sends=sends, recvs=recvs, step=step):
                    hop(i, place(i, origin), origin, me, sends.at[i, step], recvs.at[i, step]).wait_send()

    for k in range(parts - 1, 0, -1):
        exchanged(k, lax.rem(me + k, parts), me).wait_send()
        exchanged(k, me, lax.rem(me + parts - k, parts)).wait_recv()


def gather_weights(blocks, out, small, chosen, cid):
    parts = lax.axis_size("expert")
    sem = pltpu.SemaphoreType.DMA
    rows, cols = blocks.shape[0], blocks.shape[1] + small.shape[1]
    return pl.pallas_call(
        functools.partial(weights_kernel, parts),
        out_shape=[
            jax.ShapeDtypeStruct((rows, cols), blocks.dtype),
            jax.ShapeDtypeStruct((rows, out.shape[1]), blocks.dtype),
            jax.ShapeDtypeStruct((rows, chosen.shape[1]), blocks.dtype),
        ],
        in_specs=[ANY] * 4,
        out_specs=[ANY] * 3,
        scratch_shapes=[sem((4,)), sem((parts - 1,)), sem((parts - 1,))] + [sem((3, parts - 1))] * 4,
        cost_estimate=transfer_cost(rows * (cols + out.shape[1])),
        compiler_params=pltpu.CompilerParams(collective_id=cid, has_side_effects=True),
        name="gather_weights",
    )(blocks, out, small, chosen)


def diagonal_mask(column_ref, row_ref, block):
    here = pl.ds(block * BLOCK, BLOCK)
    seg_query = column_ref[here, :]
    seg_key = row_ref[:, here]
    shape = (BLOCK, BLOCK)
    causal = lax.broadcasted_iota(jnp.int32, shape, 1) <= lax.broadcasted_iota(jnp.int32, shape, 0)
    same = (seg_query == seg_key) & causal
    return same | ((seg_key == 0) & (seg_query != 0))


def masked_scores(query, key_ref, column_ref, row_ref, block):
    scale = HEAD ** (-0.5)
    here = pl.ds(block * BLOCK, BLOCK)
    own = dot_right(query, key_ref[here, :]) * scale
    own = jnp.where(diagonal_mask(column_ref, row_ref, block), own, MASKED)
    if block == 0:
        return own
    ahead = dot_right(query, key_ref[: block * BLOCK, :]) * scale
    return jnp.concatenate([ahead, own], axis=1)


def attention_kernel(column_ref, row_ref, query_ref, key_ref, value_ref, mixed_ref, lse_ref):
    total = query_ref.shape[0]
    for block in range(total // BLOCK):
        here = pl.ds(block * BLOCK, BLOCK)
        scores = masked_scores(query_ref[here, :], key_ref, column_ref, row_ref, block)
        top = jnp.max(scores, axis=1, keepdims=True)
        expd = jnp.exp(scores - top)
        mass = jnp.sum(expd, axis=1, keepdims=True)
        probs = (expd / mass).astype(jnp.bfloat16)
        mixed = dot_plain(probs, value_ref[: (block + 1) * BLOCK, :])
        mixed_ref[here, :] = mixed.astype(jnp.bfloat16)
        lse_ref[0, here, :] = top + jnp.log(mass)


def head_specs(total, heads):
    return [
        pl.BlockSpec((total, HEAD), lambda h, part=part: (0, part * heads + h)) for part in range(3)
    ]


def run_attention(column, row, qkv):
    total, heads = qkv.shape[0], qkv.shape[1] // (3 * HEAD)
    whole = pl.BlockSpec(memory_space=pltpu.VMEM)
    return pl.pallas_call(
        attention_kernel,
        grid=(heads,),
        in_specs=[whole, whole] + head_specs(total, heads),
        out_specs=[
            pl.BlockSpec((total, HEAD), lambda h: (0, h)),
            pl.BlockSpec((1, total, 1), lambda h: (h, 0, 0)),
        ],
        out_shape=[
            jax.ShapeDtypeStruct((total, heads * HEAD), jnp.bfloat16),
            jax.ShapeDtypeStruct((heads, total, 1), jnp.float32),
        ],
        compiler_params=pltpu.CompilerParams(
            dimension_semantics=("arbitrary",), vmem_limit_bytes=48 * 1024 * 1024
        ),
        cost_estimate=pl.CostEstimate(
            flops=3 * heads * total * total * HEAD,
            bytes_accessed=8 * total * heads * HEAD,
            transcendentals=heads * total * total // 2,
        ),
        name="attention",
    )(column, row, qkv, qkv, qkv)


def attention_back_kernel(
    column_ref, row_ref, query_ref, key_ref, value_ref, grad_ref, lse_ref, back_query_ref, back_key_ref, back_value_ref, key_acc, value_acc
):
    scale = HEAD ** (-0.5)
    total = query_ref.shape[0]
    key_acc[...] = jnp.zeros_like(key_acc)
    value_acc[...] = jnp.zeros_like(value_acc)
    for block in range(total // BLOCK):
        here = pl.ds(block * BLOCK, BLOCK)
        upto = pl.ds(0, (block + 1) * BLOCK)
        query, grad = query_ref[here, :], grad_ref[here, :]
        scores = masked_scores(query, key_ref, column_ref, row_ref, block)
        probs = jnp.exp(scores - lse_ref[0, here, :])
        prob_back = dot_right(grad, value_ref[upto, :])
        delta = jnp.sum(probs * prob_back, axis=1, keepdims=True)
        score_grad = (probs * (prob_back - delta)).astype(jnp.bfloat16)
        back_query_ref[here, :] = (dot_plain(score_grad, key_ref[upto, :]) * scale).astype(jnp.bfloat16)
        key_acc[upto, :] += dot_left(score_grad, query)
        value_acc[upto, :] += dot_left(probs.astype(jnp.bfloat16), grad)
    back_key_ref[...] = (key_acc[...] * scale).astype(jnp.bfloat16)
    back_value_ref[...] = value_acc[...].astype(jnp.bfloat16)


def run_attention_back(column, row, qkv, grad, lse):
    total, heads = qkv.shape[0], qkv.shape[1] // (3 * HEAD)
    whole = pl.BlockSpec(memory_space=pltpu.VMEM)
    head = pl.BlockSpec((total, HEAD), lambda h: (0, h))
    return pl.pallas_call(
        attention_back_kernel,
        grid=(heads,),
        in_specs=[whole, whole]
        + head_specs(total, heads)
        + [head, pl.BlockSpec((1, total, 1), lambda h: (h, 0, 0))],
        out_specs=[head] * 3,
        out_shape=[jax.ShapeDtypeStruct((total, heads * HEAD), jnp.bfloat16)] * 3,
        scratch_shapes=[pltpu.VMEM((total, HEAD), jnp.float32)] * 2,
        compiler_params=pltpu.CompilerParams(
            dimension_semantics=("arbitrary",), vmem_limit_bytes=48 * 1024 * 1024
        ),
        cost_estimate=pl.CostEstimate(
            flops=8 * heads * total * total * HEAD,
            bytes_accessed=16 * total * heads * HEAD,
            transcendentals=heads * total * total // 2,
        ),
        name="attention_back",
    )(column, row, qkv, qkv, qkv, grad, lse)


def own_lift(lift_ref, j):
    row = lax.broadcasted_iota(jnp.int32, (LANES, TILE), 0)
    own = (row >= j * RANK) & (row < (j + 1) * RANK)
    return jnp.where(own, lift_ref[...].astype(jnp.float32), 0.0).astype(jnp.bfloat16)


def gate_column(gates_ref, here, j):
    shape = (ROWS, LANES)
    mine = lax.broadcasted_iota(jnp.int32, shape, 1) == lax.axis_index("expert") * EXP_DEV + j
    return mine, jnp.sum(
        jnp.where(mine, gates_ref[here, :].astype(jnp.float32), 0.0), axis=1, keepdims=True
    )


def row_chunk(b, rows=None):
    rows = rows or ROWS
    return pl.ds(pl.multiple_of(b * rows, rows), rows)


def forward_kernel(
    rows_ref,
    gates_ref,
    down_ref,
    lift_gate_ref,
    lift_up_ref,
    in_gate_ref,
    in_up_ref,
    out_ref,
    *refs,
):
    output_ref, ranks_ref, gate_ref, up_ref, output_acc, stage, sems = refs
    j, f = pl.program_id(0), pl.program_id(1)
    total = rows_ref.shape[0]

    @pl.when((j == 0) & (f == 0))
    def _():
        @pl.loop(0, total // ROWS)
        def _(b):
            here = row_chunk(b)
            ranks_ref[here, :] = dot_right(rows_ref[here, :], down_ref[...]).astype(jnp.bfloat16)
            output_acc[here, :] = jnp.zeros((ROWS, D), jnp.float32)

    lift_gate, lift_up = own_lift(lift_gate_ref, j), own_lift(lift_up_ref, j)

    @pl.loop(0, total // ROWS)
    def _(b):
        here = row_chunk(b)
        rows = rows_ref[here, :]
        _, column = gate_column(gates_ref, here, j)
        gate = dot_plain(rows, in_gate_ref[0]) + dot_plain(ranks_ref[here, :], lift_gate)
        up = dot_plain(rows, in_up_ref[0]) + dot_plain(ranks_ref[here, :], lift_up)
        gate_ref[0, here, :] = gate.astype(jnp.bfloat16)
        up_ref[0, here, :] = up.astype(jnp.bfloat16)
        hidden = (column * (gate * jax.nn.sigmoid(gate) * up)).astype(jnp.bfloat16)
        output_acc[here, :] += dot_plain(hidden, out_ref[0])

    @pl.when((j == EXP_DEV - 1) & (f == FF // TILE - 1))
    def _():
        def copy(b):
            slot = lax.rem(b, 2)
            here = row_chunk(b, stage.shape[1])
            return pltpu.make_async_copy(stage.at[slot], output_ref.at[here], sems.at[slot])

        steps = total // stage.shape[1]

        @pl.loop(0, steps)
        def _(b):
            @pl.when(b >= 2)
            def _():
                copy(b - 2).wait()

            here = row_chunk(b, stage.shape[1])
            stage[lax.rem(b, 2)] = output_acc[here, :].astype(jnp.bfloat16)
            copy(b).start()

        for b in range(steps - 2, steps):
            copy(b).wait()


def weight_specs():
    tiles = FF // TILE
    return [
        pl.BlockSpec((LANES, TILE), lambda j, f: (0, f)),
        pl.BlockSpec((LANES, TILE), lambda j, f: (0, f + tiles)),
        pl.BlockSpec((1, D, TILE), lambda j, f: (j, 0, f)),
        pl.BlockSpec((1, D, TILE), lambda j, f: (j, 0, f + tiles)),
        pl.BlockSpec((1, TILE, D), lambda j, f: (j, f, 0)),
    ]


EXPERT_PARAMS = pltpu.CompilerParams(
    dimension_semantics=("arbitrary", "arbitrary"), vmem_limit_bytes=60 * 1024 * 1024
)


def experts_forward(rows, gates, down, lift, matrix_in, matrix_out):
    total = rows.shape[0]
    kept = pl.BlockSpec((1, total, TILE), lambda j, f: (j, 0, f))
    return pl.pallas_call(
        forward_kernel,
        grid=(EXP_DEV, FF // TILE),
        in_specs=[VMEM] * 3 + weight_specs(),
        out_specs=[
            ANY,
            pl.BlockSpec((total, LANES), lambda j, f: (0, 0), pipeline_mode=pl.Buffered(1)),
            kept,
            kept,
        ],
        out_shape=[
            jax.ShapeDtypeStruct((total, D), jnp.bfloat16),
            jax.ShapeDtypeStruct((total, LANES), jnp.bfloat16),
            jax.ShapeDtypeStruct((EXP_DEV, total, FF), jnp.bfloat16),
            jax.ShapeDtypeStruct((EXP_DEV, total, FF), jnp.bfloat16),
        ],
        scratch_shapes=[
            pltpu.VMEM((total, D), jnp.float32),
            pltpu.VMEM((2, 160, D), jnp.bfloat16),
            pltpu.SemaphoreType.DMA((2,)),
        ],
        compiler_params=EXPERT_PARAMS,
        cost_estimate=pl.CostEstimate(
            flops=10 * EXP_DEV * total * D * FF,
            bytes_accessed=EXP_DEV * 6 * D * FF + 8 * total * D,
            transcendentals=EXP_DEV * total * FF,
        ),
        name="experts_forward",
    )(rows, gates, down, lift, lift, matrix_in, matrix_in, matrix_out)


def backward_kernel(
    parts,
    gates_ref,
    ranks_ref,
    down_ref,
    lift_gate_ref,
    lift_up_ref,
    in_gate_ref,
    in_up_ref,
    out_ref,
    gate_ref,
    up_ref,
    *refs,
):
    blocks, refs = refs[:parts], refs[parts:]
    slot_ref, rank_ref, lift_grad_gate_ref, lift_grad_up_ref, upstream, slot_acc, rank_acc, gate_acc, lift_acc, stage, sems = refs
    j, f = pl.program_id(0), pl.program_id(1)
    total = upstream.shape[0]

    @pl.when((j == 0) & (f == 0))
    def _():
        piece = total // parts
        copies = []
        for shift in range(parts):
            owner = lax.rem(lax.axis_index("expert") + parts - shift, parts)
            there = row_chunk(owner, piece)
            copies.append(pltpu.make_async_copy(blocks[shift], upstream.at[there], sems.at[shift]))
        for copy in copies:
            copy.start()

        @pl.loop(0, total // ROWS)
        def _(b):
            here = row_chunk(b)
            slot_acc[here, :] = jnp.zeros((ROWS, D), jnp.float32)
            rank_acc[here, :] = jnp.zeros((ROWS, LANES), jnp.float32)
            gate_acc[here, :] = jnp.zeros((ROWS, LANES), jnp.float32)

        for copy in copies:
            copy.wait()

    lift_acc[...] = jnp.zeros_like(lift_acc)
    lift_gate, lift_up = own_lift(lift_gate_ref, j), own_lift(lift_up_ref, j)

    @pl.loop(0, total // ROWS)
    def _(b):
        here = row_chunk(b)
        mine, column = gate_column(gates_ref, here, j)
        raw = dot_right(upstream[here, :], out_ref[0])
        gate = gate_ref[0, here, :].astype(jnp.float32)
        up = up_ref[0, here, :].astype(jnp.float32)
        sigma = jax.nn.sigmoid(gate)
        silu = gate * sigma
        gate_grad = jnp.sum(raw * (silu * up), axis=1, keepdims=True)
        back = raw * column
        to_gate = (back * up * (sigma + silu * (1.0 - sigma))).astype(jnp.bfloat16)
        to_up = (back * silu).astype(jnp.bfloat16)
        slot_acc[here, :] += dot_right(to_gate, in_gate_ref[0]) + dot_right(
            to_up, in_up_ref[0]
        )
        rank_acc[here, :] += dot_right(to_gate, lift_gate) + dot_right(to_up, lift_up)
        gate_acc[here, :] += jnp.where(mine, gate_grad, 0.0)
        lift_acc[0] += dot_left(ranks_ref[here, :], to_gate)
        lift_acc[1] += dot_left(ranks_ref[here, :], to_up)

    own = row_chunk(j, RANK)
    lift_grad_gate_ref[0] = lift_acc[0, own, :]
    lift_grad_up_ref[0] = lift_acc[1, own, :]

    @pl.when((j == EXP_DEV - 1) & (f == FF // TILE - 1))
    def _():
        def copy(b):
            slot = lax.rem(b, 2)
            here = row_chunk(b, stage.shape[1])
            return pltpu.make_async_copy(stage.at[slot], slot_ref.at[here], sems.at[slot])

        steps = total // stage.shape[1]

        @pl.loop(0, steps)
        def _(b):
            @pl.when(b >= 2)
            def _():
                copy(b - 2).wait()

            here = row_chunk(b, stage.shape[1])
            rank_low = rank_acc[here, :].astype(jnp.bfloat16)
            rank_ref[here, :] = rank_low
            slot = slot_acc[here, :] + dot_plain(rank_low, down_ref[...])
            wide = gate_acc[here, :]
            high = wide.astype(jnp.bfloat16).astype(jnp.float32)
            both = high + pltpu.roll(wide - high, LANES // 2, 1)
            stage[lax.rem(b, 2), :, :D] = slot.astype(jnp.bfloat16)
            stage[lax.rem(b, 2), :, D:] = both.astype(jnp.bfloat16)
            copy(b).start()

        for b in range(steps - 2, steps):
            copy(b).wait()


def experts_backward(blocks, gates, ranks, down, lift, matrix_in, matrix_out, gate, up):
    total, parts = gates.shape[0], len(blocks)
    grad = pl.BlockSpec((1, RANK, TILE), lambda j, f: (j, 0, f))
    kept = pl.BlockSpec((1, total, TILE), lambda j, f: (j, 0, f))
    return pl.pallas_call(
        functools.partial(backward_kernel, parts),
        grid=(EXP_DEV, FF // TILE),
        in_specs=[VMEM] * 3 + weight_specs() + [kept, kept] + [ANY] * parts,
        out_specs=[
            ANY,
            pl.BlockSpec((total, LANES), lambda j, f: (0, 0), pipeline_mode=pl.Buffered(1)),
            grad,
            grad,
        ],
        out_shape=[
            jax.ShapeDtypeStruct((total, D + LANES), jnp.bfloat16),
            jax.ShapeDtypeStruct((total, LANES), jnp.bfloat16),
            jax.ShapeDtypeStruct((EXP_DEV, RANK, FF), jnp.float32),
            jax.ShapeDtypeStruct((EXP_DEV, RANK, FF), jnp.float32),
        ],
        scratch_shapes=[
            pltpu.VMEM((total, D), jnp.bfloat16),
            pltpu.VMEM((total, D), jnp.float32),
            pltpu.VMEM((total, LANES), jnp.float32),
            pltpu.VMEM((total, LANES), jnp.float32),
            pltpu.VMEM((2, LANES, TILE), jnp.float32),
            pltpu.VMEM((2, 160, D + LANES), jnp.bfloat16),
            pltpu.SemaphoreType.DMA((parts,)),
        ],
        compiler_params=EXPERT_PARAMS,
        cost_estimate=pl.CostEstimate(
            flops=12 * EXP_DEV * total * D * FF,
            bytes_accessed=EXP_DEV * 6 * D * FF + 8 * total * D,
            transcendentals=EXP_DEV * total * FF,
        ),
        name="experts_backward",
    )(gates, ranks, down, lift, lift, matrix_in, matrix_in, matrix_out, gate, up, *blocks)


def pick_kernel(experts, chosen_ref, small_ref, picked_ref, router_ref, gain_ref):
    row = lax.broadcasted_iota(jnp.int32, (LANES, LANES), 0)
    same = row == lax.broadcasted_iota(jnp.int32, (LANES, LANES), 1)
    every = same.astype(jnp.float32).astype(jnp.bfloat16)
    router = (same & (row < experts)).astype(jnp.float32).astype(jnp.bfloat16)
    gain_row = lax.broadcasted_iota(jnp.int32, (8, LANES), 0) + 64
    gain = gain_row == lax.broadcasted_iota(jnp.int32, (8, LANES), 1)
    picked_ref[...] = dot_right(every, chosen_ref[...]).astype(jnp.bfloat16)
    router_ref[...] = dot_right(router, small_ref[...]).astype(jnp.bfloat16)
    gain_ref[...] = dot_right(gain.astype(jnp.float32).astype(jnp.bfloat16), small_ref[...])


def pick_rows(chosen, dense, at, experts):
    return pl.pallas_call(
        functools.partial(pick_kernel, experts),
        grid=(1,),
        in_specs=[VMEM, pl.BlockSpec((D, LANES), lambda i: (0, at // LANES))],
        out_specs=[all_of(LANES, D), all_of(LANES, D), all_of(8, D)],
        out_shape=[
            jax.ShapeDtypeStruct((LANES, D), jnp.bfloat16),
            jax.ShapeDtypeStruct((LANES, D), jnp.bfloat16),
            jax.ShapeDtypeStruct((8, D), jnp.float32),
        ],
        name="pick_rows",
    )(chosen, dense)


def first_kernel(query_ref, key_ref, value_ref, rank_ref, down_ref, *refs):
    weights, out_ref = refs[:3], refs[3]
    total = dot_right(query_ref[...], weights[0][...]) + dot_right(key_ref[...], weights[1][...])
    total = total + dot_right(value_ref[...], weights[2][...]) + dot_plain(rank_ref[...], down_ref[...])
    out_ref[...] = total.astype(jnp.bfloat16)


def first_products(backs, ranks, down, dense):
    total, width = backs[0].shape
    tile = 512
    weights = [
        pl.BlockSpec((tile, width), lambda i, part=part: (i, part)) for part in range(3)
    ]
    return pl.pallas_call(
        first_kernel,
        grid=(D // tile,),
        in_specs=[VMEM] * 4 + [pl.BlockSpec((RANK, tile), lambda i: (0, i))] + weights,
        out_specs=pl.BlockSpec((total, tile), lambda i: (0, i)),
        out_shape=jax.ShapeDtypeStruct((total, D), jnp.bfloat16),
        compiler_params=pltpu.CompilerParams(vmem_limit_bytes=48 * 1024 * 1024),
        cost_estimate=pl.CostEstimate(
            flops=6 * total * width * D, bytes_accessed=6 * width * D + 2 * total * D, transcendentals=0
        ),
        name="first_products",
    )(*backs, ranks, down, dense, dense, dense)


def sublayer_params():
    return pltpu.CompilerParams(
        dimension_semantics=("arbitrary",), vmem_limit_bytes=56 * 1024 * 1024
    )


def all_of(*shape):
    return pl.BlockSpec(shape, lambda i: (0,) * len(shape))


def qkv_kernel(tokens_ref, gain_ref, down_ref, lift_ref, weight_ref, normed_ref, rank_ref, qkv_ref):
    @pl.when(pl.program_id(0) == 0)
    def _():
        rows = tokens_ref.shape[0] // 4

        @pl.loop(0, 4)
        def _(b):
            here = row_chunk(b, rows)
            values = tokens_ref[here, :].astype(jnp.float32)
            normed = (values * norm_inverse(values) * gain_ref[...]).astype(jnp.bfloat16)
            normed_ref[here, :] = normed
            rank_ref[here, :] = dot_right(normed, down_ref[...]).astype(jnp.bfloat16)

    total = dot_plain(normed_ref[...], weight_ref[...]) + dot_plain(rank_ref[...], lift_ref[...])
    qkv_ref[...] = total.astype(jnp.bfloat16)


def project_qkv(tokens, gain, down, lift, dense):
    total, width = tokens.shape[0], lift.shape[1] // 3
    return pl.pallas_call(
        qkv_kernel,
        grid=(3,),
        in_specs=[
            VMEM,
            VMEM,
            VMEM,
            pl.BlockSpec((RANK, width), lambda i: (0, i)),
            pl.BlockSpec((D, width), lambda i: (0, i)),
        ],
        out_specs=[
            all_of(total, D),
            all_of(total, RANK),
            pl.BlockSpec((total, width), lambda i: (0, i)),
        ],
        out_shape=[
            jax.ShapeDtypeStruct((total, D), jnp.bfloat16),
            jax.ShapeDtypeStruct((total, RANK), jnp.bfloat16),
            jax.ShapeDtypeStruct((total, 3 * width), jnp.bfloat16),
        ],
        compiler_params=sublayer_params(),
        cost_estimate=pl.CostEstimate(
            flops=6 * total * D * width, bytes_accessed=6 * D * width + 8 * total * D, transcendentals=0
        ),
        name="project_qkv",
    )(tokens, gain, down, lift, dense)


def middle_kernel(
    experts,
    mixed_ref,
    tokens_ref,
    down_mix_ref,
    lift_mix_ref,
    gain_ref,
    down_route_ref,
    router_ref,
    lift_route_ref,
    routed_ref,
    out_ref,
    middle_ref,
    rank_mix_ref,
    inverse_ref,
    second_ref,
    rank_route_ref,
    probs_ref,
    gates_ref,
):
    i = pl.program_id(0)
    tile = out_ref.shape[1]

    @pl.when(i == 0)
    def _():
        rank_mix_ref[...] = dot_right(mixed_ref[...], down_mix_ref[...]).astype(jnp.bfloat16)

    here = pl.ds(pl.multiple_of(i * tile, tile), tile)
    branch = dot_plain(mixed_ref[...], out_ref[...]) + dot_plain(rank_mix_ref[...], lift_mix_ref[...])
    middle_ref[:, here] = tokens_ref[...].astype(jnp.float32) + branch

    @pl.when(i == D // tile - 1)
    def _():
        middle = middle_ref[...]
        inverse = norm_inverse(middle)
        inverse_ref[...] = inverse
        second = (middle * inverse * gain_ref[...]).astype(jnp.bfloat16)
        second_ref[...] = second
        rank_route = dot_right(second, down_route_ref[...]).astype(jnp.bfloat16)
        rank_route_ref[...] = rank_route
        logits = dot_right(second, router_ref[...]) + dot_plain(rank_route, lift_route_ref[...])
        lane = lax.broadcasted_iota(jnp.int32, logits.shape, 1)
        logits = jnp.where(lane < experts, logits, MASKED)
        exped = jnp.exp(logits - jnp.max(logits, axis=1, keepdims=True))
        probs = exped / jnp.sum(exped, axis=1, keepdims=True)
        probs_ref[...] = probs
        gates_ref[...] = (probs * routed_ref[...]).astype(jnp.bfloat16)


def finish_attention(experts, mixed, tokens, down_mix, lift_mix, gain, down_route, router, lift_route, routed, out_matrix):
    piece, tile = tokens.shape[0], 512
    column = lambda i: (0, i)
    return pl.pallas_call(
        functools.partial(middle_kernel, experts),
        grid=(D // tile,),
        in_specs=[
            VMEM,
            pl.BlockSpec((piece, tile), column),
            VMEM,
            pl.BlockSpec((RANK, tile), column),
            VMEM,
            VMEM,
            VMEM,
            VMEM,
            VMEM,
            pl.BlockSpec((D, tile), column),
        ],
        out_specs=[
            all_of(piece, D),
            all_of(piece, RANK),
            all_of(piece, 1),
            all_of(piece, D),
            all_of(piece, RANK),
            all_of(piece, LANES),
            all_of(piece, LANES),
        ],
        out_shape=[
            jax.ShapeDtypeStruct((piece, D), jnp.float32),
            jax.ShapeDtypeStruct((piece, RANK), jnp.bfloat16),
            jax.ShapeDtypeStruct((piece, 1), jnp.float32),
            jax.ShapeDtypeStruct((piece, D), jnp.bfloat16),
            jax.ShapeDtypeStruct((piece, RANK), jnp.bfloat16),
            jax.ShapeDtypeStruct((piece, LANES), jnp.float32),
            jax.ShapeDtypeStruct((piece, LANES), jnp.bfloat16),
        ],
        compiler_params=sublayer_params(),
        cost_estimate=pl.CostEstimate(
            flops=2 * piece * D * D, bytes_accessed=2 * D * D + 12 * piece * D, transcendentals=piece * LANES
        ),
        name="finish_attention",
    )(mixed, tokens, down_mix, lift_mix, gain, down_route, router, lift_route, routed, out_matrix)


def middle_back_kernel(
    slot_ref,
    probs_ref,
    routed_ref,
    middle_ref,
    inverse_ref,
    cotangent_ref,
    gain_ref,
    router_ref,
    lift_route_ref,
    down_route_ref,
    lift_mix_ref,
    down_mix_ref,
    out_ref,
    mixed_ref,
    grad_ref,
    branch_ref,
    logit_ref,
    rank_route_ref,
    rank_mix_ref,
):
    @pl.when(pl.program_id(0) == 0)
    def _():
        parts = slot_ref[:, D:]
        prob_grad = (parts + pltpu.roll(parts, LANES // 2, 1)) * routed_ref[...]
        probs = probs_ref[...]
        logit_grad = probs * (prob_grad - jnp.sum(probs * prob_grad, axis=1, keepdims=True))
        logit_grad = logit_grad.astype(jnp.bfloat16)
        logit_ref[...] = logit_grad
        rank_route_grad = dot_right(logit_grad, lift_route_ref[...]).astype(jnp.bfloat16)
        rank_route_ref[...] = rank_route_grad
        upstream = slot_ref[:, :D] + dot_plain(logit_grad, router_ref[...])
        upstream = upstream + dot_plain(rank_route_grad, down_route_ref[...])
        middle_grad = cotangent_ref[...].astype(jnp.float32) + norm_backward(
            middle_ref[...], inverse_ref[...], gain_ref[...], upstream
        )
        grad_ref[...] = middle_grad
        branch_ref[...] = middle_grad.astype(jnp.bfloat16)
        rank_mix_ref[...] = dot_right(branch_ref[...], lift_mix_ref[...]).astype(jnp.bfloat16)

    mixed = dot_right(branch_ref[...], out_ref[...]) + dot_plain(rank_mix_ref[...], down_mix_ref[...])
    mixed_ref[...] = mixed.astype(jnp.bfloat16)


def middle_backward(
    width, slot, probs, routed, middle, inverse, cotangent, gain, router, lift_route, down_route, lift_mix, down_mix, out_matrix
):
    piece = middle.shape[0]
    return pl.pallas_call(
        middle_back_kernel,
        grid=(D // width,),
        in_specs=[VMEM] * 11
        + [
            pl.BlockSpec((RANK, width), lambda i: (0, i)),
            pl.BlockSpec((width, D), lambda i: (i, 0)),
        ],
        out_specs=[
            pl.BlockSpec((piece, width), lambda i: (i, 0)),
            all_of(piece, D),
            all_of(piece, D),
            all_of(piece, LANES),
            all_of(piece, RANK),
            all_of(piece, RANK),
        ],
        out_shape=[
            jax.ShapeDtypeStruct((piece * D // width, width), jnp.bfloat16),
            jax.ShapeDtypeStruct((piece, D), jnp.float32),
            jax.ShapeDtypeStruct((piece, D), jnp.bfloat16),
            jax.ShapeDtypeStruct((piece, LANES), jnp.bfloat16),
            jax.ShapeDtypeStruct((piece, RANK), jnp.bfloat16),
            jax.ShapeDtypeStruct((piece, RANK), jnp.bfloat16),
        ],
        compiler_params=sublayer_params(),
        cost_estimate=pl.CostEstimate(
            flops=2 * piece * D * D, bytes_accessed=2 * D * D + 24 * piece * D, transcendentals=0
        ),
        name="middle_backward",
    )(slot, probs, routed, middle, inverse, cotangent, gain, router, lift_route, down_route, lift_mix, down_mix, out_matrix)


def norm_inverse(values):
    return lax.rsqrt(jnp.mean(values * values, axis=-1, keepdims=True) + EPSILON)


def norm_backward(values, inverse, gain_row, upstream):
    scaled = upstream * gain_row
    return inverse * scaled - values * inverse**3 * jnp.mean(
        scaled * values, axis=-1, keepdims=True
    )


def segments_of(lengths, places):
    upto = jnp.arange(lengths.shape[0])
    limits = PROMPT + jnp.sum(
        jnp.where(upto[:, None] <= upto[None, :], lengths[:, None], 0), axis=0
    )
    passed = jnp.sum((places[:, None] >= limits[None, :]).astype(jnp.int32), axis=1)
    return jnp.where(places < PROMPT, 0, 1 + passed)


def body(
    tokens,
    cotangent,
    norm_gains,
    qkv_weight,
    out_weight,
    router_weight,
    adapter_down,
    adapter_qkv,
    adapter_out,
    adapter_router,
    expert_input,
    expert_output,
    expert_down,
    expert_lift,
    routes,
    adapter_ids,
    cont_lengths,
):
    low = jnp.bfloat16
    piece = tokens.shape[0]
    parts = lax.axis_size("expert")
    groups = lax.axis_size("dp")
    ways = parts * groups
    me = lax.axis_index("expert")
    total = parts * piece
    experts = EXP_DEV * parts
    width = D // parts
    share = D // ways
    route_rows = ADAPTERS * RANK // ways
    adapter = adapter_ids[0]

    matrix_out = lax.all_gather(expert_output, "dp", axis=1, tiled=True)

    group_ids = lax.all_gather(adapter_ids, "dp", axis=0, tiled=True)
    hot = group_ids[:, None] == jnp.arange(ADAPTERS, dtype=jnp.int32)
    group_hot = hot.astype(jnp.float32)
    adapter_cols = expert_lift.shape[3]
    pairs = jnp.stack([expert_down.transpose(0, 2, 3, 1), expert_lift])
    pairs = pairs.transpose(2, 0, 1, 3, 4).reshape(ADAPTERS, 2 * EXP_DEV * RANK * adapter_cols)
    pairs = dot_plain(hot.astype(low), pairs).astype(low)
    pairs = lax.all_to_all(
        pairs.reshape(groups, 2 * EXP_DEV * RANK, adapter_cols), "dp", split_axis=0, concat_axis=0, tiled=True
    )
    pairs = pairs.reshape(groups, 2, EXP_DEV * RANK, adapter_cols).transpose(1, 2, 0, 3)
    pairs = pairs.reshape(2, EXP_DEV * RANK, D)
    pairs = jnp.pad(pairs, ((0, 0), (0, LANES - EXP_DEV * RANK), (0, 0)))

    def columns(array, upto):
        return jnp.pad(array, ((0, share - array.shape[0]), (0, upto - array.shape[1])))

    adapters = jnp.concatenate(
        [
            adapter_down.reshape(share, ADAPTERS * 3 * RANK),
            adapter_out.reshape(ADAPTERS * RANK, share).T,
            adapter_qkv.reshape(ADAPTERS * RANK, 3, share).transpose(2, 1, 0).reshape(share, 3 * LANES),
        ],
        axis=1,
    )
    row = jnp.arange(LANES, dtype=jnp.int32)[None, :]
    ids = group_ids[:, None]
    wanted = jnp.where(
        row < 48,
        ids * 48 + row,
        jnp.where(
            row < 64,
            384 + ids * RANK + row - 48,
            jnp.where(row < 112, 512 + LANES * ((row - 64) // RANK) + ids * RANK + (row - 64) % RANK, -1),
        ),
    ).reshape(1, groups * LANES)
    chosen = jnp.arange(adapters.shape[1], dtype=jnp.int32)[:, None] == wanted
    chosen = dot_plain(adapters, chosen.astype(low)).astype(low)

    qkv_blocks = (
        qkv_weight.reshape(share, 3, parts, width).transpose(2, 0, 1, 3).reshape(parts * share, 3 * width)
    )
    small = jnp.concatenate(
        [columns(router_weight, 32), columns(adapter_router, 32), columns(norm_gains.T, 64)], axis=1
    )
    dense_line, out_line, chosen_line = gather_weights(qkv_blocks, out_weight, small, chosen, 0)
    chosen_all = lax.all_to_all(
        chosen_line.reshape(parts * share, groups, LANES).transpose(1, 0, 2),
        "dp",
        split_axis=0,
        concat_axis=0,
        tiled=True,
    ).reshape(D, LANES)
    dense_line, out_line, expert_input, matrix_out, chosen_all, pairs = lax.optimization_barrier(
        (dense_line, out_line, expert_input, matrix_out, chosen_all, pairs)
    )
    dense_all = lax.all_gather(dense_line, "dp", axis=0, tiled=True)
    (tokens_all,) = line_gather([tokens], 1, 2)
    out_matrix = lax.all_gather(out_line, "dp", axis=0, tiled=True)
    matrix_in = lax.all_gather(expert_input, "dp", axis=1, tiled=True)
    small_at = 3 * width

    picked, router_rows, gain_rows = pick_rows(chosen_all, dense_all, small_at, experts)
    down_query, down_mix, down_route = picked[:16], picked[16:32], picked[32:48]
    lift_mix = picked[48:64]
    lift_query = (
        picked[64:112].reshape(3, RANK, ways, share).transpose(1, 2, 0, 3).reshape(RANK, 3, parts, width)
    )
    lift_query = lax.dynamic_index_in_dim(lift_query, me, 2, keepdims=False).reshape(RANK, 3 * width)
    by_owner = dense_all[:, small_at : small_at + LANES].reshape(ways, share, LANES)
    lift_route = lax.dynamic_slice_in_dim(
        by_owner[:, :route_rows, 32 : 32 + experts].reshape(ADAPTERS * RANK, experts),
        adapter * RANK,
        RANK,
        0,
    )
    lift_route = jnp.pad(lift_route, ((0, 0), (0, LANES - experts)))
    routed = jnp.any(routes[:, :, None] == jnp.arange(LANES, dtype=jnp.int32), axis=1).astype(jnp.float32)
    def shifted(array, by):
        return lax.ppermute(array, "expert", [(i, (i + by) % parts) for i in range(parts)])

    early, tokens_all = lax.optimization_barrier((cotangent, tokens_all))
    early_shifts, late_shifts = [1], list(range(2, parts))
    moved = {s: shifted(early, s) for s in early_shifts}

    normed_low, rank_query, qkv_low = project_qkv(
        tokens_all, gain_rows[0:1], down_query, lift_query, dense_all
    )
    segments = segments_of(cont_lengths[0], jnp.arange(total, dtype=jnp.int32))
    segment_column, segment_row = segments[:, None], segments[None, :]
    mixed_heads, log_mass = run_attention(segment_column, segment_row, qkv_low)
    (mixed_low,) = exchange([mixed_heads], 3)

    middle, rank_mix, inverse_second, second_low, rank_route, router_probs, gates = finish_attention(
        experts,
        mixed_low,
        tokens,
        down_mix,
        lift_mix,
        gain_rows[1:2],
        down_route,
        router_rows,
        lift_route,
        routed,
        out_matrix,
    )
    held = lax.optimization_barrier([second_low] + [moved[s] for s in early_shifts])
    second_low = held[0]
    moved.update(zip(early_shifts, held[1:]))
    second_all, gates_all = line_gather([second_low, gates], 4, 2)

    late, second_all = lax.optimization_barrier((cotangent, second_all))
    moved.update({s: shifted(late, s) for s in late_shifts})
    cotangents = [cotangent] + [moved[s] for s in range(1, parts)]
    output_terms, ranks, gate, up = experts_forward(
        second_all, gates_all, pairs[0], pairs[1], matrix_in, matrix_out
    )
    output_sum = lax.psum_scatter(output_terms, "expert", scatter_dimension=0, tiled=True)
    slot_terms, rank_expert_grad, lift_gate_grad, lift_up_grad = experts_backward(
        cotangents, gates_all, ranks, pairs[0], pairs[1], matrix_in, matrix_out, gate, up
    )
    slot_sum = line_reduce(slot_terms, 5, 2)
    slot_sum, output_sum = lax.optimization_barrier((slot_sum, output_sum))

    lift_sent = jnp.concatenate([lift_gate_grad, lift_up_grad], axis=2).reshape(EXP_DEV * RANK, D)
    down_sent = dot_left(rank_expert_grad[:, : EXP_DEV * RANK], second_all)
    expert_sent = (
        jnp.concatenate([lift_sent, down_sent], axis=0)
        .astype(low)
        .reshape(2 * EXP_DEV * RANK, groups, -1)
        .transpose(1, 0, 2)
    )
    expert_got = lax.all_to_all(expert_sent, "dp", split_axis=0, concat_axis=0, tiled=True)
    by_adapter = jnp.einsum(
        "ga,gkc->akc", group_hot, expert_got.astype(jnp.float32), precision=lax.Precision.HIGHEST
    ).reshape(ADAPTERS, 2, EXP_DEV, RANK, -1)
    explift_grad = by_adapter[:, 0].transpose(1, 0, 2, 3)
    expdown_grad = by_adapter[:, 1].transpose(1, 3, 0, 2)

    mixed_grad, middle_grad, branch_grad, logit_grad, rank_route_grad, rank_mix_grad = middle_backward(
        width,
        slot_sum,
        router_probs,
        routed,
        middle,
        inverse_second,
        cotangent,
        gain_rows[1:2],
        router_rows,
        lift_route,
        down_route,
        lift_mix,
        down_mix,
        out_matrix,
    )

    (mixed_back,) = exchange([mixed_grad], 6, stack=True)
    back_query, back_key, back_value = run_attention_back(
        segment_column, segment_row, qkv_low, mixed_back, log_mass
    )
    qkv_back = jnp.concatenate([back_query, back_key, back_value], axis=1)
    rank_query_grad = dot_right(qkv_back, lift_query).astype(low)
    first_terms = first_products([back_query, back_key, back_value], rank_query_grad, down_query, dense_all)
    lift_query_grad = lax.dynamic_update_slice(
        jnp.zeros((RANK, 3, parts, width), jnp.float32),
        dot_left(rank_query, qkv_back).reshape(RANK, 3, 1, width),
        (0, 0, me, 0),
    )
    downs = jnp.concatenate(
        [
            dot_left(rank_query_grad, normed_low),
            dot_left(rank_mix_grad, mixed_low),
            dot_left(rank_route_grad, second_low),
            dot_left(rank_mix, branch_grad),
        ]
    )
    owned = jnp.concatenate(
        [
            downs.reshape(4 * RANK, ways, share).transpose(1, 0, 2).reshape(ways, -1),
            lift_query_grad.reshape(RANK, ways, 3 * share).transpose(1, 0, 2).reshape(ways, -1),
            jnp.broadcast_to(dot_left(rank_route, logit_grad)[:, :experts].reshape(1, -1), (ways, RANK * experts)),
        ],
        axis=1,
    ).astype(low)
    first_terms, output_sum = lax.optimization_barrier((first_terms, output_sum))
    first_grad = lax.psum_scatter(first_terms, "expert", scatter_dimension=0, tiled=True).astype(jnp.float32)
    got = lax.all_to_all(owned, ("dp", "expert"), split_axis=0, concat_axis=0, tiled=True)
    inputs = tokens.astype(jnp.float32)
    inverse_first = norm_inverse(inputs)
    input_grad = (
        middle_grad + norm_backward(inputs, inverse_first, gain_rows[0:1], first_grad)
    ).astype(low)
    summed = jnp.einsum(
        "ga,gek->ak",
        group_hot,
        got.astype(jnp.float32).reshape(groups, parts, -1),
        precision=lax.Precision.HIGHEST,
    )
    n_down, n_qkv = 4 * RANK * share, 3 * RANK * share
    downs = summed[:, :n_down].reshape(ADAPTERS, 4, RANK, share)
    down_grad = downs[:, :3].transpose(3, 0, 1, 2)
    proj_grad = downs[:, 3]
    qkv_grad = summed[:, n_down : n_down + n_qkv].reshape(ADAPTERS, RANK, 3 * share)
    router_grad = lax.dynamic_slice_in_dim(
        summed[:, n_down + n_qkv :].reshape(ADAPTERS * RANK, experts),
        (lax.axis_index("dp") * parts + me) * route_rows,
        route_rows,
        0,
    )
    layer_output = (middle + output_sum.astype(jnp.float32)).astype(low)
    return (
        layer_output,
        input_grad,
        down_grad,
        qkv_grad,
        proj_grad,
        router_grad,
        expdown_grad,
        explift_grad,
    )


def solution(mesh):
    placed = (
        P(("dp", "expert"), None),
        P(("dp", "expert"), None),
        P(None, ("dp", "expert")),
        P(("dp", "expert"), None),
        P(("dp", "expert"), None),
        P(("dp", "expert"), None),
        P(("dp", "expert"), None, None, None),
        P(None, None, ("dp", "expert")),
        P(None, None, ("dp", "expert")),
        P(("dp", "expert"), None),
        P("expert", "dp", None),
        P("expert", "dp", None),
        P("expert", "dp", None, None),
        P("expert", None, None, "dp"),
        P(("dp", "expert"), None),
        P("dp"),
        P("dp", None),
    )
    return jax.shard_map(
        body,
        mesh=mesh,
        in_specs=placed,
        out_specs=(
            P(("dp", "expert"), None),
            P(("dp", "expert"), None),
            P(("dp", "expert"), None, None, None),
            P(None, None, ("dp", "expert")),
            P(None, None, ("dp", "expert")),
            P(("dp", "expert"), None),
            P("expert", "dp", None, None),
            P("expert", None, None, "dp"),
        ),
        check_vma=False,
    )
```

```python
import functools

import jax
import jax.numpy as jnp
from jax import lax
from jax.experimental import pallas as pl
from jax.experimental.pallas import tpu as pltpu
from jax.sharding import PartitionSpec as P

D = 2048
HEAD = 128
FF = 1024
RANK = 16
ADAPTERS = 8
EXP_DEV = 4
PROMPT = 1024
EPSILON = 1e-05
MASKED = -1e30
LANES = 128
BLOCK = 256
ROWS = 1280
TILE = 512
HALF = EXP_DEV // 2
SMALL = 1024

MESH = pl.DeviceIdType.MESH
ANY = pl.BlockSpec(memory_space=pl.ANY)
VMEM = pl.BlockSpec(memory_space=pltpu.VMEM)


def dot_plain(left, right):
    return jnp.dot(left, right, preferred_element_type=jnp.float32)


def dot_left(left, right):
    return lax.dot_general(
        left, right, (((0,), (0,)), ((), ())), preferred_element_type=jnp.float32
    )


def dot_right(left, right):
    return lax.dot_general(
        left, right, (((1,), (1,)), ((), ())), preferred_element_type=jnp.float32
    )


def transfer_cost(elements):
    return pl.CostEstimate(flops=0, bytes_accessed=140 * elements, transcendentals=0)


def greet_line(me, parts):
    barrier = pltpu.get_barrier_semaphore()

    @pl.when(me > 0)
    def _():
        pl.semaphore_signal(barrier, inc=1, device_id={"expert": me - 1}, device_id_type=MESH)

    @pl.when(me < parts - 1)
    def _():
        pl.semaphore_signal(barrier, inc=1, device_id={"expert": me + 1}, device_id_type=MESH)

    pl.semaphore_wait(barrier, jnp.where((me > 0) & (me < parts - 1), 2, 1))


def greet_all(me, parts):
    barrier = pltpu.get_barrier_semaphore()
    for k in range(1, parts):
        pl.semaphore_signal(
            barrier, inc=1, device_id={"expert": lax.rem(me + k, parts)}, device_id_type=MESH
        )
    pl.semaphore_wait(barrier, parts - 1)


def gather_kernel(parts, pieces, count, *refs):
    srcs, dsts = refs[:count], refs[count : 2 * count]
    own_sem, send_up, recv_up, send_down, recv_down = refs[2 * count :]
    me = lax.axis_index("expert")
    greet_line(me, parts)

    def block(i, origin, piece):
        rows = srcs[i].shape[0] // pieces
        at = origin * srcs[i].shape[0] + piece * rows
        return dsts[i].at[pl.ds(pl.multiple_of(at, rows), rows)]

    def hop(i, src, origin, piece, to, send, recv, step, got):
        n = i * pieces + piece
        return pltpu.make_async_remote_copy(
            src_ref=src,
            dst_ref=block(i, origin, piece),
            send_sem=send.at[n, step],
            recv_sem=recv.at[n, got],
            device_id={"expert": to},
            device_id_type=MESH,
        )

    streams = ((1, send_up, recv_up), (-1, send_down, recv_down))
    for step in range(parts - 1):
        for piece in range(pieces):
            for i in range(count):
                for way, send, recv in streams:
                    origin, to = me - way * step, me + way
                    has = (origin >= 0) & (origin < parts)
                    if step > 0:

                        @pl.when(has)
                        def _(i=i, origin=origin, piece=piece, send=send, recv=recv, step=step):
                            here = block(i, origin, piece)
                            hop(i, here, origin, piece, me, send, recv, step, step - 1).wait_recv()

                    @pl.when(has & (to >= 0) & (to < parts))
                    def _(i=i, origin=origin, piece=piece, to=to, send=send, recv=recv, step=step):
                        rows = srcs[i].shape[0] // pieces
                        src = srcs[i].at[piece * rows : (piece + 1) * rows] if step == 0 else block(i, origin, piece)
                        hop(i, src, origin, piece, to, send, recv, step, step).start()

        if step == 0:
            for i in range(count):
                rows = srcs[i].shape[0]
                there = dsts[i].at[pl.ds(pl.multiple_of(me * rows, rows), rows)]
                pltpu.make_async_copy(srcs[i], there, own_sem.at[i]).start()
    for i in range(count):
        rows = srcs[i].shape[0]
        there = dsts[i].at[pl.ds(pl.multiple_of(me * rows, rows), rows)]
        pltpu.make_async_copy(srcs[i], there, own_sem.at[i]).wait()
    for way, send, recv in streams:
        to, last = me + way, me - way * (parts - 1)
        for i in range(count):
            for piece in range(pieces):

                @pl.when((last >= 0) & (last < parts))
                def _(i=i, piece=piece, last=last, send=send, recv=recv):
                    here = block(i, last, piece)
                    hop(i, here, last, piece, me, send, recv, 0, parts - 2).wait_recv()

                for step in range(parts - 1):
                    origin = me - way * step

                    @pl.when((origin >= 0) & (origin < parts) & (to >= 0) & (to < parts))
                    def _(i=i, piece=piece, origin=origin, send=send, recv=recv, step=step):
                        here = block(i, origin, piece)
                        hop(i, here, origin, piece, me, send, recv, step, step).wait_send()


def line_gather(arrays, cid, pieces=1):
    parts = lax.axis_size("expert")
    n = len(arrays)
    sem = pltpu.SemaphoreType.DMA
    return pl.pallas_call(
        functools.partial(gather_kernel, parts, pieces, n),
        out_shape=[jax.ShapeDtypeStruct((parts * a.shape[0],) + a.shape[1:], a.dtype) for a in arrays],
        in_specs=[ANY] * n,
        out_specs=[ANY] * n,
        scratch_shapes=[sem((n,))] + [sem((n * pieces, parts - 1))] * 4,
        cost_estimate=transfer_cost(parts * sum(a.size for a in arrays)),
        compiler_params=pltpu.CompilerParams(collective_id=cid, has_side_effects=True),
        name="line_gather_%d" % cid,
    )(*arrays)


def exchange_kernel(parts, count, stack, *refs):
    srcs, dsts = refs[:count], refs[count : 2 * count]
    own_sem, send, recv = refs[2 * count :]
    me = lax.axis_index("expert")
    greet_all(me, parts)

    def piece(i, owner):
        rows = srcs[i].shape[0] // parts
        return srcs[i].at[pl.ds(pl.multiple_of(owner * rows, rows), rows)]

    def place(i, origin):
        rows, cols = srcs[i].shape[0] // parts, srcs[i].shape[1]
        if stack:
            return dsts[i].at[pl.ds(pl.multiple_of(origin * rows, rows), rows)]
        return dsts[i].at[:, pl.ds(pl.multiple_of(origin * cols, cols), cols)]

    copies = []
    for k in list(range(parts - 1, 0, -1)):
        to = lax.rem(me + k, parts)
        for i in range(count):
            copy = pltpu.make_async_remote_copy(
                src_ref=piece(i, to),
                dst_ref=place(i, me),
                send_sem=send.at[i, k - 1],
                recv_sem=recv.at[i, k - 1],
                device_id={"expert": to},
                device_id_type=MESH,
            )
            copy.start()
            copies.append(copy)
    for i in range(count):
        own = pltpu.make_async_copy(piece(i, me), place(i, me), own_sem.at[i])
        own.start()
        own.wait()
    for copy in copies:
        copy.wait_send()
    for k in list(range(parts - 1, 0, -1)):
        origin = lax.rem(me + parts - k, parts)
        for i in range(count):
            pltpu.make_async_remote_copy(
                src_ref=piece(i, me),
                dst_ref=place(i, origin),
                send_sem=send.at[i, k - 1],
                recv_sem=recv.at[i, k - 1],
                device_id={"expert": origin},
                device_id_type=MESH,
            ).wait_recv()


def exchange(arrays, cid, stack=False):
    parts = lax.axis_size("expert")
    n = len(arrays)
    sem = pltpu.SemaphoreType.DMA
    return pl.pallas_call(
        functools.partial(exchange_kernel, parts, n, stack),
        out_shape=[
            jax.ShapeDtypeStruct(
                a.shape if stack else (a.shape[0] // parts, a.shape[1] * parts), a.dtype
            )
            for a in arrays
        ],
        in_specs=[ANY] * n,
        out_specs=[ANY] * n,
        scratch_shapes=[sem((n,)), sem((n, parts - 1)), sem((n, parts - 1))],
        cost_estimate=transfer_cost(sum(a.size for a in arrays)),
        compiler_params=pltpu.CompilerParams(collective_id=cid, has_side_effects=True),
        name="exchange_%d" % cid,
    )(*arrays)


def reduce_kernel(parts, pieces, src, out, slot_up, slot_down, send_up, recv_up, send_down, recv_down):
    me = lax.axis_index("expert")
    greet_line(me, parts)
    rows = out.shape[0]
    part = rows // pieces
    step_rows = 16

    def hop(ref, slot, step, piece, to, send, recv):
        return pltpu.make_async_remote_copy(
            src_ref=ref,
            dst_ref=slot.at[step, piece * part : (piece + 1) * part],
            send_sem=send.at[step, piece],
            recv_sem=recv.at[step, piece],
            device_id={"expert": to},
            device_id_type=MESH,
        )

    def landed(slot, step, piece, send, recv):
        return hop(slot.at[step, piece * part : (piece + 1) * part], slot, step, piece, me, send, recv)

    streams = ((True, slot_up, send_up, recv_up), (False, slot_down, send_down, recv_down))
    for step in range(parts - 1):
        for piece in range(pieces):
            for up, slot, send, recv in streams:
                line = me if up else parts - 1 - me
                dest_line = parts - 1 - step + line
                dest = dest_line if up else parts - 1 - dest_line
                to = me + 1 if up else me - 1

                @pl.when(line == 0)
                def _(dest=dest, slot=slot, step=step, piece=piece, to=to, send=send, recv=recv):
                    there = pl.ds(pl.multiple_of(dest * rows + piece * part, part), part)
                    hop(src.at[there], slot, step, piece, to, send, recv).start()

                if step > 0:

                    @pl.when((line > 0) & (step >= line) & (line < parts - 1))
                    def _(dest=dest, slot=slot, step=step, piece=piece, to=to, send=send, recv=recv):
                        landed(slot, step - 1, piece, send, recv).wait_recv()

                        @pl.loop(0, part // step_rows)
                        def _(r):
                            at = piece * part + r * step_rows
                            here = pl.ds(pl.multiple_of(at, step_rows), step_rows)
                            there = pl.ds(pl.multiple_of(dest * rows + at, step_rows), step_rows)
                            both = slot[step - 1, here, :].astype(jnp.float32) + src[there, :].astype(jnp.float32)
                            slot[step - 1, here, :] = both.astype(jnp.bfloat16)

                        sent = slot.at[step - 1, piece * part : (piece + 1) * part]
                        hop(sent, slot, step, piece, to, send, recv).start()

    @pl.loop(0, rows // step_rows)
    def _(r):
        here = pl.ds(pl.multiple_of(r * step_rows, step_rows), step_rows)
        there = pl.ds(pl.multiple_of(me * rows + r * step_rows, step_rows), step_rows)
        out[here, :] = src[there, :].astype(jnp.float32)

    last = parts - 2
    for piece in range(pieces):
        for up, slot, send, recv in streams:
            line = me if up else parts - 1 - me

            @pl.when(line > 0)
            def _(slot=slot, piece=piece, send=send, recv=recv):
                landed(slot, last, piece, send, recv).wait_recv()

                @pl.loop(0, part // step_rows)
                def _(r):
                    here = pl.ds(pl.multiple_of(piece * part + r * step_rows, step_rows), step_rows)
                    out[here, :] = out[here, :] + slot[last, here, :].astype(jnp.float32)

    for up, slot, send, recv in streams:
        line = me if up else parts - 1 - me
        for step in range(parts - 1):
            for piece in range(pieces):

                @pl.when((step >= line) & (line < parts - 1))
                def _(slot=slot, step=step, piece=piece, send=send, recv=recv):
                    landed(slot, step, piece, send, recv).wait_send()


def line_reduce(terms, cid, pieces=1):
    parts = lax.axis_size("expert")
    rows, cols = terms.shape[0] // parts, terms.shape[1]
    sem = pltpu.SemaphoreType.DMA
    return pl.pallas_call(
        functools.partial(reduce_kernel, parts, pieces),
        out_shape=jax.ShapeDtypeStruct((rows, cols), jnp.float32),
        in_specs=[VMEM],
        out_specs=VMEM,
        scratch_shapes=[pltpu.VMEM((parts - 1, rows, cols), jnp.bfloat16)] * 2
        + [sem((parts - 1, pieces))] * 4,
        cost_estimate=transfer_cost(terms.size),
        compiler_params=pltpu.CompilerParams(
            collective_id=cid, has_side_effects=True, vmem_limit_bytes=48 * 1024 * 1024
        ),
        name="line_reduce_%d" % cid,
    )(terms)


def weights_kernel(parts, blocks, out, small, chosen, dst, dst_chosen, own_sem, send, recv, send_up, recv_up, send_down, recv_down):
    me = lax.axis_index("expert")
    share = out.shape[0]
    left, wide = out.shape[1], blocks.shape[1]
    greet_all(me, parts)

    def rows(origin):
        return pl.ds(pl.multiple_of(origin * share, share), share)

    def exchanged(k, to, origin):
        return pltpu.make_async_remote_copy(
            src_ref=blocks.at[rows(to)],
            dst_ref=dst.at[rows(origin), left : left + wide],
            send_sem=send.at[k - 1],
            recv_sem=recv.at[k - 1],
            device_id={"expert": to},
            device_id_type=MESH,
        )

    shared = ((out, dst, 0), (small, dst, left + wide), (chosen, dst_chosen, 0))

    def place(i, origin):
        src, into, at = shared[i]
        return into.at[rows(origin), at : at + src.shape[1]]

    def hop(i, src, origin, to, send_sem, recv_sem):
        return pltpu.make_async_remote_copy(
            src_ref=src,
            dst_ref=place(i, origin),
            send_sem=send_sem,
            recv_sem=recv_sem,
            device_id={"expert": to},
            device_id_type=MESH,
        )

    streams = ((1, send_up, recv_up), (-1, send_down, recv_down))
    for step in range(parts - 1):
        for way, sends, recvs in streams:
            origin, to = me - way * step, me + way
            has = (origin >= 0) & (origin < parts)
            for i in range(3):
                if step > 0:

                    @pl.when(has)
                    def _(i=i, origin=origin, sends=sends, recvs=recvs, step=step):
                        hop(i, place(i, origin), origin, me, sends.at[i, step], recvs.at[i, step - 1]).wait_recv()

                @pl.when(has & (to >= 0) & (to < parts))
                def _(i=i, origin=origin, to=to, sends=sends, recvs=recvs, step=step):
                    src = shared[i][0] if step == 0 else place(i, origin)
                    hop(i, src, origin, to, sends.at[i, step], recvs.at[i, step]).start()

        if step == 0:
            for k in range(parts - 1, 0, -1):
                to = lax.rem(me + k, parts)
                exchanged(k, to, me).start()
            owns = [
                pltpu.make_async_copy(src, target, own_sem.at[i])
                for i, (src, target) in enumerate(
                    (
                        (blocks.at[rows(me)], dst.at[rows(me), left : left + wide]),
                        (out, place(0, me)),
                        (small, place(1, me)),
                        (chosen, place(2, me)),
                    )
                )
            ]
            for copy in owns:
                copy.start()

    for copy in owns:
        copy.wait()
    for way, sends, recvs in streams:
        to, last = me + way, me - way * (parts - 1)
        for i in range(3):

            @pl.when((last >= 0) & (last < parts))
            def _(i=i, last=last, sends=sends, recvs=recvs):
                hop(i, place(i, last), last, me, sends.at[i, 0], recvs.at[i, parts - 2]).wait_recv()

            for step in range(parts - 1):
                origin = me - way * step

                @pl.when((origin >= 0) & (origin < parts) & (to >= 0) & (to < parts))
                def _(i=i, origin=origin, sends=sends, recvs=recvs, step=step):
                    hop(i, place(i, origin), origin, me, sends.at[i, step], recvs.at[i, step]).wait_send()

    for k in range(parts - 1, 0, -1):
        exchanged(k, lax.rem(me + k, parts), me).wait_send()
        exchanged(k, me, lax.rem(me + parts - k, parts)).wait_recv()


def gather_weights(blocks, out, small, chosen, cid):
    parts = lax.axis_size("expert")
    sem = pltpu.SemaphoreType.DMA
    rows, cols = blocks.shape[0], out.shape[1] + blocks.shape[1] + small.shape[1]
    return pl.pallas_call(
        functools.partial(weights_kernel, parts),
        out_shape=[
            jax.ShapeDtypeStruct((rows, cols), blocks.dtype),
            jax.ShapeDtypeStruct((rows, chosen.shape[1]), blocks.dtype),
        ],
        in_specs=[ANY] * 4,
        out_specs=[ANY] * 2,
        scratch_shapes=[sem((4,)), sem((parts - 1,)), sem((parts - 1,))] + [sem((3, parts - 1))] * 4,
        cost_estimate=transfer_cost(rows * (cols + chosen.shape[1])),
        compiler_params=pltpu.CompilerParams(collective_id=cid, has_side_effects=True),
        name="gather_weights",
    )(blocks, out, small, chosen)


def diagonal_mask(column_ref, row_ref, block):
    here = pl.ds(block * BLOCK, BLOCK)
    seg_query = column_ref[here, :]
    seg_key = row_ref[:, here]
    shape = (BLOCK, BLOCK)
    causal = lax.broadcasted_iota(jnp.int32, shape, 1) <= lax.broadcasted_iota(jnp.int32, shape, 0)
    same = (seg_query == seg_key) & causal
    return same | ((seg_key == 0) & (seg_query != 0))


def masked_scores(query, key_ref, column_ref, row_ref, block):
    scale = HEAD ** (-0.5)
    here = pl.ds(block * BLOCK, BLOCK)
    own = dot_right(query, key_ref[here, :]) * scale
    own = jnp.where(diagonal_mask(column_ref, row_ref, block), own, MASKED)
    if block == 0:
        return own
    ahead = dot_right(query, key_ref[: block * BLOCK, :]) * scale
    return jnp.concatenate([ahead, own], axis=1)


def row_block(owner, rows):
    return pl.ds(pl.multiple_of(owner * rows, rows), rows)


def attention_kernel(
    parts, column_ref, row_ref, query_ref, key_ref, value_ref, mixed_ref, lse_ref, heads_out, own_sem, send, recv
):
    head, heads = pl.program_id(0), pl.num_programs(0)
    me = lax.axis_index("expert")
    total = query_ref.shape[0]
    piece = total // parts

    @pl.when(head == 0)
    def _():
        greet_all(me, parts)

    def moved(h, k, origin, to):
        lanes = pl.ds(pl.multiple_of((origin * heads + h) * HEAD, HEAD), HEAD)
        return pltpu.make_async_remote_copy(
            src_ref=heads_out.at[h, row_block(to, piece)],
            dst_ref=mixed_ref.at[:, lanes],
            send_sem=send.at[h, k - 1],
            recv_sem=recv.at[h, k - 1],
            device_id={"expert": to},
            device_id_type=MESH,
        )

    def kept(h):
        lanes = pl.ds(pl.multiple_of((me * heads + h) * HEAD, HEAD), HEAD)
        return pltpu.make_async_copy(heads_out.at[h, row_block(me, piece)], mixed_ref.at[:, lanes], own_sem.at[h])

    for block in range(total // BLOCK):
        here = pl.ds(block * BLOCK, BLOCK)
        scores = masked_scores(query_ref[here, :], key_ref, column_ref, row_ref, block)
        top = jnp.max(scores, axis=1, keepdims=True)
        expd = jnp.exp(scores - top)
        mass = jnp.sum(expd, axis=1, keepdims=True)
        probs = (expd / mass).astype(jnp.bfloat16)
        mixed = dot_plain(probs, value_ref[: (block + 1) * BLOCK, :])
        heads_out[head, here, :] = mixed.astype(jnp.bfloat16)
        lse_ref[0, here, :] = top + jnp.log(mass)

    kept(head).start()
    for k in range(parts - 1, 0, -1):
        moved(head, k, me, lax.rem(me + k, parts)).start()

    @pl.when(head == heads - 1)
    def _():
        @pl.loop(0, heads)
        def _(h):
            kept(h).wait()
            for k in range(parts - 1, 0, -1):
                moved(h, k, me, lax.rem(me + k, parts)).wait_send()
                moved(h, k, lax.rem(me + parts - k, parts), me).wait_recv()


def head_specs(total, heads):
    return [
        pl.BlockSpec((total, HEAD), lambda h, part=part: (0, part * heads + h)) for part in range(3)
    ]


def run_attention(column, row, qkv, cid):
    total, heads = qkv.shape[0], qkv.shape[1] // (3 * HEAD)
    parts = lax.axis_size("expert")
    whole = pl.BlockSpec(memory_space=pltpu.VMEM)
    sem = pltpu.SemaphoreType.DMA
    return pl.pallas_call(
        functools.partial(attention_kernel, parts),
        grid=(heads,),
        in_specs=[whole, whole] + head_specs(total, heads),
        out_specs=[ANY, pl.BlockSpec((1, total, 1), lambda h: (h, 0, 0))],
        out_shape=[
            jax.ShapeDtypeStruct((total // parts, D), jnp.bfloat16),
            jax.ShapeDtypeStruct((heads, total, 1), jnp.float32),
        ],
        scratch_shapes=[
            pltpu.VMEM((heads, total, HEAD), jnp.bfloat16),
            sem((heads,)),
            sem((heads, parts - 1)),
            sem((heads, parts - 1)),
        ],
        compiler_params=pltpu.CompilerParams(
            dimension_semantics=("arbitrary",),
            vmem_limit_bytes=48 * 1024 * 1024,
            collective_id=cid,
            has_side_effects=True,
        ),
        cost_estimate=pl.CostEstimate(
            flops=0, bytes_accessed=200 * total * heads * HEAD, transcendentals=heads * total * total // 2
        ),
        name="attention",
    )(column, row, qkv, qkv, qkv)


def attention_back_kernel(
    parts,
    column_ref,
    row_ref,
    query_ref,
    key_ref,
    value_ref,
    lse_ref,
    sent_ref,
    back_query_ref,
    back_key_ref,
    back_value_ref,
    key_acc,
    value_acc,
    grads,
    own_sem,
    send,
    recv,
):
    head, heads = pl.program_id(0), pl.num_programs(0)
    me = lax.axis_index("expert")
    scale = HEAD ** (-0.5)
    total = query_ref.shape[0]
    piece = total // parts

    def moved(h, k, origin, to):
        lanes = pl.ds(pl.multiple_of(h * HEAD, HEAD), HEAD)
        return pltpu.make_async_remote_copy(
            src_ref=sent_ref.at[row_block(to, piece), lanes],
            dst_ref=grads.at[h, row_block(origin, piece)],
            send_sem=send.at[h, k - 1],
            recv_sem=recv.at[h, k - 1],
            device_id={"expert": to},
            device_id_type=MESH,
        )

    def kept(h):
        lanes = pl.ds(pl.multiple_of(h * HEAD, HEAD), HEAD)
        return pltpu.make_async_copy(
            sent_ref.at[row_block(me, piece), lanes], grads.at[h, row_block(me, piece)], own_sem.at[h]
        )

    @pl.when(head == 0)
    def _():
        greet_all(me, parts)

        @pl.loop(0, heads)
        def _(h):
            for k in range(parts - 1, 0, -1):
                moved(h, k, me, lax.rem(me + k, parts)).start()
            kept(h).start()

    kept(head).wait()
    for k in range(parts - 1, 0, -1):
        moved(head, k, lax.rem(me + parts - k, parts), me).wait_recv()
    key_acc[...] = jnp.zeros_like(key_acc)
    value_acc[...] = jnp.zeros_like(value_acc)
    for block in range(total // BLOCK):
        here = pl.ds(block * BLOCK, BLOCK)
        upto = pl.ds(0, (block + 1) * BLOCK)
        query, grad = query_ref[here, :], grads[head, here, :]
        scores = masked_scores(query, key_ref, column_ref, row_ref, block)
        probs = jnp.exp(scores - lse_ref[0, here, :])
        prob_back = dot_right(grad, value_ref[upto, :])
        delta = jnp.sum(probs * prob_back, axis=1, keepdims=True)
        score_grad = (probs * (prob_back - delta)).astype(jnp.bfloat16)
        back_query_ref[here, :] = (dot_plain(score_grad, key_ref[upto, :]) * scale).astype(jnp.bfloat16)
        key_acc[upto, :] += dot_left(score_grad, query)
        value_acc[upto, :] += dot_left(probs.astype(jnp.bfloat16), grad)
    back_key_ref[...] = (key_acc[...] * scale).astype(jnp.bfloat16)
    back_value_ref[...] = value_acc[...].astype(jnp.bfloat16)

    @pl.when(head == heads - 1)
    def _():
        @pl.loop(0, heads)
        def _(h):
            for k in range(parts - 1, 0, -1):
                moved(h, k, me, lax.rem(me + k, parts)).wait_send()


def run_attention_back(column, row, qkv, sent, lse, cid):
    total, heads = qkv.shape[0], qkv.shape[1] // (3 * HEAD)
    parts = lax.axis_size("expert")
    whole = pl.BlockSpec(memory_space=pltpu.VMEM)
    head = pl.BlockSpec((total, HEAD), lambda h: (0, h))
    sem = pltpu.SemaphoreType.DMA
    return pl.pallas_call(
        functools.partial(attention_back_kernel, parts),
        grid=(heads,),
        in_specs=[whole, whole]
        + head_specs(total, heads)
        + [pl.BlockSpec((1, total, 1), lambda h: (h, 0, 0)), ANY],
        out_specs=[head] * 3,
        out_shape=[jax.ShapeDtypeStruct((total, heads * HEAD), jnp.bfloat16)] * 3,
        scratch_shapes=[pltpu.VMEM((total, HEAD), jnp.float32)] * 2
        + [
            pltpu.VMEM((heads, total, HEAD), jnp.bfloat16),
            sem((heads,)),
            sem((heads, parts - 1)),
            sem((heads, parts - 1)),
        ],
        compiler_params=pltpu.CompilerParams(
            dimension_semantics=("arbitrary",),
            vmem_limit_bytes=48 * 1024 * 1024,
            collective_id=cid,
            has_side_effects=True,
        ),
        cost_estimate=pl.CostEstimate(
            flops=0, bytes_accessed=200 * total * heads * HEAD, transcendentals=heads * total * total // 2
        ),
        name="attention_back",
    )(column, row, qkv, qkv, qkv, lse, sent)


def own_lift(lift_ref, j):
    row = lax.broadcasted_iota(jnp.int32, (LANES, TILE), 0)
    own = (row >= j * RANK) & (row < (j + 1) * RANK)
    return jnp.where(own, lift_ref[...].astype(jnp.float32), 0.0).astype(jnp.bfloat16)


def gate_column(gates_ref, here, j):
    shape = (ROWS, LANES)
    mine = lax.broadcasted_iota(jnp.int32, shape, 1) == lax.axis_index("expert") * EXP_DEV + j
    return mine, jnp.sum(
        jnp.where(mine, gates_ref[here, :].astype(jnp.float32), 0.0), axis=1, keepdims=True
    )


def row_chunk(b, rows=None):
    rows = rows or ROWS
    return pl.ds(pl.multiple_of(b * rows, rows), rows)


def forward_kernel(
    rows_ref,
    gates_ref,
    down_ref,
    lift_gate_ref,
    lift_up_ref,
    in_gate_ref,
    in_up_ref,
    out_ref,
    *refs,
):
    output_ref, ranks_ref, gate_ref, up_ref, output_acc, stage, sems = refs
    j, f = pl.program_id(0), pl.program_id(1)
    total = rows_ref.shape[0]

    @pl.when((j == 0) & (f == 0))
    def _():
        @pl.loop(0, total // ROWS)
        def _(b):
            here = row_chunk(b)
            ranks_ref[here, :] = dot_right(rows_ref[here, :], down_ref[...]).astype(jnp.bfloat16)
            output_acc[here, :] = jnp.zeros((ROWS, D), jnp.float32)

    lift_gate, lift_up = own_lift(lift_gate_ref, j), own_lift(lift_up_ref, j)

    @pl.loop(0, total // ROWS)
    def _(b):
        here = row_chunk(b)
        rows = rows_ref[here, :]
        _, column = gate_column(gates_ref, here, j)
        gate = dot_plain(rows, in_gate_ref[0]) + dot_plain(ranks_ref[here, :], lift_gate)
        up = dot_plain(rows, in_up_ref[0]) + dot_plain(ranks_ref[here, :], lift_up)
        gate_ref[0, here, :] = gate.astype(jnp.bfloat16)
        up_ref[0, here, :] = up.astype(jnp.bfloat16)
        hidden = (column * (gate * jax.nn.sigmoid(gate) * up)).astype(jnp.bfloat16)
        output_acc[here, :] += dot_plain(hidden, out_ref[0])

    @pl.when((j == EXP_DEV - 1) & (f == FF // TILE - 1))
    def _():
        def copy(b):
            slot = lax.rem(b, 2)
            here = row_chunk(b, stage.shape[1])
            return pltpu.make_async_copy(stage.at[slot], output_ref.at[here], sems.at[slot])

        steps = total // stage.shape[1]

        @pl.loop(0, steps)
        def _(b):
            @pl.when(b >= 2)
            def _():
                copy(b - 2).wait()

            here = row_chunk(b, stage.shape[1])
            stage[lax.rem(b, 2)] = output_acc[here, :].astype(jnp.bfloat16)
            copy(b).start()

        for b in range(steps - 2, steps):
            copy(b).wait()


def weight_specs():
    tiles = FF // TILE
    return [
        pl.BlockSpec((LANES, TILE), lambda j, f: (0, f)),
        pl.BlockSpec((LANES, TILE), lambda j, f: (0, f + tiles)),
        pl.BlockSpec((1, D, TILE), lambda j, f: (j, 0, f)),
        pl.BlockSpec((1, D, TILE), lambda j, f: (j, 0, f + tiles)),
        pl.BlockSpec((1, TILE, D), lambda j, f: (j, f, 0)),
    ]


EXPERT_PARAMS = pltpu.CompilerParams(
    dimension_semantics=("arbitrary", "arbitrary"), vmem_limit_bytes=60 * 1024 * 1024
)


def experts_forward(rows, gates, down, lift, matrix_in, matrix_out):
    total = rows.shape[0]
    kept = pl.BlockSpec((1, total, TILE), lambda j, f: (j, 0, f))
    return pl.pallas_call(
        forward_kernel,
        grid=(EXP_DEV, FF // TILE),
        in_specs=[VMEM] * 3 + weight_specs(),
        out_specs=[
            ANY,
            pl.BlockSpec((total, LANES), lambda j, f: (0, 0), pipeline_mode=pl.Buffered(1)),
            kept,
            kept,
        ],
        out_shape=[
            jax.ShapeDtypeStruct((total, D), jnp.bfloat16),
            jax.ShapeDtypeStruct((total, LANES), jnp.bfloat16),
            jax.ShapeDtypeStruct((EXP_DEV, total, FF), jnp.bfloat16),
            jax.ShapeDtypeStruct((EXP_DEV, total, FF), jnp.bfloat16),
        ],
        scratch_shapes=[
            pltpu.VMEM((total, D), jnp.float32),
            pltpu.VMEM((2, 160, D), jnp.bfloat16),
            pltpu.SemaphoreType.DMA((2,)),
        ],
        compiler_params=EXPERT_PARAMS,
        cost_estimate=pl.CostEstimate(
            flops=10 * EXP_DEV * total * D * FF,
            bytes_accessed=EXP_DEV * 6 * D * FF + 8 * total * D,
            transcendentals=EXP_DEV * total * FF,
        ),
        name="experts_forward",
    )(rows, gates, down, lift, lift, matrix_in, matrix_in, matrix_out)


def backward_kernel(
    parts,
    gates_ref,
    ranks_ref,
    down_ref,
    lift_gate_ref,
    lift_up_ref,
    in_gate_ref,
    in_up_ref,
    out_ref,
    gate_ref,
    up_ref,
    *refs,
):
    blocks, refs = refs[:parts], refs[parts:]
    slot_ref, rank_ref, lift_grad_gate_ref, lift_grad_up_ref, upstream, slot_acc, rank_acc, gate_acc, lift_acc, stage, sems = refs
    j, f = pl.program_id(0), pl.program_id(1)
    total = upstream.shape[0]

    @pl.when((j == 0) & (f == 0))
    def _():
        piece = total // parts
        copies = []
        for shift in range(parts):
            owner = lax.rem(lax.axis_index("expert") + parts - shift, parts)
            there = row_chunk(owner, piece)
            copies.append(pltpu.make_async_copy(blocks[shift], upstream.at[there], sems.at[shift]))
        for copy in copies:
            copy.start()

        @pl.loop(0, total // ROWS)
        def _(b):
            here = row_chunk(b)
            slot_acc[here, :] = jnp.zeros((ROWS, D), jnp.float32)
            rank_acc[here, :] = jnp.zeros((ROWS, LANES), jnp.float32)
            gate_acc[here, :] = jnp.zeros((ROWS, LANES), jnp.float32)

        for copy in copies:
            copy.wait()

    lift_acc[...] = jnp.zeros_like(lift_acc)
    lift_gate, lift_up = own_lift(lift_gate_ref, j), own_lift(lift_up_ref, j)

    @pl.loop(0, total // ROWS)
    def _(b):
        here = row_chunk(b)
        mine, column = gate_column(gates_ref, here, j)
        raw = dot_right(upstream[here, :], out_ref[0])
        gate = gate_ref[0, here, :].astype(jnp.float32)
        up = up_ref[0, here, :].astype(jnp.float32)
        sigma = jax.nn.sigmoid(gate)
        silu = gate * sigma
        gate_grad = jnp.sum(raw * (silu * up), axis=1, keepdims=True)
        back = raw * column
        to_gate = (back * up * (sigma + silu * (1.0 - sigma))).astype(jnp.bfloat16)
        to_up = (back * silu).astype(jnp.bfloat16)
        slot_acc[here, :] += dot_right(to_gate, in_gate_ref[0]) + dot_right(
            to_up, in_up_ref[0]
        )
        rank_acc[here, :] += dot_right(to_gate, lift_gate) + dot_right(to_up, lift_up)
        gate_acc[here, :] += jnp.where(mine, gate_grad, 0.0)
        lift_acc[0] += dot_left(ranks_ref[here, :], to_gate)
        lift_acc[1] += dot_left(ranks_ref[here, :], to_up)

    own = row_chunk(j, RANK)
    lift_grad_gate_ref[0] = lift_acc[0, own, :]
    lift_grad_up_ref[0] = lift_acc[1, own, :]

    @pl.when((j == EXP_DEV - 1) & (f == FF // TILE - 1))
    def _():
        def copy(b):
            slot = lax.rem(b, 2)
            here = row_chunk(b, stage.shape[1])
            return pltpu.make_async_copy(stage.at[slot], slot_ref.at[here], sems.at[slot])

        steps = total // stage.shape[1]

        @pl.loop(0, steps)
        def _(b):
            @pl.when(b >= 2)
            def _():
                copy(b - 2).wait()

            here = row_chunk(b, stage.shape[1])
            rank_low = rank_acc[here, :].astype(jnp.bfloat16)
            rank_ref[here, :] = rank_low
            slot = slot_acc[here, :] + dot_plain(rank_low, down_ref[...])
            wide = gate_acc[here, :]
            high = wide.astype(jnp.bfloat16).astype(jnp.float32)
            both = high + pltpu.roll(wide - high, LANES // 2, 1)
            stage[lax.rem(b, 2), :, :D] = slot.astype(jnp.bfloat16)
            stage[lax.rem(b, 2), :, D:] = both.astype(jnp.bfloat16)
            copy(b).start()

        for b in range(steps - 2, steps):
            copy(b).wait()


def experts_backward(blocks, gates, ranks, down, lift, matrix_in, matrix_out, gate, up):
    total, parts = gates.shape[0], len(blocks)
    grad = pl.BlockSpec((1, RANK, TILE), lambda j, f: (j, 0, f))
    kept = pl.BlockSpec((1, total, TILE), lambda j, f: (j, 0, f))
    return pl.pallas_call(
        functools.partial(backward_kernel, parts),
        grid=(EXP_DEV, FF // TILE),
        in_specs=[VMEM] * 3 + weight_specs() + [kept, kept] + [ANY] * parts,
        out_specs=[
            ANY,
            pl.BlockSpec((total, LANES), lambda j, f: (0, 0), pipeline_mode=pl.Buffered(1)),
            grad,
            grad,
        ],
        out_shape=[
            jax.ShapeDtypeStruct((total, D + LANES), jnp.bfloat16),
            jax.ShapeDtypeStruct((total, LANES), jnp.bfloat16),
            jax.ShapeDtypeStruct((EXP_DEV, RANK, FF), jnp.float32),
            jax.ShapeDtypeStruct((EXP_DEV, RANK, FF), jnp.float32),
        ],
        scratch_shapes=[
            pltpu.VMEM((total, D), jnp.bfloat16),
            pltpu.VMEM((total, D), jnp.float32),
            pltpu.VMEM((total, LANES), jnp.float32),
            pltpu.VMEM((total, LANES), jnp.float32),
            pltpu.VMEM((2, LANES, TILE), jnp.float32),
            pltpu.VMEM((2, 160, D + LANES), jnp.bfloat16),
            pltpu.SemaphoreType.DMA((parts,)),
        ],
        compiler_params=EXPERT_PARAMS,
        cost_estimate=pl.CostEstimate(
            flops=12 * EXP_DEV * total * D * FF,
            bytes_accessed=EXP_DEV * 6 * D * FF + 8 * total * D,
            transcendentals=EXP_DEV * total * FF,
        ),
        name="experts_backward",
    )(gates, ranks, down, lift, lift, matrix_in, matrix_in, matrix_out, gate, up, *blocks)


def pick_kernel(experts, chosen_ref, small_ref, picked_ref, router_ref, gain_ref):
    row = lax.broadcasted_iota(jnp.int32, (LANES, LANES), 0)
    same = row == lax.broadcasted_iota(jnp.int32, (LANES, LANES), 1)
    every = same.astype(jnp.float32).astype(jnp.bfloat16)
    router = (same & (row < experts)).astype(jnp.float32).astype(jnp.bfloat16)
    gain_row = lax.broadcasted_iota(jnp.int32, (8, LANES), 0) + 64
    gain = gain_row == lax.broadcasted_iota(jnp.int32, (8, LANES), 1)
    picked_ref[...] = dot_right(every, chosen_ref[...]).astype(jnp.bfloat16)
    router_ref[...] = dot_right(router, small_ref[...]).astype(jnp.bfloat16)
    gain_ref[...] = dot_right(gain.astype(jnp.float32).astype(jnp.bfloat16), small_ref[...])


def pick_rows(chosen, dense, at, experts):
    return pl.pallas_call(
        functools.partial(pick_kernel, experts),
        grid=(1,),
        in_specs=[VMEM, pl.BlockSpec((D, LANES), lambda i: (0, at // LANES))],
        out_specs=[all_of(LANES, D), all_of(LANES, D), all_of(8, D)],
        out_shape=[
            jax.ShapeDtypeStruct((LANES, D), jnp.bfloat16),
            jax.ShapeDtypeStruct((LANES, D), jnp.bfloat16),
            jax.ShapeDtypeStruct((8, D), jnp.float32),
        ],
        name="pick_rows",
    )(chosen, dense)


def first_kernel(query_ref, key_ref, value_ref, rank_ref, down_ref, *refs):
    weights, out_ref = refs[:3], refs[3]
    total = dot_right(query_ref[...], weights[0][...]) + dot_right(key_ref[...], weights[1][...])
    total = total + dot_right(value_ref[...], weights[2][...]) + dot_plain(rank_ref[...], down_ref[...])
    out_ref[...] = total.astype(jnp.bfloat16)


def first_products(backs, ranks, down, dense):
    total, width = backs[0].shape
    tile = 512
    weights = [
        pl.BlockSpec((tile, width), lambda i, part=part: (i, D // width + part)) for part in range(3)
    ]
    return pl.pallas_call(
        first_kernel,
        grid=(D // tile,),
        in_specs=[VMEM] * 4 + [pl.BlockSpec((RANK, tile), lambda i: (0, i))] + weights,
        out_specs=pl.BlockSpec((total, tile), lambda i: (0, i)),
        out_shape=jax.ShapeDtypeStruct((total, D), jnp.bfloat16),
        compiler_params=pltpu.CompilerParams(vmem_limit_bytes=48 * 1024 * 1024),
        cost_estimate=pl.CostEstimate(
            flops=6 * total * width * D, bytes_accessed=6 * width * D + 2 * total * D, transcendentals=0
        ),
        name="first_products",
    )(*backs, ranks, down, dense, dense, dense)


def sublayer_params():
    return pltpu.CompilerParams(
        dimension_semantics=("arbitrary",), vmem_limit_bytes=56 * 1024 * 1024
    )


def all_of(*shape):
    return pl.BlockSpec(shape, lambda i: (0,) * len(shape))


def qkv_kernel(tokens_ref, gain_ref, down_ref, lift_ref, weight_ref, normed_ref, rank_ref, qkv_ref):
    @pl.when(pl.program_id(0) == 0)
    def _():
        rows = tokens_ref.shape[0] // 4

        @pl.loop(0, 4)
        def _(b):
            here = row_chunk(b, rows)
            values = tokens_ref[here, :].astype(jnp.float32)
            normed = (values * norm_inverse(values) * gain_ref[...]).astype(jnp.bfloat16)
            normed_ref[here, :] = normed
            rank_ref[here, :] = dot_right(normed, down_ref[...]).astype(jnp.bfloat16)

    total = dot_plain(normed_ref[...], weight_ref[...]) + dot_plain(rank_ref[...], lift_ref[...])
    qkv_ref[...] = total.astype(jnp.bfloat16)


def project_qkv(tokens, gain, down, lift, dense):
    total, width = tokens.shape[0], lift.shape[1] // 3
    return pl.pallas_call(
        qkv_kernel,
        grid=(3,),
        in_specs=[
            VMEM,
            VMEM,
            VMEM,
            pl.BlockSpec((RANK, width), lambda i: (0, i)),
            pl.BlockSpec((D, width), lambda i: (0, D // width + i)),
        ],
        out_specs=[
            all_of(total, D),
            all_of(total, RANK),
            pl.BlockSpec((total, width), lambda i: (0, i)),
        ],
        out_shape=[
            jax.ShapeDtypeStruct((total, D), jnp.bfloat16),
            jax.ShapeDtypeStruct((total, RANK), jnp.bfloat16),
            jax.ShapeDtypeStruct((total, 3 * width), jnp.bfloat16),
        ],
        compiler_params=sublayer_params(),
        cost_estimate=pl.CostEstimate(
            flops=6 * total * D * width, bytes_accessed=6 * D * width + 8 * total * D, transcendentals=0
        ),
        name="project_qkv",
    )(tokens, gain, down, lift, dense)


def middle_kernel(
    experts,
    mixed_ref,
    tokens_ref,
    down_mix_ref,
    lift_mix_ref,
    gain_ref,
    down_route_ref,
    router_ref,
    lift_route_ref,
    routed_ref,
    out_ref,
    middle_ref,
    rank_mix_ref,
    inverse_ref,
    second_ref,
    rank_route_ref,
    probs_ref,
    gates_ref,
):
    i = pl.program_id(0)
    tile = out_ref.shape[1]

    @pl.when(i == 0)
    def _():
        rank_mix_ref[...] = dot_right(mixed_ref[...], down_mix_ref[...]).astype(jnp.bfloat16)

    here = pl.ds(pl.multiple_of(i * tile, tile), tile)
    branch = dot_plain(mixed_ref[...], out_ref[...]) + dot_plain(rank_mix_ref[...], lift_mix_ref[...])
    middle_ref[:, here] = tokens_ref[...].astype(jnp.float32) + branch

    @pl.when(i == D // tile - 1)
    def _():
        middle = middle_ref[...]
        inverse = norm_inverse(middle)
        inverse_ref[...] = inverse
        second = (middle * inverse * gain_ref[...]).astype(jnp.bfloat16)
        second_ref[...] = second
        rank_route = dot_right(second, down_route_ref[...]).astype(jnp.bfloat16)
        rank_route_ref[...] = rank_route
        logits = dot_right(second, router_ref[...]) + dot_plain(rank_route, lift_route_ref[...])
        lane = lax.broadcasted_iota(jnp.int32, logits.shape, 1)
        logits = jnp.where(lane < experts, logits, MASKED)
        exped = jnp.exp(logits - jnp.max(logits, axis=1, keepdims=True))
        probs = exped / jnp.sum(exped, axis=1, keepdims=True)
        probs_ref[...] = probs
        gates_ref[...] = (probs * routed_ref[...]).astype(jnp.bfloat16)


def finish_attention(experts, mixed, tokens, down_mix, lift_mix, gain, down_route, router, lift_route, routed, out_matrix):
    piece, tile = tokens.shape[0], 512
    column = lambda i: (0, i)
    return pl.pallas_call(
        functools.partial(middle_kernel, experts),
        grid=(D // tile,),
        in_specs=[
            VMEM,
            pl.BlockSpec((piece, tile), column),
            VMEM,
            pl.BlockSpec((RANK, tile), column),
            VMEM,
            VMEM,
            VMEM,
            VMEM,
            VMEM,
            pl.BlockSpec((D, tile), column),
        ],
        out_specs=[
            all_of(piece, D),
            all_of(piece, RANK),
            all_of(piece, 1),
            all_of(piece, D),
            all_of(piece, RANK),
            all_of(piece, LANES),
            all_of(piece, LANES),
        ],
        out_shape=[
            jax.ShapeDtypeStruct((piece, D), jnp.float32),
            jax.ShapeDtypeStruct((piece, RANK), jnp.bfloat16),
            jax.ShapeDtypeStruct((piece, 1), jnp.float32),
            jax.ShapeDtypeStruct((piece, D), jnp.bfloat16),
            jax.ShapeDtypeStruct((piece, RANK), jnp.bfloat16),
            jax.ShapeDtypeStruct((piece, LANES), jnp.float32),
            jax.ShapeDtypeStruct((piece, LANES), jnp.bfloat16),
        ],
        compiler_params=sublayer_params(),
        cost_estimate=pl.CostEstimate(
            flops=2 * piece * D * D, bytes_accessed=2 * D * D + 12 * piece * D, transcendentals=piece * LANES
        ),
        name="finish_attention",
    )(mixed, tokens, down_mix, lift_mix, gain, down_route, router, lift_route, routed, out_matrix)


def middle_back_kernel(
    slot_ref,
    probs_ref,
    routed_ref,
    middle_ref,
    inverse_ref,
    cotangent_ref,
    gain_ref,
    router_ref,
    lift_route_ref,
    down_route_ref,
    lift_mix_ref,
    down_mix_ref,
    out_ref,
    mixed_ref,
    grad_ref,
    branch_ref,
    logit_ref,
    rank_route_ref,
    rank_mix_ref,
):
    @pl.when(pl.program_id(0) == 0)
    def _():
        parts = slot_ref[:, D:]
        prob_grad = (parts + pltpu.roll(parts, LANES // 2, 1)) * routed_ref[...]
        probs = probs_ref[...]
        logit_grad = probs * (prob_grad - jnp.sum(probs * prob_grad, axis=1, keepdims=True))
        logit_grad = logit_grad.astype(jnp.bfloat16)
        logit_ref[...] = logit_grad
        rank_route_grad = dot_right(logit_grad, lift_route_ref[...]).astype(jnp.bfloat16)
        rank_route_ref[...] = rank_route_grad
        upstream = slot_ref[:, :D] + dot_plain(logit_grad, router_ref[...])
        upstream = upstream + dot_plain(rank_route_grad, down_route_ref[...])
        middle_grad = cotangent_ref[...].astype(jnp.float32) + norm_backward(
            middle_ref[...], inverse_ref[...], gain_ref[...], upstream
        )
        grad_ref[...] = middle_grad
        branch_ref[...] = middle_grad.astype(jnp.bfloat16)
        rank_mix_ref[...] = dot_right(branch_ref[...], lift_mix_ref[...]).astype(jnp.bfloat16)

    mixed = dot_right(branch_ref[...], out_ref[...]) + dot_plain(rank_mix_ref[...], down_mix_ref[...])
    mixed_ref[...] = mixed.astype(jnp.bfloat16)


def middle_backward(
    width, slot, probs, routed, middle, inverse, cotangent, gain, router, lift_route, down_route, lift_mix, down_mix, out_matrix
):
    piece = middle.shape[0]
    return pl.pallas_call(
        middle_back_kernel,
        grid=(D // width,),
        in_specs=[VMEM] * 11
        + [
            pl.BlockSpec((RANK, width), lambda i: (0, i)),
            pl.BlockSpec((width, D), lambda i: (i, 0)),
        ],
        out_specs=[
            pl.BlockSpec((piece, width), lambda i: (i, 0)),
            all_of(piece, D),
            all_of(piece, D),
            all_of(piece, LANES),
            all_of(piece, RANK),
            all_of(piece, RANK),
        ],
        out_shape=[
            jax.ShapeDtypeStruct((piece * D // width, width), jnp.bfloat16),
            jax.ShapeDtypeStruct((piece, D), jnp.float32),
            jax.ShapeDtypeStruct((piece, D), jnp.bfloat16),
            jax.ShapeDtypeStruct((piece, LANES), jnp.bfloat16),
            jax.ShapeDtypeStruct((piece, RANK), jnp.bfloat16),
            jax.ShapeDtypeStruct((piece, RANK), jnp.bfloat16),
        ],
        compiler_params=sublayer_params(),
        cost_estimate=pl.CostEstimate(
            flops=2 * piece * D * D, bytes_accessed=2 * D * D + 24 * piece * D, transcendentals=0
        ),
        name="middle_backward",
    )(slot, probs, routed, middle, inverse, cotangent, gain, router, lift_route, down_route, lift_mix, down_mix, out_matrix)


def norm_inverse(values):
    return lax.rsqrt(jnp.mean(values * values, axis=-1, keepdims=True) + EPSILON)


def norm_backward(values, inverse, gain_row, upstream):
    scaled = upstream * gain_row
    return inverse * scaled - values * inverse**3 * jnp.mean(
        scaled * values, axis=-1, keepdims=True
    )


def segments_of(lengths, places):
    upto = jnp.arange(lengths.shape[0])
    limits = PROMPT + jnp.sum(
        jnp.where(upto[:, None] <= upto[None, :], lengths[:, None], 0), axis=0
    )
    passed = jnp.sum((places[:, None] >= limits[None, :]).astype(jnp.int32), axis=1)
    return jnp.where(places < PROMPT, 0, 1 + passed)


def body(
    tokens,
    cotangent,
    norm_gains,
    qkv_weight,
    out_weight,
    router_weight,
    adapter_down,
    adapter_qkv,
    adapter_out,
    adapter_router,
    expert_input,
    expert_output,
    expert_down,
    expert_lift,
    routes,
    adapter_ids,
    cont_lengths,
):
    low = jnp.bfloat16
    piece = tokens.shape[0]
    parts = lax.axis_size("expert")
    groups = lax.axis_size("dp")
    ways = parts * groups
    me = lax.axis_index("expert")
    total = parts * piece
    experts = EXP_DEV * parts
    width = D // parts
    share = D // ways
    route_rows = ADAPTERS * RANK // ways
    adapter = adapter_ids[0]

    matrix_out = lax.all_gather(expert_output, "dp", axis=1, tiled=True)

    group_ids = lax.all_gather(adapter_ids, "dp", axis=0, tiled=True)
    hot = group_ids[:, None] == jnp.arange(ADAPTERS, dtype=jnp.int32)
    group_hot = hot.astype(jnp.float32)
    adapter_cols = expert_lift.shape[3]
    pairs = jnp.stack([expert_down.transpose(0, 2, 3, 1), expert_lift])
    pairs = pairs.transpose(2, 0, 1, 3, 4).reshape(ADAPTERS, 2 * EXP_DEV * RANK * adapter_cols)
    pairs = dot_plain(hot.astype(low), pairs).astype(low)
    pairs = lax.all_to_all(
        pairs.reshape(groups, 2 * EXP_DEV * RANK, adapter_cols), "dp", split_axis=0, concat_axis=0, tiled=True
    )
    pairs = pairs.reshape(groups, 2, EXP_DEV * RANK, adapter_cols).transpose(1, 2, 0, 3)
    pairs = pairs.reshape(2, EXP_DEV * RANK, D)
    pairs = jnp.pad(pairs, ((0, 0), (0, LANES - EXP_DEV * RANK), (0, 0)))

    def columns(array, upto):
        return jnp.pad(array, ((0, share - array.shape[0]), (0, upto - array.shape[1])))

    adapters = jnp.concatenate(
        [
            adapter_down.reshape(share, ADAPTERS * 3 * RANK),
            adapter_out.reshape(ADAPTERS * RANK, share).T,
            adapter_qkv.reshape(ADAPTERS * RANK, 3, share).transpose(2, 1, 0).reshape(share, 3 * LANES),
        ],
        axis=1,
    )
    row = jnp.arange(LANES, dtype=jnp.int32)[None, :]
    ids = group_ids[:, None]
    wanted = jnp.where(
        row < 48,
        ids * 48 + row,
        jnp.where(
            row < 64,
            384 + ids * RANK + row - 48,
            jnp.where(row < 112, 512 + LANES * ((row - 64) // RANK) + ids * RANK + (row - 64) % RANK, -1),
        ),
    ).reshape(1, groups * LANES)
    chosen = jnp.arange(adapters.shape[1], dtype=jnp.int32)[:, None] == wanted
    chosen = dot_plain(adapters, chosen.astype(low)).astype(low)

    qkv_blocks = (
        qkv_weight.reshape(share, 3, parts, width).transpose(2, 0, 1, 3).reshape(parts * share, 3 * width)
    )
    small = jnp.concatenate(
        [columns(router_weight, 32), columns(adapter_router, 32), columns(norm_gains.T, 64)], axis=1
    )
    dense_line, chosen_line = gather_weights(qkv_blocks, out_weight, small, chosen, 0)
    chosen_all = lax.all_to_all(
        chosen_line.reshape(parts * share, groups, LANES).transpose(1, 0, 2),
        "dp",
        split_axis=0,
        concat_axis=0,
        tiled=True,
    ).reshape(D, LANES)
    dense_line, expert_input, matrix_out, chosen_all, pairs = lax.optimization_barrier(
        (dense_line, expert_input, matrix_out, chosen_all, pairs)
    )
    dense_all = lax.all_gather(dense_line, "dp", axis=0, tiled=True)
    (tokens_all,) = line_gather([tokens], 1, 2)
    matrix_in = lax.all_gather(expert_input, "dp", axis=1, tiled=True)
    small_at = D + 3 * width

    picked, router_rows, gain_rows = pick_rows(chosen_all, dense_all, small_at, experts)
    down_query, down_mix, down_route = picked[:16], picked[16:32], picked[32:48]
    lift_mix = picked[48:64]
    lift_query = (
        picked[64:112].reshape(3, RANK, ways, share).transpose(1, 2, 0, 3).reshape(RANK, 3, parts, width)
    )
    lift_query = lax.dynamic_index_in_dim(lift_query, me, 2, keepdims=False).reshape(RANK, 3 * width)
    by_owner = dense_all[:, small_at : small_at + LANES].reshape(ways, share, LANES)
    lift_route = lax.dynamic_slice_in_dim(
        by_owner[:, :route_rows, 32 : 32 + experts].reshape(ADAPTERS * RANK, experts),
        adapter * RANK,
        RANK,
        0,
    )
    lift_route = jnp.pad(lift_route, ((0, 0), (0, LANES - experts)))
    routed = jnp.any(routes[:, :, None] == jnp.arange(LANES, dtype=jnp.int32), axis=1).astype(jnp.float32)
    def shifted(array, by):
        return lax.ppermute(array, "expert", [(i, (i + by) % parts) for i in range(parts)])

    early, tokens_all = lax.optimization_barrier((cotangent, tokens_all))
    early_shifts, late_shifts = [1], list(range(2, parts))
    moved = {s: shifted(early, s) for s in early_shifts}

    normed_low, rank_query, qkv_low = project_qkv(
        tokens_all, gain_rows[0:1], down_query, lift_query, dense_all
    )
    segments = segments_of(cont_lengths[0], jnp.arange(total, dtype=jnp.int32))
    segment_column, segment_row = segments[:, None], segments[None, :]
    mixed_low, log_mass = run_attention(segment_column, segment_row, qkv_low, 3)

    middle, rank_mix, inverse_second, second_low, rank_route, router_probs, gates = finish_attention(
        experts,
        mixed_low,
        tokens,
        down_mix,
        lift_mix,
        gain_rows[1:2],
        down_route,
        router_rows,
        lift_route,
        routed,
        dense_all,
    )
    held = lax.optimization_barrier([second_low] + [moved[s] for s in early_shifts])
    second_low = held[0]
    moved.update(zip(early_shifts, held[1:]))
    second_all, gates_all = line_gather([second_low, gates], 4, 2)

    late, second_all = lax.optimization_barrier((cotangent, second_all))
    moved.update({s: shifted(late, s) for s in late_shifts})
    cotangents = [cotangent] + [moved[s] for s in range(1, parts)]
    output_terms, ranks, gate, up = experts_forward(
        second_all, gates_all, pairs[0], pairs[1], matrix_in, matrix_out
    )
    output_sum = lax.psum_scatter(output_terms, "expert", scatter_dimension=0, tiled=True)
    slot_terms, rank_expert_grad, lift_gate_grad, lift_up_grad = experts_backward(
        cotangents, gates_all, ranks, pairs[0], pairs[1], matrix_in, matrix_out, gate, up
    )
    slot_sum = line_reduce(slot_terms, 5, 2)
    slot_sum, output_sum = lax.optimization_barrier((slot_sum, output_sum))

    lift_sent = jnp.concatenate([lift_gate_grad, lift_up_grad], axis=2).reshape(EXP_DEV * RANK, D)
    down_sent = dot_left(rank_expert_grad[:, : EXP_DEV * RANK], second_all)
    expert_sent = (
        jnp.concatenate([lift_sent, down_sent], axis=0)
        .astype(low)
        .reshape(2 * EXP_DEV * RANK, groups, -1)
        .transpose(1, 0, 2)
    )
    expert_got = lax.all_to_all(expert_sent, "dp", split_axis=0, concat_axis=0, tiled=True)
    by_adapter = jnp.einsum(
        "ga,gkc->akc", group_hot, expert_got.astype(jnp.float32), precision=lax.Precision.HIGHEST
    ).reshape(ADAPTERS, 2, EXP_DEV, RANK, -1)
    explift_grad = by_adapter[:, 0].transpose(1, 0, 2, 3)
    expdown_grad = by_adapter[:, 1].transpose(1, 3, 0, 2)

    mixed_grad, middle_grad, branch_grad, logit_grad, rank_route_grad, rank_mix_grad = middle_backward(
        width,
        slot_sum,
        router_probs,
        routed,
        middle,
        inverse_second,
        cotangent,
        gain_rows[1:2],
        router_rows,
        lift_route,
        down_route,
        lift_mix,
        down_mix,
        dense_all,
    )

    back_query, back_key, back_value = run_attention_back(
        segment_column, segment_row, qkv_low, mixed_grad, log_mass, 6
    )
    qkv_back = jnp.concatenate([back_query, back_key, back_value], axis=1)
    rank_query_grad = dot_right(qkv_back, lift_query).astype(low)
    first_terms = first_products([back_query, back_key, back_value], rank_query_grad, down_query, dense_all)
    lift_query_grad = lax.dynamic_update_slice(
        jnp.zeros((RANK, 3, parts, width), jnp.float32),
        dot_left(rank_query, qkv_back).reshape(RANK, 3, 1, width),
        (0, 0, me, 0),
    )
    downs = jnp.concatenate(
        [
            dot_left(rank_query_grad, normed_low),
            dot_left(rank_mix_grad, mixed_low),
            dot_left(rank_route_grad, second_low),
            dot_left(rank_mix, branch_grad),
        ]
    )
    owned = jnp.concatenate(
        [
            downs.reshape(4 * RANK, ways, share).transpose(1, 0, 2).reshape(ways, -1),
            lift_query_grad.reshape(RANK, ways, 3 * share).transpose(1, 0, 2).reshape(ways, -1),
            jnp.broadcast_to(dot_left(rank_route, logit_grad)[:, :experts].reshape(1, -1), (ways, RANK * experts)),
        ],
        axis=1,
    ).astype(low)
    first_terms, output_sum = lax.optimization_barrier((first_terms, output_sum))
    first_grad = lax.psum_scatter(first_terms, "expert", scatter_dimension=0, tiled=True).astype(jnp.float32)
    got = lax.all_to_all(owned, ("dp", "expert"), split_axis=0, concat_axis=0, tiled=True)
    inputs = tokens.astype(jnp.float32)
    inverse_first = norm_inverse(inputs)
    input_grad = (
        middle_grad + norm_backward(inputs, inverse_first, gain_rows[0:1], first_grad)
    ).astype(low)
    summed = jnp.einsum(
        "ga,gek->ak",
        group_hot,
        got.astype(jnp.float32).reshape(groups, parts, -1),
        precision=lax.Precision.HIGHEST,
    )
    n_down, n_qkv = 4 * RANK * share, 3 * RANK * share
    downs = summed[:, :n_down].reshape(ADAPTERS, 4, RANK, share)
    down_grad = downs[:, :3].transpose(3, 0, 1, 2)
    proj_grad = downs[:, 3]
    qkv_grad = summed[:, n_down : n_down + n_qkv].reshape(ADAPTERS, RANK, 3 * share)
    router_grad = lax.dynamic_slice_in_dim(
        summed[:, n_down + n_qkv :].reshape(ADAPTERS * RANK, experts),
        (lax.axis_index("dp") * parts + me) * route_rows,
        route_rows,
        0,
    )
    layer_output = (middle + output_sum.astype(jnp.float32)).astype(low)
    return (
        layer_output,
        input_grad,
        down_grad,
        qkv_grad,
        proj_grad,
        router_grad,
        expdown_grad,
        explift_grad,
    )


def solution(mesh):
    placed = (
        P(("dp", "expert"), None),
        P(("dp", "expert"), None),
        P(None, ("dp", "expert")),
        P(("dp", "expert"), None),
        P(("dp", "expert"), None),
        P(("dp", "expert"), None),
        P(("dp", "expert"), None, None, None),
        P(None, None, ("dp", "expert")),
        P(None, None, ("dp", "expert")),
        P(("dp", "expert"), None),
        P("expert", "dp", None),
        P("expert", "dp", None),
        P("expert", "dp", None, None),
        P("expert", None, None, "dp"),
        P(("dp", "expert"), None),
        P("dp"),
        P("dp", None),
    )
    return jax.shard_map(
        body,
        mesh=mesh,
        in_specs=placed,
        out_specs=(
            P(("dp", "expert"), None),
            P(("dp", "expert"), None),
            P(("dp", "expert"), None, None, None),
            P(None, None, ("dp", "expert")),
            P(None, None, ("dp", "expert")),
            P(("dp", "expert"), None),
            P("expert", "dp", None, None),
            P("expert", None, None, "dp"),
        ),
        check_vma=False,
    )
```

```python
import functools

import jax
import jax.numpy as jnp
from jax import lax
from jax.experimental import pallas as pl
from jax.experimental.pallas import tpu as pltpu
from jax.sharding import PartitionSpec as P

D = 2048
HEAD = 128
FF = 1024
RANK = 16
ADAPTERS = 8
EXP_DEV = 4
PROMPT = 1024
EPSILON = 1e-05
MASKED = -1e30
LANES = 128
BLOCK = 256
ROWS = 1280
TILE = 512
HALF = EXP_DEV // 2
SMALL = 1024

MESH = pl.DeviceIdType.MESH
ANY = pl.BlockSpec(memory_space=pl.ANY)
VMEM = pl.BlockSpec(memory_space=pltpu.VMEM)


def dot_plain(left, right):
    return jnp.dot(left, right, preferred_element_type=jnp.float32)


def dot_left(left, right):
    return lax.dot_general(
        left, right, (((0,), (0,)), ((), ())), preferred_element_type=jnp.float32
    )


def dot_right(left, right):
    return lax.dot_general(
        left, right, (((1,), (1,)), ((), ())), preferred_element_type=jnp.float32
    )


def transfer_cost(elements):
    return pl.CostEstimate(flops=0, bytes_accessed=140 * elements, transcendentals=0)


def greet_line(me, parts):
    barrier = pltpu.get_barrier_semaphore()

    @pl.when(me > 0)
    def _():
        pl.semaphore_signal(barrier, inc=1, device_id={"expert": me - 1}, device_id_type=MESH)

    @pl.when(me < parts - 1)
    def _():
        pl.semaphore_signal(barrier, inc=1, device_id={"expert": me + 1}, device_id_type=MESH)

    pl.semaphore_wait(barrier, jnp.where((me > 0) & (me < parts - 1), 2, 1))


def greet_all(me, parts):
    barrier = pltpu.get_barrier_semaphore()
    for k in range(1, parts):
        pl.semaphore_signal(
            barrier, inc=1, device_id={"expert": lax.rem(me + k, parts)}, device_id_type=MESH
        )
    pl.semaphore_wait(barrier, parts - 1)


def gather_kernel(parts, pieces, count, *refs):
    srcs, dsts = refs[:count], refs[count : 2 * count]
    own_sem, send_up, recv_up, send_down, recv_down = refs[2 * count :]
    me = lax.axis_index("expert")
    greet_line(me, parts)

    def block(i, origin, piece):
        rows = srcs[i].shape[0] // pieces
        at = origin * srcs[i].shape[0] + piece * rows
        return dsts[i].at[pl.ds(pl.multiple_of(at, rows), rows)]

    def hop(i, src, origin, piece, to, send, recv, step, got):
        n = i * pieces + piece
        return pltpu.make_async_remote_copy(
            src_ref=src,
            dst_ref=block(i, origin, piece),
            send_sem=send.at[n, step],
            recv_sem=recv.at[n, got],
            device_id={"expert": to},
            device_id_type=MESH,
        )

    streams = ((1, send_up, recv_up), (-1, send_down, recv_down))
    for step in range(parts - 1):
        for piece in range(pieces):
            for i in range(count):
                for way, send, recv in streams:
                    origin, to = me - way * step, me + way
                    has = (origin >= 0) & (origin < parts)
                    if step > 0:

                        @pl.when(has)
                        def _(i=i, origin=origin, piece=piece, send=send, recv=recv, step=step):
                            here = block(i, origin, piece)
                            hop(i, here, origin, piece, me, send, recv, step, step - 1).wait_recv()

                    @pl.when(has & (to >= 0) & (to < parts))
                    def _(i=i, origin=origin, piece=piece, to=to, send=send, recv=recv, step=step):
                        rows = srcs[i].shape[0] // pieces
                        src = srcs[i].at[piece * rows : (piece + 1) * rows] if step == 0 else block(i, origin, piece)
                        hop(i, src, origin, piece, to, send, recv, step, step).start()

        if step == 0:
            for i in range(count):
                rows = srcs[i].shape[0]
                there = dsts[i].at[pl.ds(pl.multiple_of(me * rows, rows), rows)]
                pltpu.make_async_copy(srcs[i], there, own_sem.at[i]).start()
    for i in range(count):
        rows = srcs[i].shape[0]
        there = dsts[i].at[pl.ds(pl.multiple_of(me * rows, rows), rows)]
        pltpu.make_async_copy(srcs[i], there, own_sem.at[i]).wait()
    for way, send, recv in streams:
        to, last = me + way, me - way * (parts - 1)
        for i in range(count):
            for piece in range(pieces):

                @pl.when((last >= 0) & (last < parts))
                def _(i=i, piece=piece, last=last, send=send, recv=recv):
                    here = block(i, last, piece)
                    hop(i, here, last, piece, me, send, recv, 0, parts - 2).wait_recv()

                for step in range(parts - 1):
                    origin = me - way * step

                    @pl.when((origin >= 0) & (origin < parts) & (to >= 0) & (to < parts))
                    def _(i=i, piece=piece, origin=origin, send=send, recv=recv, step=step):
                        here = block(i, origin, piece)
                        hop(i, here, origin, piece, me, send, recv, step, step).wait_send()


def line_gather(arrays, cid, pieces=1):
    parts = lax.axis_size("expert")
    n = len(arrays)
    sem = pltpu.SemaphoreType.DMA
    return pl.pallas_call(
        functools.partial(gather_kernel, parts, pieces, n),
        out_shape=[jax.ShapeDtypeStruct((parts * a.shape[0],) + a.shape[1:], a.dtype) for a in arrays],
        in_specs=[ANY] * n,
        out_specs=[ANY] * n,
        scratch_shapes=[sem((n,))] + [sem((n * pieces, parts - 1))] * 4,
        cost_estimate=transfer_cost(parts * sum(a.size for a in arrays)),
        compiler_params=pltpu.CompilerParams(collective_id=cid, has_side_effects=True),
        name="line_gather_%d" % cid,
    )(*arrays)


def exchange_kernel(parts, count, stack, *refs):
    srcs, dsts = refs[:count], refs[count : 2 * count]
    own_sem, send, recv = refs[2 * count :]
    me = lax.axis_index("expert")
    greet_all(me, parts)

    def piece(i, owner):
        rows = srcs[i].shape[0] // parts
        return srcs[i].at[pl.ds(pl.multiple_of(owner * rows, rows), rows)]

    def place(i, origin):
        rows, cols = srcs[i].shape[0] // parts, srcs[i].shape[1]
        if stack:
            return dsts[i].at[pl.ds(pl.multiple_of(origin * rows, rows), rows)]
        return dsts[i].at[:, pl.ds(pl.multiple_of(origin * cols, cols), cols)]

    copies = []
    for k in list(range(parts - 1, 0, -1)):
        to = lax.rem(me + k, parts)
        for i in range(count):
            copy = pltpu.make_async_remote_copy(
                src_ref=piece(i, to),
                dst_ref=place(i, me),
                send_sem=send.at[i, k - 1],
                recv_sem=recv.at[i, k - 1],
                device_id={"expert": to},
                device_id_type=MESH,
            )
            copy.start()
            copies.append(copy)
    for i in range(count):
        own = pltpu.make_async_copy(piece(i, me), place(i, me), own_sem.at[i])
        own.start()
        own.wait()
    for copy in copies:
        copy.wait_send()
    for k in list(range(parts - 1, 0, -1)):
        origin = lax.rem(me + parts - k, parts)
        for i in range(count):
            pltpu.make_async_remote_copy(
                src_ref=piece(i, me),
                dst_ref=place(i, origin),
                send_sem=send.at[i, k - 1],
                recv_sem=recv.at[i, k - 1],
                device_id={"expert": origin},
                device_id_type=MESH,
            ).wait_recv()


def exchange(arrays, cid, stack=False):
    parts = lax.axis_size("expert")
    n = len(arrays)
    sem = pltpu.SemaphoreType.DMA
    return pl.pallas_call(
        functools.partial(exchange_kernel, parts, n, stack),
        out_shape=[
            jax.ShapeDtypeStruct(
                a.shape if stack else (a.shape[0] // parts, a.shape[1] * parts), a.dtype
            )
            for a in arrays
        ],
        in_specs=[ANY] * n,
        out_specs=[ANY] * n,
        scratch_shapes=[sem((n,)), sem((n, parts - 1)), sem((n, parts - 1))],
        cost_estimate=transfer_cost(sum(a.size for a in arrays)),
        compiler_params=pltpu.CompilerParams(collective_id=cid, has_side_effects=True),
        name="exchange_%d" % cid,
    )(*arrays)


def reduce_kernel(parts, pieces, src, out, slot_up, slot_down, send_up, recv_up, send_down, recv_down):
    me = lax.axis_index("expert")
    greet_line(me, parts)
    rows = out.shape[0]
    part = rows // pieces
    step_rows = 16

    def hop(ref, slot, step, piece, to, send, recv):
        return pltpu.make_async_remote_copy(
            src_ref=ref,
            dst_ref=slot.at[step, piece * part : (piece + 1) * part],
            send_sem=send.at[step, piece],
            recv_sem=recv.at[step, piece],
            device_id={"expert": to},
            device_id_type=MESH,
        )

    def landed(slot, step, piece, send, recv):
        return hop(slot.at[step, piece * part : (piece + 1) * part], slot, step, piece, me, send, recv)

    streams = ((True, slot_up, send_up, recv_up), (False, slot_down, send_down, recv_down))
    for step in range(parts - 1):
        for piece in range(pieces):
            for up, slot, send, recv in streams:
                line = me if up else parts - 1 - me
                dest_line = parts - 1 - step + line
                dest = dest_line if up else parts - 1 - dest_line
                to = me + 1 if up else me - 1

                @pl.when(line == 0)
                def _(dest=dest, slot=slot, step=step, piece=piece, to=to, send=send, recv=recv):
                    there = pl.ds(pl.multiple_of(dest * rows + piece * part, part), part)
                    hop(src.at[there], slot, step, piece, to, send, recv).start()

                if step > 0:

                    @pl.when((line > 0) & (step >= line) & (line < parts - 1))
                    def _(dest=dest, slot=slot, step=step, piece=piece, to=to, send=send, recv=recv):
                        landed(slot, step - 1, piece, send, recv).wait_recv()

                        @pl.loop(0, part // step_rows)
                        def _(r):
                            at = piece * part + r * step_rows
                            here = pl.ds(pl.multiple_of(at, step_rows), step_rows)
                            there = pl.ds(pl.multiple_of(dest * rows + at, step_rows), step_rows)
                            both = slot[step - 1, here, :].astype(jnp.float32) + src[there, :].astype(jnp.float32)
                            slot[step - 1, here, :] = both.astype(jnp.bfloat16)

                        sent = slot.at[step - 1, piece * part : (piece + 1) * part]
                        hop(sent, slot, step, piece, to, send, recv).start()

    @pl.loop(0, rows // step_rows)
    def _(r):
        here = pl.ds(pl.multiple_of(r * step_rows, step_rows), step_rows)
        there = pl.ds(pl.multiple_of(me * rows + r * step_rows, step_rows), step_rows)
        out[here, :] = src[there, :].astype(jnp.float32)

    last = parts - 2
    for piece in range(pieces):
        for up, slot, send, recv in streams:
            line = me if up else parts - 1 - me

            @pl.when(line > 0)
            def _(slot=slot, piece=piece, send=send, recv=recv):
                landed(slot, last, piece, send, recv).wait_recv()

                @pl.loop(0, part // step_rows)
                def _(r):
                    here = pl.ds(pl.multiple_of(piece * part + r * step_rows, step_rows), step_rows)
                    out[here, :] = out[here, :] + slot[last, here, :].astype(jnp.float32)

    for up, slot, send, recv in streams:
        line = me if up else parts - 1 - me
        for step in range(parts - 1):
            for piece in range(pieces):

                @pl.when((step >= line) & (line < parts - 1))
                def _(slot=slot, step=step, piece=piece, send=send, recv=recv):
                    landed(slot, step, piece, send, recv).wait_send()


def line_reduce(terms, cid, pieces=1):
    parts = lax.axis_size("expert")
    rows, cols = terms.shape[0] // parts, terms.shape[1]
    sem = pltpu.SemaphoreType.DMA
    return pl.pallas_call(
        functools.partial(reduce_kernel, parts, pieces),
        out_shape=jax.ShapeDtypeStruct((rows, cols), jnp.float32),
        in_specs=[VMEM],
        out_specs=VMEM,
        scratch_shapes=[pltpu.VMEM((parts - 1, rows, cols), jnp.bfloat16)] * 2
        + [sem((parts - 1, pieces))] * 4,
        cost_estimate=transfer_cost(terms.size),
        compiler_params=pltpu.CompilerParams(
            collective_id=cid, has_side_effects=True, vmem_limit_bytes=48 * 1024 * 1024
        ),
        name="line_reduce_%d" % cid,
    )(terms)


def weights_kernel(parts, blocks, out, small, chosen, dst, dst_chosen, own_sem, send, recv, send_up, recv_up, send_down, recv_down):
    me = lax.axis_index("expert")
    share = out.shape[0]
    left, wide = out.shape[1], blocks.shape[1]
    greet_all(me, parts)

    def rows(origin):
        return pl.ds(pl.multiple_of(origin * share, share), share)

    def exchanged(k, to, origin):
        return pltpu.make_async_remote_copy(
            src_ref=blocks.at[rows(to)],
            dst_ref=dst.at[rows(origin), left : left + wide],
            send_sem=send.at[k - 1],
            recv_sem=recv.at[k - 1],
            device_id={"expert": to},
            device_id_type=MESH,
        )

    shared = ((out, dst, 0), (small, dst, left + wide), (chosen, dst_chosen, 0))

    def place(i, origin):
        src, into, at = shared[i]
        return into.at[rows(origin), at : at + src.shape[1]]

    def hop(i, src, origin, to, send_sem, recv_sem):
        return pltpu.make_async_remote_copy(
            src_ref=src,
            dst_ref=place(i, origin),
            send_sem=send_sem,
            recv_sem=recv_sem,
            device_id={"expert": to},
            device_id_type=MESH,
        )

    streams = ((1, send_up, recv_up), (-1, send_down, recv_down))
    for step in range(parts - 1):
        for way, sends, recvs in streams:
            origin, to = me - way * step, me + way
            has = (origin >= 0) & (origin < parts)
            for i in range(3):
                if step > 0:

                    @pl.when(has)
                    def _(i=i, origin=origin, sends=sends, recvs=recvs, step=step):
                        hop(i, place(i, origin), origin, me, sends.at[i, step], recvs.at[i, step - 1]).wait_recv()

                @pl.when(has & (to >= 0) & (to < parts))
                def _(i=i, origin=origin, to=to, sends=sends, recvs=recvs, step=step):
                    src = shared[i][0] if step == 0 else place(i, origin)
                    hop(i, src, origin, to, sends.at[i, step], recvs.at[i, step]).start()

        if step == 0:
            for k in range(parts - 1, 0, -1):
                to = lax.rem(me + k, parts)
                exchanged(k, to, me).start()
            owns = [
                pltpu.make_async_copy(src, target, own_sem.at[i])
                for i, (src, target) in enumerate(
                    (
                        (blocks.at[rows(me)], dst.at[rows(me), left : left + wide]),
                        (out, place(0, me)),
                        (small, place(1, me)),
                        (chosen, place(2, me)),
                    )
                )
            ]
            for copy in owns:
                copy.start()

    for copy in owns:
        copy.wait()
    for way, sends, recvs in streams:
        to, last = me + way, me - way * (parts - 1)
        for i in range(3):

            @pl.when((last >= 0) & (last < parts))
            def _(i=i, last=last, sends=sends, recvs=recvs):
                hop(i, place(i, last), last, me, sends.at[i, 0], recvs.at[i, parts - 2]).wait_recv()

            for step in range(parts - 1):
                origin = me - way * step

                @pl.when((origin >= 0) & (origin < parts) & (to >= 0) & (to < parts))
                def _(i=i, origin=origin, sends=sends, recvs=recvs, step=step):
                    hop(i, place(i, origin), origin, me, sends.at[i, step], recvs.at[i, step]).wait_send()

    for k in range(parts - 1, 0, -1):
        exchanged(k, lax.rem(me + k, parts), me).wait_send()
        exchanged(k, me, lax.rem(me + parts - k, parts)).wait_recv()


def gather_weights(blocks, out, small, chosen, cid):
    parts = lax.axis_size("expert")
    sem = pltpu.SemaphoreType.DMA
    rows, cols = blocks.shape[0], out.shape[1] + blocks.shape[1] + small.shape[1]
    return pl.pallas_call(
        functools.partial(weights_kernel, parts),
        out_shape=[
            jax.ShapeDtypeStruct((rows, cols), blocks.dtype),
            jax.ShapeDtypeStruct((rows, chosen.shape[1]), blocks.dtype),
        ],
        in_specs=[ANY] * 4,
        out_specs=[ANY] * 2,
        scratch_shapes=[sem((4,)), sem((parts - 1,)), sem((parts - 1,))] + [sem((3, parts - 1))] * 4,
        cost_estimate=transfer_cost(rows * (cols + chosen.shape[1])),
        compiler_params=pltpu.CompilerParams(collective_id=cid, has_side_effects=True),
        name="gather_weights",
    )(blocks, out, small, chosen)


def diagonal_mask(column_ref, row_ref, block):
    here = pl.ds(block * BLOCK, BLOCK)
    seg_query = column_ref[here, :]
    seg_key = row_ref[:, here]
    shape = (BLOCK, BLOCK)
    causal = lax.broadcasted_iota(jnp.int32, shape, 1) <= lax.broadcasted_iota(jnp.int32, shape, 0)
    same = (seg_query == seg_key) & causal
    return same | ((seg_key == 0) & (seg_query != 0))


def masked_scores(query, key_ref, column_ref, row_ref, block):
    scale = HEAD ** (-0.5)
    here = pl.ds(block * BLOCK, BLOCK)
    own = dot_right(query, key_ref[here, :]) * scale
    own = jnp.where(diagonal_mask(column_ref, row_ref, block), own, MASKED)
    if block == 0:
        return own
    ahead = dot_right(query, key_ref[: block * BLOCK, :]) * scale
    return jnp.concatenate([ahead, own], axis=1)


def row_block(owner, rows):
    return pl.ds(pl.multiple_of(owner * rows, rows), rows)


def attention_kernel(
    parts, column_ref, row_ref, query_ref, key_ref, value_ref, mixed_ref, lse_ref, heads_out, own_sem, send, recv
):
    head, heads = pl.program_id(0), pl.num_programs(0)
    me = lax.axis_index("expert")
    total = query_ref.shape[0]
    piece = total // parts

    @pl.when(head == 0)
    def _():
        greet_all(me, parts)

    def moved(h, k, origin, to):
        lanes = pl.ds(pl.multiple_of((origin * heads + h) * HEAD, HEAD), HEAD)
        return pltpu.make_async_remote_copy(
            src_ref=heads_out.at[h, row_block(to, piece)],
            dst_ref=mixed_ref.at[:, lanes],
            send_sem=send.at[h, k - 1],
            recv_sem=recv.at[h, k - 1],
            device_id={"expert": to},
            device_id_type=MESH,
        )

    def kept(h):
        lanes = pl.ds(pl.multiple_of((me * heads + h) * HEAD, HEAD), HEAD)
        return pltpu.make_async_copy(heads_out.at[h, row_block(me, piece)], mixed_ref.at[:, lanes], own_sem.at[h])

    for block in range(total // BLOCK):
        here = pl.ds(block * BLOCK, BLOCK)
        scores = masked_scores(query_ref[here, :], key_ref, column_ref, row_ref, block)
        top = jnp.max(scores, axis=1, keepdims=True)
        expd = jnp.exp(scores - top)
        mass = jnp.sum(expd, axis=1, keepdims=True)
        probs = (expd / mass).astype(jnp.bfloat16)
        mixed = dot_plain(probs, value_ref[: (block + 1) * BLOCK, :])
        heads_out[head, here, :] = mixed.astype(jnp.bfloat16)
        lse_ref[0, here, :] = top + jnp.log(mass)

    kept(head).start()
    for k in range(parts - 1, 0, -1):
        moved(head, k, me, lax.rem(me + k, parts)).start()

    @pl.when(head == heads - 1)
    def _():
        @pl.loop(0, heads)
        def _(h):
            kept(h).wait()
            for k in range(parts - 1, 0, -1):
                moved(h, k, me, lax.rem(me + k, parts)).wait_send()
                moved(h, k, lax.rem(me + parts - k, parts), me).wait_recv()


def head_specs(total, heads):
    return [
        pl.BlockSpec((total, HEAD), lambda h, part=part: (0, part * heads + h)) for part in range(3)
    ]


def run_attention(column, row, qkv, cid):
    total, heads = qkv.shape[0], qkv.shape[1] // (3 * HEAD)
    parts = lax.axis_size("expert")
    whole = pl.BlockSpec(memory_space=pltpu.VMEM)
    sem = pltpu.SemaphoreType.DMA
    return pl.pallas_call(
        functools.partial(attention_kernel, parts),
        grid=(heads,),
        in_specs=[whole, whole] + head_specs(total, heads),
        out_specs=[ANY, pl.BlockSpec((1, total, 1), lambda h: (h, 0, 0))],
        out_shape=[
            jax.ShapeDtypeStruct((total // parts, D), jnp.bfloat16),
            jax.ShapeDtypeStruct((heads, total, 1), jnp.float32),
        ],
        scratch_shapes=[
            pltpu.VMEM((heads, total, HEAD), jnp.bfloat16),
            sem((heads,)),
            sem((heads, parts - 1)),
            sem((heads, parts - 1)),
        ],
        compiler_params=pltpu.CompilerParams(
            dimension_semantics=("arbitrary",),
            vmem_limit_bytes=48 * 1024 * 1024,
            collective_id=cid,
            has_side_effects=True,
        ),
        cost_estimate=pl.CostEstimate(
            flops=0, bytes_accessed=200 * total * heads * HEAD, transcendentals=heads * total * total // 2
        ),
        name="attention",
    )(column, row, qkv, qkv, qkv)


def attention_back_kernel(
    parts,
    column_ref,
    row_ref,
    query_ref,
    key_ref,
    value_ref,
    lse_ref,
    sent_ref,
    back_query_ref,
    back_key_ref,
    back_value_ref,
    key_acc,
    value_acc,
    grads,
    own_sem,
    send,
    recv,
):
    head, heads = pl.program_id(0), pl.num_programs(0)
    me = lax.axis_index("expert")
    scale = HEAD ** (-0.5)
    total = query_ref.shape[0]
    piece = total // parts

    def moved(h, k, origin, to):
        lanes = pl.ds(pl.multiple_of(h * HEAD, HEAD), HEAD)
        return pltpu.make_async_remote_copy(
            src_ref=sent_ref.at[row_block(to, piece), lanes],
            dst_ref=grads.at[h, row_block(origin, piece)],
            send_sem=send.at[h, k - 1],
            recv_sem=recv.at[h, k - 1],
            device_id={"expert": to},
            device_id_type=MESH,
        )

    def kept(h):
        lanes = pl.ds(pl.multiple_of(h * HEAD, HEAD), HEAD)
        return pltpu.make_async_copy(
            sent_ref.at[row_block(me, piece), lanes], grads.at[h, row_block(me, piece)], own_sem.at[h]
        )

    @pl.when(head == 0)
    def _():
        greet_all(me, parts)

        @pl.loop(0, heads)
        def _(h):
            for k in range(parts - 1, 0, -1):
                moved(h, k, me, lax.rem(me + k, parts)).start()
            kept(h).start()

    kept(head).wait()
    for k in range(parts - 1, 0, -1):
        moved(head, k, lax.rem(me + parts - k, parts), me).wait_recv()
    key_acc[...] = jnp.zeros_like(key_acc)
    value_acc[...] = jnp.zeros_like(value_acc)
    for block in range(total // BLOCK):
        here = pl.ds(block * BLOCK, BLOCK)
        upto = pl.ds(0, (block + 1) * BLOCK)
        query, grad = query_ref[here, :], grads[head, here, :]
        scores = masked_scores(query, key_ref, column_ref, row_ref, block)
        probs = jnp.exp(scores - lse_ref[0, here, :])
        prob_back = dot_right(grad, value_ref[upto, :])
        delta = jnp.sum(probs * prob_back, axis=1, keepdims=True)
        score_grad = (probs * (prob_back - delta)).astype(jnp.bfloat16)
        back_query_ref[here, :] = (dot_plain(score_grad, key_ref[upto, :]) * scale).astype(jnp.bfloat16)
        key_acc[upto, :] += dot_left(score_grad, query)
        value_acc[upto, :] += dot_left(probs.astype(jnp.bfloat16), grad)
    back_key_ref[...] = (key_acc[...] * scale).astype(jnp.bfloat16)
    back_value_ref[...] = value_acc[...].astype(jnp.bfloat16)

    @pl.when(head == heads - 1)
    def _():
        @pl.loop(0, heads)
        def _(h):
            for k in range(parts - 1, 0, -1):
                moved(h, k, me, lax.rem(me + k, parts)).wait_send()


def run_attention_back(column, row, qkv, sent, lse, cid):
    total, heads = qkv.shape[0], qkv.shape[1] // (3 * HEAD)
    parts = lax.axis_size("expert")
    whole = pl.BlockSpec(memory_space=pltpu.VMEM)
    head = pl.BlockSpec((total, HEAD), lambda h: (0, h))
    sem = pltpu.SemaphoreType.DMA
    return pl.pallas_call(
        functools.partial(attention_back_kernel, parts),
        grid=(heads,),
        in_specs=[whole, whole]
        + head_specs(total, heads)
        + [pl.BlockSpec((1, total, 1), lambda h: (h, 0, 0)), ANY],
        out_specs=[head] * 3,
        out_shape=[jax.ShapeDtypeStruct((total, heads * HEAD), jnp.bfloat16)] * 3,
        scratch_shapes=[pltpu.VMEM((total, HEAD), jnp.float32)] * 2
        + [
            pltpu.VMEM((heads, total, HEAD), jnp.bfloat16),
            sem((heads,)),
            sem((heads, parts - 1)),
            sem((heads, parts - 1)),
        ],
        compiler_params=pltpu.CompilerParams(
            dimension_semantics=("arbitrary",),
            vmem_limit_bytes=48 * 1024 * 1024,
            collective_id=cid,
            has_side_effects=True,
        ),
        cost_estimate=pl.CostEstimate(
            flops=0, bytes_accessed=200 * total * heads * HEAD, transcendentals=heads * total * total // 2
        ),
        name="attention_back",
    )(column, row, qkv, qkv, qkv, lse, sent)


def own_lift(lift_ref, j):
    row = lax.broadcasted_iota(jnp.int32, (LANES, TILE), 0)
    own = (row >= j * RANK) & (row < (j + 1) * RANK)
    return jnp.where(own, lift_ref[...].astype(jnp.float32), 0.0).astype(jnp.bfloat16)


def gate_column(gates_ref, here, j):
    shape = (ROWS, LANES)
    mine = lax.broadcasted_iota(jnp.int32, shape, 1) == lax.axis_index("expert") * EXP_DEV + j
    return mine, jnp.sum(
        jnp.where(mine, gates_ref[here, :].astype(jnp.float32), 0.0), axis=1, keepdims=True
    )


def row_chunk(b, rows=None):
    rows = rows or ROWS
    return pl.ds(pl.multiple_of(b * rows, rows), rows)


def forward_kernel(
    rows_ref,
    gates_ref,
    down_ref,
    lift_gate_ref,
    lift_up_ref,
    in_gate_ref,
    in_up_ref,
    out_ref,
    *refs,
):
    output_ref, output_rest_ref, ranks_ref, gate_ref, up_ref, output_acc, stage, sems = refs
    j, f = pl.program_id(0), pl.program_id(1)
    total = rows_ref.shape[0]

    @pl.when((j == 0) & (f == 0))
    def _():
        @pl.loop(0, total // ROWS)
        def _(b):
            here = row_chunk(b)
            ranks_ref[here, :] = dot_right(rows_ref[here, :], down_ref[...]).astype(jnp.bfloat16)
            output_acc[here, :] = jnp.zeros((ROWS, D), jnp.float32)

    lift_gate, lift_up = own_lift(lift_gate_ref, j), own_lift(lift_up_ref, j)

    @pl.loop(0, total // ROWS)
    def _(b):
        here = row_chunk(b)
        rows = rows_ref[here, :]
        _, column = gate_column(gates_ref, here, j)
        gate = dot_plain(rows, in_gate_ref[0]) + dot_plain(ranks_ref[here, :], lift_gate)
        up = dot_plain(rows, in_up_ref[0]) + dot_plain(ranks_ref[here, :], lift_up)
        gate_ref[0, here, :] = gate.astype(jnp.bfloat16)
        up_ref[0, here, :] = up.astype(jnp.bfloat16)
        hidden = (column * (gate * jax.nn.sigmoid(gate) * up)).astype(jnp.bfloat16)
        output_acc[here, :] += dot_plain(hidden, out_ref[0])

    @pl.when((j == EXP_DEV - 1) & (f == FF // TILE - 1))
    def _():
        def copies(b):
            slot = lax.rem(b, 2)
            here = row_chunk(b, stage.shape[1])
            half = D // 2
            return [
                pltpu.make_async_copy(
                    stage.at[slot, :, h * half : (h + 1) * half], refs_out[h].at[here], sems.at[slot, h]
                )
                for h in range(2)
            ]

        refs_out = (output_ref, output_rest_ref)
        steps = total // stage.shape[1]

        @pl.loop(0, steps)
        def _(b):
            @pl.when(b >= 2)
            def _():
                for copy in copies(b - 2):
                    copy.wait()

            here = row_chunk(b, stage.shape[1])
            stage[lax.rem(b, 2)] = output_acc[here, :].astype(jnp.bfloat16)
            for copy in copies(b):
                copy.start()

        for b in range(steps - 2, steps):
            for copy in copies(b):
                copy.wait()


def weight_specs():
    tiles = FF // TILE
    return [
        pl.BlockSpec((LANES, TILE), lambda j, f: (0, f)),
        pl.BlockSpec((LANES, TILE), lambda j, f: (0, f + tiles)),
        pl.BlockSpec((1, D, TILE), lambda j, f: (j, 0, f)),
        pl.BlockSpec((1, D, TILE), lambda j, f: (j, 0, f + tiles)),
        pl.BlockSpec((1, TILE, D), lambda j, f: (j, f, 0)),
    ]


EXPERT_PARAMS = pltpu.CompilerParams(
    dimension_semantics=("arbitrary", "arbitrary"), vmem_limit_bytes=60 * 1024 * 1024
)


def experts_forward(rows, gates, down, lift, matrix_in, matrix_out):
    total = rows.shape[0]
    kept = pl.BlockSpec((1, total, TILE), lambda j, f: (j, 0, f))
    return pl.pallas_call(
        forward_kernel,
        grid=(EXP_DEV, FF // TILE),
        in_specs=[VMEM] * 3 + weight_specs(),
        out_specs=[
            ANY,
            ANY,
            pl.BlockSpec((total, LANES), lambda j, f: (0, 0), pipeline_mode=pl.Buffered(1)),
            kept,
            kept,
        ],
        out_shape=[
            jax.ShapeDtypeStruct((total, D // 2), jnp.bfloat16),
            jax.ShapeDtypeStruct((total, D // 2), jnp.bfloat16),
            jax.ShapeDtypeStruct((total, LANES), jnp.bfloat16),
            jax.ShapeDtypeStruct((EXP_DEV, total, FF), jnp.bfloat16),
            jax.ShapeDtypeStruct((EXP_DEV, total, FF), jnp.bfloat16),
        ],
        scratch_shapes=[
            pltpu.VMEM((total, D), jnp.float32),
            pltpu.VMEM((2, 160, D), jnp.bfloat16),
            pltpu.SemaphoreType.DMA((2, 2)),
        ],
        compiler_params=EXPERT_PARAMS,
        cost_estimate=pl.CostEstimate(
            flops=10 * EXP_DEV * total * D * FF,
            bytes_accessed=EXP_DEV * 6 * D * FF + 8 * total * D,
            transcendentals=EXP_DEV * total * FF,
        ),
        name="experts_forward",
    )(rows, gates, down, lift, lift, matrix_in, matrix_in, matrix_out)


def backward_kernel(
    parts,
    gates_ref,
    ranks_ref,
    down_ref,
    lift_gate_ref,
    lift_up_ref,
    in_gate_ref,
    in_up_ref,
    out_ref,
    gate_hbm,
    up_hbm,
    *refs,
):
    blocks, refs = refs[:parts], refs[parts:]
    sum_ref, rank_ref, lift_grad_ref, upstream, slot_acc, rank_acc, gate_acc, terms, gates, ups, load_sems, kept_sems = refs[:12]
    slot_up, slot_down, send_up, recv_up, send_down, recv_down = refs[12:]
    q, j, f = pl.program_id(0), pl.program_id(1), pl.program_id(2)
    tiles = FF // TILE
    me = lax.axis_index("expert")
    total = upstream.shape[0]
    piece, rows = total // parts, total // 2
    part = piece // 2
    own_half = jnp.where(me < parts // 2, 1 - q, q)
    begin = pl.multiple_of(own_half * rows, rows)
    here = pl.ds(begin, rows)
    inner = j * tiles + f
    step = q * EXP_DEV * tiles + inner
    slot_now = lax.rem(step, 2)

    def fetches(at):
        half = at // (EXP_DEV * tiles)
        first = pl.multiple_of(jnp.where(me < parts // 2, 1 - half, half) * rows, rows)
        source = (
            lax.rem(at // tiles, EXP_DEV),
            pl.ds(first, rows),
            pl.ds(pl.multiple_of(lax.rem(at, tiles) * TILE, TILE), TILE),
        )
        slot = lax.rem(at, 2)
        return (
            pltpu.make_async_copy(gate_hbm.at[source], gates.at[slot], kept_sems.at[slot, 0]),
            pltpu.make_async_copy(up_hbm.at[source], ups.at[slot], kept_sems.at[slot, 1]),
        )

    def hop(ref, slot, at, n, to, send, recv):
        return pltpu.make_async_remote_copy(
            src_ref=ref,
            dst_ref=slot.at[at, n * part : (n + 1) * part],
            send_sem=send.at[at, n],
            recv_sem=recv.at[at, n],
            device_id={"expert": to},
            device_id_type=MESH,
        )

    def landed(slot, at, n, send, recv):
        return hop(slot.at[at, n * part : (n + 1) * part], slot, at, n, me, send, recv)

    streams = ((True, slot_up, send_up, recv_up), (False, slot_down, send_down, recv_down))

    def where_to(up, at):
        line = me if up else parts - 1 - me
        dest_line = parts - 1 - at + line
        return line, (me + 1 if up else me - 1), (dest_line if up else parts - 1 - dest_line)

    def send_first(up, slot, send, recv, at):
        line, to, dest = where_to(up, at)

        @pl.when(line == 0)
        def _():
            for n in range(2):
                there = pl.ds(pl.multiple_of(dest * piece + n * part, part), part)
                hop(terms.at[there], slot, at, n, to, send, recv).start()

    def pass_on(up, slot, send, recv, at, n):
        _, to, dest = where_to(up, at)
        landed(slot, at - 1, n, send, recv).wait_recv()
        chunk = 16

        @pl.loop(0, part // chunk)
        def _(r):
            local = pl.ds(pl.multiple_of(n * part + r * chunk, chunk), chunk)
            there = pl.ds(pl.multiple_of(dest * piece + n * part + r * chunk, chunk), chunk)
            both = slot[at - 1, local, :].astype(jnp.float32) + terms[there, :].astype(jnp.float32)
            slot[at - 1, local, :] = both.astype(jnp.bfloat16)

        hop(slot.at[at - 1, n * part : (n + 1) * part], slot, at, n, to, send, recv).start()

    @pl.when(step == 0)
    def _():
        greet_line(me, parts)
        copies = []
        for shift in range(parts):
            there = row_chunk(lax.rem(me + parts - shift, parts), piece)
            copies.append(pltpu.make_async_copy(blocks[shift], upstream.at[there], load_sems.at[shift]))
        for copy in copies:
            copy.start()
        for copy in fetches(step):
            copy.start()
        lift_grad_ref[...] = jnp.zeros_like(lift_grad_ref)
        for copy in copies:
            copy.wait()

    @pl.when(step + 1 < 2 * EXP_DEV * tiles)
    def _():
        for copy in fetches(step + 1):
            copy.start()

    @pl.when(inner == 0)
    def _():
        slot_acc[...] = jnp.zeros_like(slot_acc)
        rank_acc[...] = jnp.zeros_like(rank_acc)
        gate_acc[...] = jnp.zeros_like(gate_acc)

    lift_gate, lift_up = own_lift(lift_gate_ref, j), own_lift(lift_up_ref, j)
    for copy in fetches(step):
        copy.wait()
    mine = lax.broadcasted_iota(jnp.int32, (rows, LANES), 1) == me * EXP_DEV + j
    column = jnp.sum(jnp.where(mine, gates_ref[here, :].astype(jnp.float32), 0.0), axis=1, keepdims=True)
    raw = dot_right(upstream[here, :], out_ref[0])
    gate = gates[slot_now].astype(jnp.float32)
    up_part = ups[slot_now].astype(jnp.float32)
    sigma = jax.nn.sigmoid(gate)
    silu = gate * sigma
    gate_grad = jnp.sum(raw * (silu * up_part), axis=1, keepdims=True)
    back = raw * column
    to_gate = (back * up_part * (sigma + silu * (1.0 - sigma))).astype(jnp.bfloat16)
    to_up = (back * silu).astype(jnp.bfloat16)
    slot_acc[...] += dot_right(to_gate, in_gate_ref[0]) + dot_right(to_up, in_up_ref[0])
    rank_acc[...] += dot_right(to_gate, lift_gate) + dot_right(to_up, lift_up)
    gate_acc[...] += jnp.where(mine, gate_grad, 0.0)
    ranks = ranks_ref[here, :]
    for side, grad in enumerate((to_gate, to_up)):
        lanes = pl.ds(pl.multiple_of(side * FF + f * TILE, TILE), TILE)
        lift_grad_ref[:, lanes] += jnp.where(
            lax.broadcasted_iota(jnp.int32, (LANES, TILE), 0) // RANK == j, dot_left(ranks, grad), 0.0
        )

    @pl.when(inner == EXP_DEV * tiles - 1)
    def _():
        size = rows // 4

        @pl.loop(0, 4)
        def _(b):
            local = row_chunk(b, size)
            there = pl.ds(pl.multiple_of(begin + b * size, size), size)
            rank_low = rank_acc[local, :].astype(jnp.bfloat16)
            rank_ref[there, :] = rank_low
            slot = slot_acc[local, :] + dot_plain(rank_low, down_ref[...])
            terms[there, :D] = slot.astype(jnp.bfloat16)
            wide = gate_acc[local, :]
            high = wide.astype(jnp.bfloat16).astype(jnp.float32)
            both = high + pltpu.roll(wide - high, LANES // 2, 1)
            terms[there, D:] = both.astype(jnp.bfloat16)

    @pl.when((q == 0) & (inner == EXP_DEV * tiles - 1))
    def _():
        for at in range(parts // 2):
            for stream in streams:
                send_first(*stream, at)

    @pl.when((q == 1) & (inner == EXP_DEV * tiles - 3))
    def _():
        for stream in streams:
            line, _, _ = where_to(stream[0], 1)

            @pl.when(line == 1)
            def _(stream=stream):
                for n in range(2):
                    pass_on(*stream, 1, n)

    @pl.when((q == 1) & (inner == EXP_DEV * tiles - 1))
    def _():
        for at in range(1, parts - 1):
            if at >= parts // 2:
                for stream in streams:
                    send_first(*stream, at)
            for n in range(2):
                for stream in streams:
                    line, _, _ = where_to(stream[0], at)
                    early = (line == 1) & (at == 1)

                    @pl.when((line > 0) & (at >= line) & (line < parts - 1) & jnp.logical_not(early))
                    def _(stream=stream, at=at, n=n):
                        pass_on(*stream, at, n)

        chunk = 16
        last = parts - 2

        @pl.loop(0, piece // chunk)
        def _(r):
            local = row_chunk(r, chunk)
            there = pl.ds(pl.multiple_of(me * piece + r * chunk, chunk), chunk)
            sum_ref[local, :] = terms[there, :].astype(jnp.float32)

        for n in range(2):
            for up, slot, send, recv in streams:
                line, _, _ = where_to(up, 0)

                @pl.when(line > 0)
                def _(slot=slot, n=n, send=send, recv=recv):
                    landed(slot, last, n, send, recv).wait_recv()

                    @pl.loop(0, part // chunk)
                    def _(r):
                        local = pl.ds(pl.multiple_of(n * part + r * chunk, chunk), chunk)
                        sum_ref[local, :] = sum_ref[local, :] + slot[last, local, :].astype(jnp.float32)

        for up, slot, send, recv in streams:
            line, _, _ = where_to(up, 0)
            for at in range(parts - 1):
                for n in range(2):

                    @pl.when((at >= line) & (line < parts - 1))
                    def _(slot=slot, at=at, n=n, send=send, recv=recv):
                        landed(slot, at, n, send, recv).wait_send()


def experts_backward(blocks, gates, ranks, down, lift, matrix_in, matrix_out, gate, up, cid):
    total, parts = gates.shape[0], len(blocks)
    rows, piece, tiles = total // 2, total // parts, FF // TILE
    once = dict(pipeline_mode=pl.Buffered(1))
    sem = pltpu.SemaphoreType.DMA
    weights = [
        pl.BlockSpec((LANES, TILE), lambda q, j, f: (0, f)),
        pl.BlockSpec((LANES, TILE), lambda q, j, f: (0, f + tiles)),
        pl.BlockSpec((1, D, TILE), lambda q, j, f: (j, 0, f)),
        pl.BlockSpec((1, D, TILE), lambda q, j, f: (j, 0, f + tiles)),
        pl.BlockSpec((1, TILE, D), lambda q, j, f: (j, f, 0)),
    ]
    whole = lambda q, j, f: (0, 0)
    return pl.pallas_call(
        functools.partial(backward_kernel, parts),
        grid=(2, EXP_DEV, tiles),
        in_specs=[VMEM] * 3 + weights + [ANY] * (2 + parts),
        out_specs=[
            pl.BlockSpec((piece, D + LANES), whole, **once),
            pl.BlockSpec((total, LANES), whole, **once),
            pl.BlockSpec((LANES, 2 * FF), whole, **once),
        ],
        out_shape=[
            jax.ShapeDtypeStruct((piece, D + LANES), jnp.float32),
            jax.ShapeDtypeStruct((total, LANES), jnp.bfloat16),
            jax.ShapeDtypeStruct((LANES, 2 * FF), jnp.float32),
        ],
        scratch_shapes=[
            pltpu.VMEM((total, D), jnp.bfloat16),
            pltpu.VMEM((rows, D), jnp.float32),
            pltpu.VMEM((rows, LANES), jnp.float32),
            pltpu.VMEM((rows, LANES), jnp.float32),
            pltpu.VMEM((total, D + LANES), jnp.bfloat16),
            pltpu.VMEM((2, rows, TILE), jnp.bfloat16),
            pltpu.VMEM((2, rows, TILE), jnp.bfloat16),
            sem((parts,)),
            sem((2, 2)),
            pltpu.VMEM((parts - 1, piece, D + LANES), jnp.bfloat16),
            pltpu.VMEM((parts - 1, piece, D + LANES), jnp.bfloat16),
        ]
        + [sem((parts - 1, 2))] * 4,
        compiler_params=pltpu.CompilerParams(
            dimension_semantics=("arbitrary",) * 3,
            vmem_limit_bytes=60 * 1024 * 1024,
            collective_id=cid,
            has_side_effects=True,
        ),
        cost_estimate=pl.CostEstimate(
            flops=32 * EXP_DEV * total * D * FF,
            bytes_accessed=EXP_DEV * 6 * D * FF + 8 * total * D,
            transcendentals=EXP_DEV * total * FF,
        ),
        name="experts_backward",
    )(gates, ranks, down, lift, lift, matrix_in, matrix_in, matrix_out, gate, up, *blocks)


def pick_kernel(experts, chosen_ref, small_ref, picked_ref, router_ref, gain_ref):
    row = lax.broadcasted_iota(jnp.int32, (LANES, LANES), 0)
    same = row == lax.broadcasted_iota(jnp.int32, (LANES, LANES), 1)
    every = same.astype(jnp.float32).astype(jnp.bfloat16)
    router = (same & (row < experts)).astype(jnp.float32).astype(jnp.bfloat16)
    gain_row = lax.broadcasted_iota(jnp.int32, (8, LANES), 0) + 64
    gain = gain_row == lax.broadcasted_iota(jnp.int32, (8, LANES), 1)
    picked_ref[...] = dot_right(every, chosen_ref[...]).astype(jnp.bfloat16)
    router_ref[...] = dot_right(router, small_ref[...]).astype(jnp.bfloat16)
    gain_ref[...] = dot_right(gain.astype(jnp.float32).astype(jnp.bfloat16), small_ref[...])


def pick_rows(chosen, dense, at, experts):
    return pl.pallas_call(
        functools.partial(pick_kernel, experts),
        grid=(1,),
        in_specs=[VMEM, pl.BlockSpec((D, LANES), lambda i: (0, at // LANES))],
        out_specs=[all_of(LANES, D), all_of(LANES, D), all_of(8, D)],
        out_shape=[
            jax.ShapeDtypeStruct((LANES, D), jnp.bfloat16),
            jax.ShapeDtypeStruct((LANES, D), jnp.bfloat16),
            jax.ShapeDtypeStruct((8, D), jnp.float32),
        ],
        name="pick_rows",
    )(chosen, dense)


def first_kernel(query_ref, key_ref, value_ref, rank_ref, down_ref, *refs):
    weights, out_ref = refs[:3], refs[3]
    total = dot_right(query_ref[...], weights[0][...]) + dot_right(key_ref[...], weights[1][...])
    total = total + dot_right(value_ref[...], weights[2][...]) + dot_plain(rank_ref[...], down_ref[...])
    out_ref[...] = total.astype(jnp.bfloat16)


def first_products(backs, ranks, down, dense):
    total, width = backs[0].shape
    tile = 512
    weights = [
        pl.BlockSpec((tile, width), lambda i, part=part: (i, D // width + part)) for part in range(3)
    ]
    return pl.pallas_call(
        first_kernel,
        grid=(D // tile,),
        in_specs=[VMEM] * 4 + [pl.BlockSpec((RANK, tile), lambda i: (0, i))] + weights,
        out_specs=pl.BlockSpec((total, tile), lambda i: (0, i)),
        out_shape=jax.ShapeDtypeStruct((total, D), jnp.bfloat16),
        compiler_params=pltpu.CompilerParams(vmem_limit_bytes=48 * 1024 * 1024),
        cost_estimate=pl.CostEstimate(
            flops=6 * total * width * D, bytes_accessed=6 * width * D + 2 * total * D, transcendentals=0
        ),
        name="first_products",
    )(*backs, ranks, down, dense, dense, dense)


def sublayer_params():
    return pltpu.CompilerParams(
        dimension_semantics=("arbitrary",), vmem_limit_bytes=56 * 1024 * 1024
    )


def all_of(*shape):
    return pl.BlockSpec(shape, lambda i: (0,) * len(shape))


def qkv_kernel(tokens_ref, gain_ref, down_ref, lift_ref, weight_ref, normed_ref, rank_ref, qkv_ref):
    @pl.when(pl.program_id(0) == 0)
    def _():
        rows = tokens_ref.shape[0] // 4

        @pl.loop(0, 4)
        def _(b):
            here = row_chunk(b, rows)
            values = tokens_ref[here, :].astype(jnp.float32)
            normed = (values * norm_inverse(values) * gain_ref[...]).astype(jnp.bfloat16)
            normed_ref[here, :] = normed
            rank_ref[here, :] = dot_right(normed, down_ref[...]).astype(jnp.bfloat16)

    total = dot_plain(normed_ref[...], weight_ref[...]) + dot_plain(rank_ref[...], lift_ref[...])
    qkv_ref[...] = total.astype(jnp.bfloat16)


def project_qkv(tokens, gain, down, lift, dense):
    total, width = tokens.shape[0], lift.shape[1] // 3
    return pl.pallas_call(
        qkv_kernel,
        grid=(3,),
        in_specs=[
            VMEM,
            VMEM,
            VMEM,
            pl.BlockSpec((RANK, width), lambda i: (0, i)),
            pl.BlockSpec((D, width), lambda i: (0, D // width + i)),
        ],
        out_specs=[
            all_of(total, D),
            all_of(total, RANK),
            pl.BlockSpec((total, width), lambda i: (0, i)),
        ],
        out_shape=[
            jax.ShapeDtypeStruct((total, D), jnp.bfloat16),
            jax.ShapeDtypeStruct((total, RANK), jnp.bfloat16),
            jax.ShapeDtypeStruct((total, 3 * width), jnp.bfloat16),
        ],
        compiler_params=sublayer_params(),
        cost_estimate=pl.CostEstimate(
            flops=6 * total * D * width, bytes_accessed=6 * D * width + 8 * total * D, transcendentals=0
        ),
        name="project_qkv",
    )(tokens, gain, down, lift, dense)


def middle_kernel(
    experts,
    mixed_ref,
    tokens_ref,
    down_mix_ref,
    lift_mix_ref,
    gain_ref,
    down_route_ref,
    router_ref,
    lift_route_ref,
    routed_ref,
    out_ref,
    middle_ref,
    rank_mix_ref,
    inverse_ref,
    second_ref,
    rank_route_ref,
    probs_ref,
    gates_ref,
):
    i = pl.program_id(0)
    tile = out_ref.shape[1]

    @pl.when(i == 0)
    def _():
        rank_mix_ref[...] = dot_right(mixed_ref[...], down_mix_ref[...]).astype(jnp.bfloat16)

    here = pl.ds(pl.multiple_of(i * tile, tile), tile)
    branch = dot_plain(mixed_ref[...], out_ref[...]) + dot_plain(rank_mix_ref[...], lift_mix_ref[...])
    middle_ref[:, here] = tokens_ref[...].astype(jnp.float32) + branch

    @pl.when(i == D // tile - 1)
    def _():
        middle = middle_ref[...]
        inverse = norm_inverse(middle)
        inverse_ref[...] = inverse
        second = (middle * inverse * gain_ref[...]).astype(jnp.bfloat16)
        second_ref[...] = second
        rank_route = dot_right(second, down_route_ref[...]).astype(jnp.bfloat16)
        rank_route_ref[...] = rank_route
        logits = dot_right(second, router_ref[...]) + dot_plain(rank_route, lift_route_ref[...])
        lane = lax.broadcasted_iota(jnp.int32, logits.shape, 1)
        logits = jnp.where(lane < experts, logits, MASKED)
        exped = jnp.exp(logits - jnp.max(logits, axis=1, keepdims=True))
        probs = exped / jnp.sum(exped, axis=1, keepdims=True)
        probs_ref[...] = probs
        gates_ref[...] = (probs * routed_ref[...]).astype(jnp.bfloat16)


def finish_attention(experts, mixed, tokens, down_mix, lift_mix, gain, down_route, router, lift_route, routed, out_matrix):
    piece, tile = tokens.shape[0], 512
    column = lambda i: (0, i)
    return pl.pallas_call(
        functools.partial(middle_kernel, experts),
        grid=(D // tile,),
        in_specs=[
            VMEM,
            pl.BlockSpec((piece, tile), column),
            VMEM,
            pl.BlockSpec((RANK, tile), column),
            VMEM,
            VMEM,
            VMEM,
            VMEM,
            VMEM,
            pl.BlockSpec((D, tile), column),
        ],
        out_specs=[
            all_of(piece, D),
            all_of(piece, RANK),
            all_of(piece, 1),
            all_of(piece, D),
            all_of(piece, RANK),
            all_of(piece, LANES),
            all_of(piece, LANES),
        ],
        out_shape=[
            jax.ShapeDtypeStruct((piece, D), jnp.float32),
            jax.ShapeDtypeStruct((piece, RANK), jnp.bfloat16),
            jax.ShapeDtypeStruct((piece, 1), jnp.float32),
            jax.ShapeDtypeStruct((piece, D), jnp.bfloat16),
            jax.ShapeDtypeStruct((piece, RANK), jnp.bfloat16),
            jax.ShapeDtypeStruct((piece, LANES), jnp.float32),
            jax.ShapeDtypeStruct((piece, LANES), jnp.bfloat16),
        ],
        compiler_params=sublayer_params(),
        cost_estimate=pl.CostEstimate(
            flops=2 * piece * D * D, bytes_accessed=2 * D * D + 12 * piece * D, transcendentals=piece * LANES
        ),
        name="finish_attention",
    )(mixed, tokens, down_mix, lift_mix, gain, down_route, router, lift_route, routed, out_matrix)


def middle_back_kernel(
    slot_ref,
    probs_ref,
    routed_ref,
    middle_ref,
    inverse_ref,
    cotangent_ref,
    gain_ref,
    router_ref,
    lift_route_ref,
    down_route_ref,
    lift_mix_ref,
    down_mix_ref,
    out_ref,
    mixed_ref,
    grad_ref,
    branch_ref,
    logit_ref,
    rank_route_ref,
    rank_mix_ref,
):
    @pl.when(pl.program_id(0) == 0)
    def _():
        parts = slot_ref[:, D:]
        prob_grad = (parts + pltpu.roll(parts, LANES // 2, 1)) * routed_ref[...]
        probs = probs_ref[...]
        logit_grad = probs * (prob_grad - jnp.sum(probs * prob_grad, axis=1, keepdims=True))
        logit_grad = logit_grad.astype(jnp.bfloat16)
        logit_ref[...] = logit_grad
        rank_route_grad = dot_right(logit_grad, lift_route_ref[...]).astype(jnp.bfloat16)
        rank_route_ref[...] = rank_route_grad
        upstream = slot_ref[:, :D] + dot_plain(logit_grad, router_ref[...])
        upstream = upstream + dot_plain(rank_route_grad, down_route_ref[...])
        middle_grad = cotangent_ref[...].astype(jnp.float32) + norm_backward(
            middle_ref[...], inverse_ref[...], gain_ref[...], upstream
        )
        grad_ref[...] = middle_grad
        branch_ref[...] = middle_grad.astype(jnp.bfloat16)
        rank_mix_ref[...] = dot_right(branch_ref[...], lift_mix_ref[...]).astype(jnp.bfloat16)

    mixed = dot_right(branch_ref[...], out_ref[...]) + dot_plain(rank_mix_ref[...], down_mix_ref[...])
    mixed_ref[...] = mixed.astype(jnp.bfloat16)


def middle_backward(
    width, slot, probs, routed, middle, inverse, cotangent, gain, router, lift_route, down_route, lift_mix, down_mix, out_matrix
):
    piece = middle.shape[0]
    return pl.pallas_call(
        middle_back_kernel,
        grid=(D // width,),
        in_specs=[VMEM] * 11
        + [
            pl.BlockSpec((RANK, width), lambda i: (0, i)),
            pl.BlockSpec((width, D), lambda i: (i, 0)),
        ],
        out_specs=[
            pl.BlockSpec((piece, width), lambda i: (i, 0)),
            all_of(piece, D),
            all_of(piece, D),
            all_of(piece, LANES),
            all_of(piece, RANK),
            all_of(piece, RANK),
        ],
        out_shape=[
            jax.ShapeDtypeStruct((piece * D // width, width), jnp.bfloat16),
            jax.ShapeDtypeStruct((piece, D), jnp.float32),
            jax.ShapeDtypeStruct((piece, D), jnp.bfloat16),
            jax.ShapeDtypeStruct((piece, LANES), jnp.bfloat16),
            jax.ShapeDtypeStruct((piece, RANK), jnp.bfloat16),
            jax.ShapeDtypeStruct((piece, RANK), jnp.bfloat16),
        ],
        compiler_params=sublayer_params(),
        cost_estimate=pl.CostEstimate(
            flops=2 * piece * D * D, bytes_accessed=2 * D * D + 24 * piece * D, transcendentals=0
        ),
        name="middle_backward",
    )(slot, probs, routed, middle, inverse, cotangent, gain, router, lift_route, down_route, lift_mix, down_mix, out_matrix)


def norm_inverse(values):
    return lax.rsqrt(jnp.mean(values * values, axis=-1, keepdims=True) + EPSILON)


def norm_backward(values, inverse, gain_row, upstream):
    scaled = upstream * gain_row
    return inverse * scaled - values * inverse**3 * jnp.mean(
        scaled * values, axis=-1, keepdims=True
    )


def segments_of(lengths, places):
    upto = jnp.arange(lengths.shape[0])
    limits = PROMPT + jnp.sum(
        jnp.where(upto[:, None] <= upto[None, :], lengths[:, None], 0), axis=0
    )
    passed = jnp.sum((places[:, None] >= limits[None, :]).astype(jnp.int32), axis=1)
    return jnp.where(places < PROMPT, 0, 1 + passed)


def body(
    tokens,
    cotangent,
    norm_gains,
    qkv_weight,
    out_weight,
    router_weight,
    adapter_down,
    adapter_qkv,
    adapter_out,
    adapter_router,
    expert_input,
    expert_output,
    expert_down,
    expert_lift,
    routes,
    adapter_ids,
    cont_lengths,
):
    low = jnp.bfloat16
    piece = tokens.shape[0]
    parts = lax.axis_size("expert")
    groups = lax.axis_size("dp")
    ways = parts * groups
    me = lax.axis_index("expert")
    total = parts * piece
    experts = EXP_DEV * parts
    width = D // parts
    share = D // ways
    route_rows = ADAPTERS * RANK // ways
    adapter = adapter_ids[0]

    matrix_out = lax.all_gather(expert_output, "dp", axis=1, tiled=True)

    group_ids = lax.all_gather(adapter_ids, "dp", axis=0, tiled=True)
    hot = group_ids[:, None] == jnp.arange(ADAPTERS, dtype=jnp.int32)
    group_hot = hot.astype(jnp.float32)
    adapter_cols = expert_lift.shape[3]
    pairs = jnp.stack([expert_down.transpose(0, 2, 3, 1), expert_lift])
    pairs = pairs.transpose(2, 0, 1, 3, 4).reshape(ADAPTERS, 2 * EXP_DEV * RANK * adapter_cols)
    pairs = dot_plain(hot.astype(low), pairs).astype(low)
    pairs = lax.all_to_all(
        pairs.reshape(groups, 2 * EXP_DEV * RANK, adapter_cols), "dp", split_axis=0, concat_axis=0, tiled=True
    )
    pairs = pairs.reshape(groups, 2, EXP_DEV * RANK, adapter_cols).transpose(1, 2, 0, 3)
    pairs = pairs.reshape(2, EXP_DEV * RANK, D)
    pairs = jnp.pad(pairs, ((0, 0), (0, LANES - EXP_DEV * RANK), (0, 0)))

    def columns(array, upto):
        return jnp.pad(array, ((0, share - array.shape[0]), (0, upto - array.shape[1])))

    adapters = jnp.concatenate(
        [
            adapter_down.reshape(share, ADAPTERS * 3 * RANK),
            adapter_out.reshape(ADAPTERS * RANK, share).T,
            adapter_qkv.reshape(ADAPTERS * RANK, 3, share).transpose(2, 1, 0).reshape(share, 3 * LANES),
        ],
        axis=1,
    )
    row = jnp.arange(LANES, dtype=jnp.int32)[None, :]
    ids = group_ids[:, None]
    wanted = jnp.where(
        row < 48,
        ids * 48 + row,
        jnp.where(
            row < 64,
            384 + ids * RANK + row - 48,
            jnp.where(row < 112, 512 + LANES * ((row - 64) // RANK) + ids * RANK + (row - 64) % RANK, -1),
        ),
    ).reshape(1, groups * LANES)
    chosen = jnp.arange(adapters.shape[1], dtype=jnp.int32)[:, None] == wanted
    chosen = dot_plain(adapters, chosen.astype(low)).astype(low)

    qkv_blocks = (
        qkv_weight.reshape(share, 3, parts, width).transpose(2, 0, 1, 3).reshape(parts * share, 3 * width)
    )
    small = jnp.concatenate(
        [columns(router_weight, 32), columns(adapter_router, 32), columns(norm_gains.T, 64)], axis=1
    )
    dense_line, chosen_line = gather_weights(qkv_blocks, out_weight, small, chosen, 0)
    chosen_all = lax.all_to_all(
        chosen_line.reshape(parts * share, groups, LANES).transpose(1, 0, 2),
        "dp",
        split_axis=0,
        concat_axis=0,
        tiled=True,
    ).reshape(D, LANES)
    dense_line, expert_input, matrix_out, chosen_all, pairs = lax.optimization_barrier(
        (dense_line, expert_input, matrix_out, chosen_all, pairs)
    )
    dense_all = lax.all_gather(dense_line, "dp", axis=0, tiled=True)
    (tokens_all,) = line_gather([tokens], 1, 2)
    matrix_in = lax.all_gather(expert_input, "dp", axis=1, tiled=True)
    small_at = D + 3 * width

    picked, router_rows, gain_rows = pick_rows(chosen_all, dense_all, small_at, experts)
    down_query, down_mix, down_route = picked[:16], picked[16:32], picked[32:48]
    lift_mix = picked[48:64]
    lift_query = (
        picked[64:112].reshape(3, RANK, ways, share).transpose(1, 2, 0, 3).reshape(RANK, 3, parts, width)
    )
    lift_query = lax.dynamic_index_in_dim(lift_query, me, 2, keepdims=False).reshape(RANK, 3 * width)
    by_owner = dense_all[:, small_at : small_at + LANES].reshape(ways, share, LANES)
    lift_route = lax.dynamic_slice_in_dim(
        by_owner[:, :route_rows, 32 : 32 + experts].reshape(ADAPTERS * RANK, experts),
        adapter * RANK,
        RANK,
        0,
    )
    lift_route = jnp.pad(lift_route, ((0, 0), (0, LANES - experts)))
    routed = jnp.any(routes[:, :, None] == jnp.arange(LANES, dtype=jnp.int32), axis=1).astype(jnp.float32)
    def shifted(array, by):
        return lax.ppermute(array, "expert", [(i, (i + by) % parts) for i in range(parts)])

    early, tokens_all = lax.optimization_barrier((cotangent, tokens_all))
    early_shifts, late_shifts = [1], list(range(2, parts))
    moved = {s: shifted(early, s) for s in early_shifts}

    normed_low, rank_query, qkv_low = project_qkv(
        tokens_all, gain_rows[0:1], down_query, lift_query, dense_all
    )
    segments = segments_of(cont_lengths[0], jnp.arange(total, dtype=jnp.int32))
    segment_column, segment_row = segments[:, None], segments[None, :]
    mixed_low, log_mass = run_attention(segment_column, segment_row, qkv_low, 3)

    middle, rank_mix, inverse_second, second_low, rank_route, router_probs, gates = finish_attention(
        experts,
        mixed_low,
        tokens,
        down_mix,
        lift_mix,
        gain_rows[1:2],
        down_route,
        router_rows,
        lift_route,
        routed,
        dense_all,
    )
    held = lax.optimization_barrier([second_low] + [moved[s] for s in early_shifts])
    second_low = held[0]
    moved.update(zip(early_shifts, held[1:]))
    second_all, gates_all = line_gather([second_low, gates], 4, 2)

    late, second_all = lax.optimization_barrier((cotangent, second_all))
    moved.update({s: shifted(late, s) for s in late_shifts})
    cotangents = [cotangent] + [moved[s] for s in range(1, parts)]
    output_left, output_right, ranks, gate, up = experts_forward(
        second_all, gates_all, pairs[0], pairs[1], matrix_in, matrix_out
    )
    output_left = lax.psum_scatter(output_left, "expert", scatter_dimension=0, tiled=True)
    slot_sum, rank_expert_grad, lift_expert_grad = experts_backward(
        cotangents, gates_all, ranks, pairs[0], pairs[1], matrix_in, matrix_out, gate, up, 5
    )
    output_left, output_right, slot_sum = lax.optimization_barrier(
        (output_left, output_right, slot_sum)
    )
    output_right = lax.psum_scatter(output_right, "expert", scatter_dimension=0, tiled=True)
    output_sum = jnp.concatenate([output_left, output_right], axis=1)
    layer_output = (middle + output_sum.astype(jnp.float32)).astype(low)

    lift_sent = lift_expert_grad[: EXP_DEV * RANK]
    down_sent = dot_left(rank_expert_grad[:, : EXP_DEV * RANK], second_all)
    expert_sent = (
        jnp.concatenate([lift_sent, down_sent], axis=0)
        .astype(low)
        .reshape(2 * EXP_DEV * RANK, groups, -1)
        .transpose(1, 0, 2)
    )
    expert_got = lax.all_to_all(expert_sent, "dp", split_axis=0, concat_axis=0, tiled=True)
    by_adapter = jnp.einsum(
        "ga,gkc->akc", group_hot, expert_got.astype(jnp.float32), precision=lax.Precision.HIGHEST
    ).reshape(ADAPTERS, 2, EXP_DEV, RANK, -1)
    explift_grad = by_adapter[:, 0].transpose(1, 0, 2, 3)
    expdown_grad = by_adapter[:, 1].transpose(1, 3, 0, 2)

    mixed_grad, middle_grad, branch_grad, logit_grad, rank_route_grad, rank_mix_grad = middle_backward(
        width,
        slot_sum,
        router_probs,
        routed,
        middle,
        inverse_second,
        cotangent,
        gain_rows[1:2],
        router_rows,
        lift_route,
        down_route,
        lift_mix,
        down_mix,
        dense_all,
    )

    back_query, back_key, back_value = run_attention_back(
        segment_column, segment_row, qkv_low, mixed_grad, log_mass, 6
    )
    qkv_back = jnp.concatenate([back_query, back_key, back_value], axis=1)
    rank_query_grad = dot_right(qkv_back, lift_query).astype(low)
    first_terms = first_products([back_query, back_key, back_value], rank_query_grad, down_query, dense_all)
    lift_query_grad = lax.dynamic_update_slice(
        jnp.zeros((RANK, 3, parts, width), jnp.float32),
        dot_left(rank_query, qkv_back).reshape(RANK, 3, 1, width),
        (0, 0, me, 0),
    )
    downs = jnp.concatenate(
        [
            dot_left(rank_query_grad, normed_low),
            dot_left(rank_mix_grad, mixed_low),
            dot_left(rank_route_grad, second_low),
            dot_left(rank_mix, branch_grad),
        ]
    )
    owned = jnp.concatenate(
        [
            downs.reshape(4 * RANK, ways, share).transpose(1, 0, 2).reshape(ways, -1),
            lift_query_grad.reshape(RANK, ways, 3 * share).transpose(1, 0, 2).reshape(ways, -1),
            jnp.broadcast_to(dot_left(rank_route, logit_grad)[:, :experts].reshape(1, -1), (ways, RANK * experts)),
        ],
        axis=1,
    ).astype(low)
    first_grad = lax.psum_scatter(first_terms, "expert", scatter_dimension=0, tiled=True).astype(jnp.float32)
    got = lax.all_to_all(owned, ("dp", "expert"), split_axis=0, concat_axis=0, tiled=True)
    inputs = tokens.astype(jnp.float32)
    inverse_first = norm_inverse(inputs)
    input_grad = (
        middle_grad + norm_backward(inputs, inverse_first, gain_rows[0:1], first_grad)
    ).astype(low)
    summed = jnp.einsum(
        "ga,gek->ak",
        group_hot,
        got.astype(jnp.float32).reshape(groups, parts, -1),
        precision=lax.Precision.HIGHEST,
    )
    n_down, n_qkv = 4 * RANK * share, 3 * RANK * share
    downs = summed[:, :n_down].reshape(ADAPTERS, 4, RANK, share)
    down_grad = downs[:, :3].transpose(3, 0, 1, 2)
    proj_grad = downs[:, 3]
    qkv_grad = summed[:, n_down : n_down + n_qkv].reshape(ADAPTERS, RANK, 3 * share)
    router_grad = lax.dynamic_slice_in_dim(
        summed[:, n_down + n_qkv :].reshape(ADAPTERS * RANK, experts),
        (lax.axis_index("dp") * parts + me) * route_rows,
        route_rows,
        0,
    )
    return (
        layer_output,
        input_grad,
        down_grad,
        qkv_grad,
        proj_grad,
        router_grad,
        expdown_grad,
        explift_grad,
    )


def solution(mesh):
    placed = (
        P(("dp", "expert"), None),
        P(("dp", "expert"), None),
        P(None, ("dp", "expert")),
        P(("dp", "expert"), None),
        P(("dp", "expert"), None),
        P(("dp", "expert"), None),
        P(("dp", "expert"), None, None, None),
        P(None, None, ("dp", "expert")),
        P(None, None, ("dp", "expert")),
        P(("dp", "expert"), None),
        P("expert", "dp", None),
        P("expert", "dp", None),
        P("expert", "dp", None, None),
        P("expert", None, None, "dp"),
        P(("dp", "expert"), None),
        P("dp"),
        P("dp", None),
    )
    return jax.shard_map(
        body,
        mesh=mesh,
        in_specs=placed,
        out_specs=(
            P(("dp", "expert"), None),
            P(("dp", "expert"), None),
            P(("dp", "expert"), None, None, None),
            P(None, None, ("dp", "expert")),
            P(None, None, ("dp", "expert")),
            P(("dp", "expert"), None),
            P("expert", "dp", None, None),
            P("expert", None, None, "dp"),
        ),
        check_vma=False,
    )
```

```python
import functools

import jax
import jax.numpy as jnp
from jax import lax
from jax.experimental import pallas as pl
from jax.experimental.pallas import tpu as pltpu
from jax.sharding import PartitionSpec as P

D = 2048
HEAD = 128
FF = 1024
RANK = 16
ADAPTERS = 8
EXP_DEV = 4
PROMPT = 1024
EPSILON = 1e-05
MASKED = -1e30
LANES = 128
BLOCK = 256
ROWS = 1280
TILE = 512
HALF = EXP_DEV // 2
SMALL = 1024

MESH = pl.DeviceIdType.MESH
ANY = pl.BlockSpec(memory_space=pl.ANY)
VMEM = pl.BlockSpec(memory_space=pltpu.VMEM)


def dot_plain(left, right):
    return jnp.dot(left, right, preferred_element_type=jnp.float32)


def dot_left(left, right):
    return lax.dot_general(
        left, right, (((0,), (0,)), ((), ())), preferred_element_type=jnp.float32
    )


def dot_right(left, right):
    return lax.dot_general(
        left, right, (((1,), (1,)), ((), ())), preferred_element_type=jnp.float32
    )


def transfer_cost(elements):
    return pl.CostEstimate(flops=0, bytes_accessed=140 * elements, transcendentals=0)


def greet_line(me, parts):
    barrier = pltpu.get_barrier_semaphore()

    @pl.when(me > 0)
    def _():
        pl.semaphore_signal(barrier, inc=1, device_id={"expert": me - 1}, device_id_type=MESH)

    @pl.when(me < parts - 1)
    def _():
        pl.semaphore_signal(barrier, inc=1, device_id={"expert": me + 1}, device_id_type=MESH)

    pl.semaphore_wait(barrier, jnp.where((me > 0) & (me < parts - 1), 2, 1))


def greet_all(me, parts):
    barrier = pltpu.get_barrier_semaphore()
    for k in range(1, parts):
        pl.semaphore_signal(
            barrier, inc=1, device_id={"expert": lax.rem(me + k, parts)}, device_id_type=MESH
        )
    pl.semaphore_wait(barrier, parts - 1)


def gather_kernel(parts, pieces, count, *refs):
    srcs, dsts = refs[:count], refs[count : 2 * count]
    own_sem, send_up, recv_up, send_down, recv_down = refs[2 * count :]
    me = lax.axis_index("expert")
    greet_line(me, parts)

    def block(i, origin, piece):
        rows = srcs[i].shape[0] // pieces
        at = origin * srcs[i].shape[0] + piece * rows
        return dsts[i].at[pl.ds(pl.multiple_of(at, rows), rows)]

    def hop(i, src, origin, piece, to, send, recv, step, got):
        n = i * pieces + piece
        return pltpu.make_async_remote_copy(
            src_ref=src,
            dst_ref=block(i, origin, piece),
            send_sem=send.at[n, step],
            recv_sem=recv.at[n, got],
            device_id={"expert": to},
            device_id_type=MESH,
        )

    streams = ((1, send_up, recv_up), (-1, send_down, recv_down))
    for step in range(parts - 1):
        for piece in range(pieces):
            for i in range(count):
                for way, send, recv in streams:
                    origin, to = me - way * step, me + way
                    has = (origin >= 0) & (origin < parts)
                    if step > 0:

                        @pl.when(has)
                        def _(i=i, origin=origin, piece=piece, send=send, recv=recv, step=step):
                            here = block(i, origin, piece)
                            hop(i, here, origin, piece, me, send, recv, step, step - 1).wait_recv()

                    @pl.when(has & (to >= 0) & (to < parts))
                    def _(i=i, origin=origin, piece=piece, to=to, send=send, recv=recv, step=step):
                        rows = srcs[i].shape[0] // pieces
                        src = srcs[i].at[piece * rows : (piece + 1) * rows] if step == 0 else block(i, origin, piece)
                        hop(i, src, origin, piece, to, send, recv, step, step).start()

        if step == 0:
            for i in range(count):
                rows = srcs[i].shape[0]
                there = dsts[i].at[pl.ds(pl.multiple_of(me * rows, rows), rows)]
                pltpu.make_async_copy(srcs[i], there, own_sem.at[i]).start()
    for i in range(count):
        rows = srcs[i].shape[0]
        there = dsts[i].at[pl.ds(pl.multiple_of(me * rows, rows), rows)]
        pltpu.make_async_copy(srcs[i], there, own_sem.at[i]).wait()
    for way, send, recv in streams:
        to, last = me + way, me - way * (parts - 1)
        for i in range(count):
            for piece in range(pieces):

                @pl.when((last >= 0) & (last < parts))
                def _(i=i, piece=piece, last=last, send=send, recv=recv):
                    here = block(i, last, piece)
                    hop(i, here, last, piece, me, send, recv, 0, parts - 2).wait_recv()

                for step in range(parts - 1):
                    origin = me - way * step

                    @pl.when((origin >= 0) & (origin < parts) & (to >= 0) & (to < parts))
                    def _(i=i, piece=piece, origin=origin, send=send, recv=recv, step=step):
                        here = block(i, origin, piece)
                        hop(i, here, origin, piece, me, send, recv, step, step).wait_send()


def line_gather(arrays, cid, pieces=1):
    parts = lax.axis_size("expert")
    n = len(arrays)
    sem = pltpu.SemaphoreType.DMA
    return pl.pallas_call(
        functools.partial(gather_kernel, parts, pieces, n),
        out_shape=[jax.ShapeDtypeStruct((parts * a.shape[0],) + a.shape[1:], a.dtype) for a in arrays],
        in_specs=[ANY] * n,
        out_specs=[ANY] * n,
        scratch_shapes=[sem((n,))] + [sem((n * pieces, parts - 1))] * 4,
        cost_estimate=transfer_cost(parts * sum(a.size for a in arrays)),
        compiler_params=pltpu.CompilerParams(collective_id=cid, has_side_effects=True),
        name="line_gather_%d" % cid,
    )(*arrays)


def exchange_kernel(parts, count, stack, *refs):
    srcs, dsts = refs[:count], refs[count : 2 * count]
    own_sem, send, recv = refs[2 * count :]
    me = lax.axis_index("expert")
    greet_all(me, parts)

    def piece(i, owner):
        rows = srcs[i].shape[0] // parts
        return srcs[i].at[pl.ds(pl.multiple_of(owner * rows, rows), rows)]

    def place(i, origin):
        rows, cols = srcs[i].shape[0] // parts, srcs[i].shape[1]
        if stack:
            return dsts[i].at[pl.ds(pl.multiple_of(origin * rows, rows), rows)]
        return dsts[i].at[:, pl.ds(pl.multiple_of(origin * cols, cols), cols)]

    copies = []
    for k in list(range(parts - 1, 0, -1)):
        to = lax.rem(me + k, parts)
        for i in range(count):
            copy = pltpu.make_async_remote_copy(
                src_ref=piece(i, to),
                dst_ref=place(i, me),
                send_sem=send.at[i, k - 1],
                recv_sem=recv.at[i, k - 1],
                device_id={"expert": to},
                device_id_type=MESH,
            )
            copy.start()
            copies.append(copy)
    for i in range(count):
        own = pltpu.make_async_copy(piece(i, me), place(i, me), own_sem.at[i])
        own.start()
        own.wait()
    for copy in copies:
        copy.wait_send()
    for k in list(range(parts - 1, 0, -1)):
        origin = lax.rem(me + parts - k, parts)
        for i in range(count):
            pltpu.make_async_remote_copy(
                src_ref=piece(i, me),
                dst_ref=place(i, origin),
                send_sem=send.at[i, k - 1],
                recv_sem=recv.at[i, k - 1],
                device_id={"expert": origin},
                device_id_type=MESH,
            ).wait_recv()


def exchange(arrays, cid, stack=False):
    parts = lax.axis_size("expert")
    n = len(arrays)
    sem = pltpu.SemaphoreType.DMA
    return pl.pallas_call(
        functools.partial(exchange_kernel, parts, n, stack),
        out_shape=[
            jax.ShapeDtypeStruct(
                a.shape if stack else (a.shape[0] // parts, a.shape[1] * parts), a.dtype
            )
            for a in arrays
        ],
        in_specs=[ANY] * n,
        out_specs=[ANY] * n,
        scratch_shapes=[sem((n,)), sem((n, parts - 1)), sem((n, parts - 1))],
        cost_estimate=transfer_cost(sum(a.size for a in arrays)),
        compiler_params=pltpu.CompilerParams(collective_id=cid, has_side_effects=True),
        name="exchange_%d" % cid,
    )(*arrays)


def reduce_kernel(parts, pieces, src, out, slot_up, slot_down, send_up, recv_up, send_down, recv_down):
    me = lax.axis_index("expert")
    greet_line(me, parts)
    rows = out.shape[0]
    part = rows // pieces
    step_rows = 16

    def hop(ref, slot, step, piece, to, send, recv):
        return pltpu.make_async_remote_copy(
            src_ref=ref,
            dst_ref=slot.at[step, piece * part : (piece + 1) * part],
            send_sem=send.at[step, piece],
            recv_sem=recv.at[step, piece],
            device_id={"expert": to},
            device_id_type=MESH,
        )

    def landed(slot, step, piece, send, recv):
        return hop(slot.at[step, piece * part : (piece + 1) * part], slot, step, piece, me, send, recv)

    streams = ((True, slot_up, send_up, recv_up), (False, slot_down, send_down, recv_down))
    for step in range(parts - 1):
        for piece in range(pieces):
            for up, slot, send, recv in streams:
                line = me if up else parts - 1 - me
                dest_line = parts - 1 - step + line
                dest = dest_line if up else parts - 1 - dest_line
                to = me + 1 if up else me - 1

                @pl.when(line == 0)
                def _(dest=dest, slot=slot, step=step, piece=piece, to=to, send=send, recv=recv):
                    there = pl.ds(pl.multiple_of(dest * rows + piece * part, part), part)
                    hop(src.at[there], slot, step, piece, to, send, recv).start()

                if step > 0:

                    @pl.when((line > 0) & (step >= line) & (line < parts - 1))
                    def _(dest=dest, slot=slot, step=step, piece=piece, to=to, send=send, recv=recv):
                        landed(slot, step - 1, piece, send, recv).wait_recv()

                        @pl.loop(0, part // step_rows)
                        def _(r):
                            at = piece * part + r * step_rows
                            here = pl.ds(pl.multiple_of(at, step_rows), step_rows)
                            there = pl.ds(pl.multiple_of(dest * rows + at, step_rows), step_rows)
                            both = slot[step - 1, here, :].astype(jnp.float32) + src[there, :].astype(jnp.float32)
                            slot[step - 1, here, :] = both.astype(jnp.bfloat16)

                        sent = slot.at[step - 1, piece * part : (piece + 1) * part]
                        hop(sent, slot, step, piece, to, send, recv).start()

    @pl.loop(0, rows // step_rows)
    def _(r):
        here = pl.ds(pl.multiple_of(r * step_rows, step_rows), step_rows)
        there = pl.ds(pl.multiple_of(me * rows + r * step_rows, step_rows), step_rows)
        out[here, :] = src[there, :].astype(jnp.float32)

    last = parts - 2
    for piece in range(pieces):
        for up, slot, send, recv in streams:
            line = me if up else parts - 1 - me

            @pl.when(line > 0)
            def _(slot=slot, piece=piece, send=send, recv=recv):
                landed(slot, last, piece, send, recv).wait_recv()

                @pl.loop(0, part // step_rows)
                def _(r):
                    here = pl.ds(pl.multiple_of(piece * part + r * step_rows, step_rows), step_rows)
                    out[here, :] = out[here, :] + slot[last, here, :].astype(jnp.float32)

    for up, slot, send, recv in streams:
        line = me if up else parts - 1 - me
        for step in range(parts - 1):
            for piece in range(pieces):

                @pl.when((step >= line) & (line < parts - 1))
                def _(slot=slot, step=step, piece=piece, send=send, recv=recv):
                    landed(slot, step, piece, send, recv).wait_send()


def line_reduce(terms, cid, pieces=1):
    parts = lax.axis_size("expert")
    rows, cols = terms.shape[0] // parts, terms.shape[1]
    sem = pltpu.SemaphoreType.DMA
    return pl.pallas_call(
        functools.partial(reduce_kernel, parts, pieces),
        out_shape=jax.ShapeDtypeStruct((rows, cols), jnp.float32),
        in_specs=[VMEM],
        out_specs=VMEM,
        scratch_shapes=[pltpu.VMEM((parts - 1, rows, cols), jnp.bfloat16)] * 2
        + [sem((parts - 1, pieces))] * 4,
        cost_estimate=transfer_cost(terms.size),
        compiler_params=pltpu.CompilerParams(
            collective_id=cid, has_side_effects=True, vmem_limit_bytes=48 * 1024 * 1024
        ),
        name="line_reduce_%d" % cid,
    )(terms)


def weights_kernel(parts, blocks, out, small, chosen, dst, dst_chosen, own_sem, send, recv, send_up, recv_up, send_down, recv_down):
    me = lax.axis_index("expert")
    share = out.shape[0]
    left, wide = out.shape[1], blocks.shape[1]
    greet_all(me, parts)

    def rows(origin):
        return pl.ds(pl.multiple_of(origin * share, share), share)

    def exchanged(k, to, origin):
        return pltpu.make_async_remote_copy(
            src_ref=blocks.at[rows(to)],
            dst_ref=dst.at[rows(origin), left : left + wide],
            send_sem=send.at[k - 1],
            recv_sem=recv.at[k - 1],
            device_id={"expert": to},
            device_id_type=MESH,
        )

    shared = ((out, dst, 0), (small, dst, left + wide), (chosen, dst_chosen, 0))

    def place(i, origin):
        src, into, at = shared[i]
        return into.at[rows(origin), at : at + src.shape[1]]

    def hop(i, src, origin, to, send_sem, recv_sem):
        return pltpu.make_async_remote_copy(
            src_ref=src,
            dst_ref=place(i, origin),
            send_sem=send_sem,
            recv_sem=recv_sem,
            device_id={"expert": to},
            device_id_type=MESH,
        )

    streams = ((1, send_up, recv_up), (-1, send_down, recv_down))
    for step in range(parts - 1):
        for way, sends, recvs in streams:
            origin, to = me - way * step, me + way
            has = (origin >= 0) & (origin < parts)
            for i in range(3):
                if step > 0:

                    @pl.when(has)
                    def _(i=i, origin=origin, sends=sends, recvs=recvs, step=step):
                        hop(i, place(i, origin), origin, me, sends.at[i, step], recvs.at[i, step - 1]).wait_recv()

                @pl.when(has & (to >= 0) & (to < parts))
                def _(i=i, origin=origin, to=to, sends=sends, recvs=recvs, step=step):
                    src = shared[i][0] if step == 0 else place(i, origin)
                    hop(i, src, origin, to, sends.at[i, step], recvs.at[i, step]).start()

        if step == 0:
            for k in range(parts - 1, 0, -1):
                to = lax.rem(me + k, parts)
                exchanged(k, to, me).start()
            owns = [
                pltpu.make_async_copy(src, target, own_sem.at[i])
                for i, (src, target) in enumerate(
                    (
                        (blocks.at[rows(me)], dst.at[rows(me), left : left + wide]),
                        (out, place(0, me)),
                        (small, place(1, me)),
                        (chosen, place(2, me)),
                    )
                )
            ]
            for copy in owns:
                copy.start()

    for copy in owns:
        copy.wait()
    for way, sends, recvs in streams:
        to, last = me + way, me - way * (parts - 1)
        for i in range(3):

            @pl.when((last >= 0) & (last < parts))
            def _(i=i, last=last, sends=sends, recvs=recvs):
                hop(i, place(i, last), last, me, sends.at[i, 0], recvs.at[i, parts - 2]).wait_recv()

            for step in range(parts - 1):
                origin = me - way * step

                @pl.when((origin >= 0) & (origin < parts) & (to >= 0) & (to < parts))
                def _(i=i, origin=origin, sends=sends, recvs=recvs, step=step):
                    hop(i, place(i, origin), origin, me, sends.at[i, step], recvs.at[i, step]).wait_send()

    for k in range(parts - 1, 0, -1):
        exchanged(k, lax.rem(me + k, parts), me).wait_send()
        exchanged(k, me, lax.rem(me + parts - k, parts)).wait_recv()


def gather_weights(blocks, out, small, chosen, cid):
    parts = lax.axis_size("expert")
    sem = pltpu.SemaphoreType.DMA
    rows, cols = blocks.shape[0], out.shape[1] + blocks.shape[1] + small.shape[1]
    return pl.pallas_call(
        functools.partial(weights_kernel, parts),
        out_shape=[
            jax.ShapeDtypeStruct((rows, cols), blocks.dtype),
            jax.ShapeDtypeStruct((rows, chosen.shape[1]), blocks.dtype),
        ],
        in_specs=[ANY] * 4,
        out_specs=[ANY] * 2,
        scratch_shapes=[sem((4,)), sem((parts - 1,)), sem((parts - 1,))] + [sem((3, parts - 1))] * 4,
        cost_estimate=transfer_cost(rows * (cols + chosen.shape[1])),
        compiler_params=pltpu.CompilerParams(collective_id=cid, has_side_effects=True),
        name="gather_weights",
    )(blocks, out, small, chosen)


def diagonal_mask(column_ref, row_ref, block):
    here = pl.ds(block * BLOCK, BLOCK)
    seg_query = column_ref[here, :]
    seg_key = row_ref[:, here]
    shape = (BLOCK, BLOCK)
    causal = lax.broadcasted_iota(jnp.int32, shape, 1) <= lax.broadcasted_iota(jnp.int32, shape, 0)
    same = (seg_query == seg_key) & causal
    return same | ((seg_key == 0) & (seg_query != 0))


def masked_scores(query, key_ref, column_ref, row_ref, block):
    scale = HEAD ** (-0.5)
    here = pl.ds(block * BLOCK, BLOCK)
    own = dot_right(query, key_ref[here, :]) * scale
    own = jnp.where(diagonal_mask(column_ref, row_ref, block), own, MASKED)
    if block == 0:
        return own
    ahead = dot_right(query, key_ref[: block * BLOCK, :]) * scale
    return jnp.concatenate([ahead, own], axis=1)


def row_block(owner, rows):
    return pl.ds(pl.multiple_of(owner * rows, rows), rows)


def attention_kernel(
    parts, column_ref, row_ref, query_ref, key_ref, value_ref, mixed_ref, lse_ref, heads_out, own_sem, send, recv
):
    head, heads = pl.program_id(0), pl.num_programs(0)
    me = lax.axis_index("expert")
    total = query_ref.shape[0]
    piece = total // parts

    @pl.when(head == 0)
    def _():
        greet_all(me, parts)

    def moved(h, k, origin, to):
        lanes = pl.ds(pl.multiple_of((origin * heads + h) * HEAD, HEAD), HEAD)
        return pltpu.make_async_remote_copy(
            src_ref=heads_out.at[h, row_block(to, piece)],
            dst_ref=mixed_ref.at[:, lanes],
            send_sem=send.at[h, k - 1],
            recv_sem=recv.at[h, k - 1],
            device_id={"expert": to},
            device_id_type=MESH,
        )

    def kept(h):
        lanes = pl.ds(pl.multiple_of((me * heads + h) * HEAD, HEAD), HEAD)
        return pltpu.make_async_copy(heads_out.at[h, row_block(me, piece)], mixed_ref.at[:, lanes], own_sem.at[h])

    for block in range(total // BLOCK):
        here = pl.ds(block * BLOCK, BLOCK)
        scores = masked_scores(query_ref[here, :], key_ref, column_ref, row_ref, block)
        top = jnp.max(scores, axis=1, keepdims=True)
        expd = jnp.exp(scores - top)
        mass = jnp.sum(expd, axis=1, keepdims=True)
        probs = (expd / mass).astype(jnp.bfloat16)
        mixed = dot_plain(probs, value_ref[: (block + 1) * BLOCK, :])
        heads_out[head, here, :] = mixed.astype(jnp.bfloat16)
        lse_ref[0, here, :] = top + jnp.log(mass)

    kept(head).start()
    for k in range(parts - 1, 0, -1):
        moved(head, k, me, lax.rem(me + k, parts)).start()

    @pl.when(head == heads - 1)
    def _():
        @pl.loop(0, heads)
        def _(h):
            kept(h).wait()
            for k in range(parts - 1, 0, -1):
                moved(h, k, me, lax.rem(me + k, parts)).wait_send()
                moved(h, k, lax.rem(me + parts - k, parts), me).wait_recv()


def head_specs(total, heads):
    return [
        pl.BlockSpec((total, HEAD), lambda h, part=part: (0, part * heads + h)) for part in range(3)
    ]


def run_attention(column, row, qkv, cid):
    total, heads = qkv.shape[0], qkv.shape[1] // (3 * HEAD)
    parts = lax.axis_size("expert")
    whole = pl.BlockSpec(memory_space=pltpu.VMEM)
    sem = pltpu.SemaphoreType.DMA
    return pl.pallas_call(
        functools.partial(attention_kernel, parts),
        grid=(heads,),
        in_specs=[whole, whole] + head_specs(total, heads),
        out_specs=[ANY, pl.BlockSpec((1, total, 1), lambda h: (h, 0, 0))],
        out_shape=[
            jax.ShapeDtypeStruct((total // parts, D), jnp.bfloat16),
            jax.ShapeDtypeStruct((heads, total, 1), jnp.float32),
        ],
        scratch_shapes=[
            pltpu.VMEM((heads, total, HEAD), jnp.bfloat16),
            sem((heads,)),
            sem((heads, parts - 1)),
            sem((heads, parts - 1)),
        ],
        compiler_params=pltpu.CompilerParams(
            dimension_semantics=("arbitrary",),
            vmem_limit_bytes=48 * 1024 * 1024,
            collective_id=cid,
            has_side_effects=True,
        ),
        cost_estimate=pl.CostEstimate(
            flops=0, bytes_accessed=200 * total * heads * HEAD, transcendentals=heads * total * total // 2
        ),
        name="attention",
    )(column, row, qkv, qkv, qkv)


def attention_back_kernel(
    parts,
    column_ref,
    row_ref,
    query_ref,
    key_ref,
    value_ref,
    lse_ref,
    sent_ref,
    back_query_ref,
    back_key_ref,
    back_value_ref,
    key_acc,
    value_acc,
    grads,
    own_sem,
    send,
    recv,
):
    head, heads = pl.program_id(0), pl.num_programs(0)
    me = lax.axis_index("expert")
    scale = HEAD ** (-0.5)
    total = query_ref.shape[0]
    piece = total // parts

    def moved(h, k, origin, to):
        lanes = pl.ds(pl.multiple_of(h * HEAD, HEAD), HEAD)
        return pltpu.make_async_remote_copy(
            src_ref=sent_ref.at[row_block(to, piece), lanes],
            dst_ref=grads.at[h, row_block(origin, piece)],
            send_sem=send.at[h, k - 1],
            recv_sem=recv.at[h, k - 1],
            device_id={"expert": to},
            device_id_type=MESH,
        )

    def kept(h):
        lanes = pl.ds(pl.multiple_of(h * HEAD, HEAD), HEAD)
        return pltpu.make_async_copy(
            sent_ref.at[row_block(me, piece), lanes], grads.at[h, row_block(me, piece)], own_sem.at[h]
        )

    @pl.when(head == 0)
    def _():
        greet_all(me, parts)

        @pl.loop(0, heads)
        def _(h):
            for k in range(parts - 1, 0, -1):
                moved(h, k, me, lax.rem(me + k, parts)).start()
            kept(h).start()

    kept(head).wait()
    for k in range(parts - 1, 0, -1):
        moved(head, k, lax.rem(me + parts - k, parts), me).wait_recv()
    key_acc[...] = jnp.zeros_like(key_acc)
    value_acc[...] = jnp.zeros_like(value_acc)
    for block in range(total // BLOCK):
        here = pl.ds(block * BLOCK, BLOCK)
        upto = pl.ds(0, (block + 1) * BLOCK)
        query, grad = query_ref[here, :], grads[head, here, :]
        scores = masked_scores(query, key_ref, column_ref, row_ref, block)
        probs = jnp.exp(scores - lse_ref[0, here, :])
        prob_back = dot_right(grad, value_ref[upto, :])
        delta = jnp.sum(probs * prob_back, axis=1, keepdims=True)
        score_grad = (probs * (prob_back - delta)).astype(jnp.bfloat16)
        back_query_ref[here, :] = (dot_plain(score_grad, key_ref[upto, :]) * scale).astype(jnp.bfloat16)
        key_acc[upto, :] += dot_left(score_grad, query)
        value_acc[upto, :] += dot_left(probs.astype(jnp.bfloat16), grad)
    back_key_ref[...] = (key_acc[...] * scale).astype(jnp.bfloat16)
    back_value_ref[...] = value_acc[...].astype(jnp.bfloat16)

    @pl.when(head == heads - 1)
    def _():
        @pl.loop(0, heads)
        def _(h):
            for k in range(parts - 1, 0, -1):
                moved(h, k, me, lax.rem(me + k, parts)).wait_send()


def run_attention_back(column, row, qkv, sent, lse, cid):
    total, heads = qkv.shape[0], qkv.shape[1] // (3 * HEAD)
    parts = lax.axis_size("expert")
    whole = pl.BlockSpec(memory_space=pltpu.VMEM)
    head = pl.BlockSpec((total, HEAD), lambda h: (0, h))
    sem = pltpu.SemaphoreType.DMA
    return pl.pallas_call(
        functools.partial(attention_back_kernel, parts),
        grid=(heads,),
        in_specs=[whole, whole]
        + head_specs(total, heads)
        + [pl.BlockSpec((1, total, 1), lambda h: (h, 0, 0)), ANY],
        out_specs=[head] * 3,
        out_shape=[jax.ShapeDtypeStruct((total, heads * HEAD), jnp.bfloat16)] * 3,
        scratch_shapes=[pltpu.VMEM((total, HEAD), jnp.float32)] * 2
        + [
            pltpu.VMEM((heads, total, HEAD), jnp.bfloat16),
            sem((heads,)),
            sem((heads, parts - 1)),
            sem((heads, parts - 1)),
        ],
        compiler_params=pltpu.CompilerParams(
            dimension_semantics=("arbitrary",),
            vmem_limit_bytes=48 * 1024 * 1024,
            collective_id=cid,
            has_side_effects=True,
        ),
        cost_estimate=pl.CostEstimate(
            flops=0, bytes_accessed=200 * total * heads * HEAD, transcendentals=heads * total * total // 2
        ),
        name="attention_back",
    )(column, row, qkv, qkv, qkv, lse, sent)


def own_lift(lift_ref, j):
    row = lax.broadcasted_iota(jnp.int32, (LANES, TILE), 0)
    own = (row >= j * RANK) & (row < (j + 1) * RANK)
    return jnp.where(own, lift_ref[...].astype(jnp.float32), 0.0).astype(jnp.bfloat16)


def gate_column(gates_ref, here, j):
    shape = (ROWS, LANES)
    mine = lax.broadcasted_iota(jnp.int32, shape, 1) == lax.axis_index("expert") * EXP_DEV + j
    return mine, jnp.sum(
        jnp.where(mine, gates_ref[here, :].astype(jnp.float32), 0.0), axis=1, keepdims=True
    )


def row_chunk(b, rows=None):
    rows = rows or ROWS
    return pl.ds(pl.multiple_of(b * rows, rows), rows)


def forward_kernel(
    rows_ref,
    gates_ref,
    down_ref,
    lift_gate_ref,
    lift_up_ref,
    in_gate_ref,
    in_up_ref,
    out_ref,
    *refs,
):
    output_ref, output_rest_ref, ranks_ref, gate_ref, up_ref, output_acc, stage, sems = refs
    j, f = pl.program_id(0), pl.program_id(1)
    total = rows_ref.shape[0]

    @pl.when((j == 0) & (f == 0))
    def _():
        @pl.loop(0, total // ROWS)
        def _(b):
            here = row_chunk(b)
            ranks_ref[here, :] = dot_right(rows_ref[here, :], down_ref[...]).astype(jnp.bfloat16)
            output_acc[here, :] = jnp.zeros((ROWS, D), jnp.float32)

    lift_gate, lift_up = own_lift(lift_gate_ref, j), own_lift(lift_up_ref, j)

    @pl.loop(0, total // ROWS)
    def _(b):
        here = row_chunk(b)
        rows = rows_ref[here, :]
        _, column = gate_column(gates_ref, here, j)
        gate = dot_plain(rows, in_gate_ref[0]) + dot_plain(ranks_ref[here, :], lift_gate)
        up = dot_plain(rows, in_up_ref[0]) + dot_plain(ranks_ref[here, :], lift_up)
        gate_ref[0, here, :] = gate.astype(jnp.bfloat16)
        up_ref[0, here, :] = up.astype(jnp.bfloat16)
        hidden = (column * (gate * jax.nn.sigmoid(gate) * up)).astype(jnp.bfloat16)
        output_acc[here, :] += dot_plain(hidden, out_ref[0])

    @pl.when((j == EXP_DEV - 1) & (f == FF // TILE - 1))
    def _():
        def copies(b):
            slot = lax.rem(b, 2)
            here = row_chunk(b, stage.shape[1])
            half = D // 2
            return [
                pltpu.make_async_copy(
                    stage.at[slot, :, h * half : (h + 1) * half], refs_out[h].at[here], sems.at[slot, h]
                )
                for h in range(2)
            ]

        refs_out = (output_ref, output_rest_ref)
        steps = total // stage.shape[1]

        @pl.loop(0, steps)
        def _(b):
            @pl.when(b >= 2)
            def _():
                for copy in copies(b - 2):
                    copy.wait()

            here = row_chunk(b, stage.shape[1])
            stage[lax.rem(b, 2)] = output_acc[here, :].astype(jnp.bfloat16)
            for copy in copies(b):
                copy.start()

        for b in range(steps - 2, steps):
            for copy in copies(b):
                copy.wait()


def weight_specs():
    tiles = FF // TILE
    return [
        pl.BlockSpec((LANES, TILE), lambda j, f: (0, f)),
        pl.BlockSpec((LANES, TILE), lambda j, f: (0, f + tiles)),
        pl.BlockSpec((1, D, TILE), lambda j, f: (j, 0, f)),
        pl.BlockSpec((1, D, TILE), lambda j, f: (j, 0, f + tiles)),
        pl.BlockSpec((1, TILE, D), lambda j, f: (j, f, 0)),
    ]


EXPERT_PARAMS = pltpu.CompilerParams(
    dimension_semantics=("arbitrary", "arbitrary"), vmem_limit_bytes=60 * 1024 * 1024
)


def experts_forward(rows, gates, down, lift, matrix_in, matrix_out):
    total = rows.shape[0]
    kept = pl.BlockSpec((1, total, TILE), lambda j, f: (j, 0, f))
    return pl.pallas_call(
        forward_kernel,
        grid=(EXP_DEV, FF // TILE),
        in_specs=[VMEM] * 3 + weight_specs(),
        out_specs=[
            ANY,
            ANY,
            pl.BlockSpec((total, LANES), lambda j, f: (0, 0), pipeline_mode=pl.Buffered(1)),
            kept,
            kept,
        ],
        out_shape=[
            jax.ShapeDtypeStruct((total, D // 2), jnp.bfloat16),
            jax.ShapeDtypeStruct((total, D // 2), jnp.bfloat16),
            jax.ShapeDtypeStruct((total, LANES), jnp.bfloat16),
            jax.ShapeDtypeStruct((EXP_DEV, total, FF), jnp.bfloat16),
            jax.ShapeDtypeStruct((EXP_DEV, total, FF), jnp.bfloat16),
        ],
        scratch_shapes=[
            pltpu.VMEM((total, D), jnp.float32),
            pltpu.VMEM((2, 160, D), jnp.bfloat16),
            pltpu.SemaphoreType.DMA((2, 2)),
        ],
        compiler_params=EXPERT_PARAMS,
        cost_estimate=pl.CostEstimate(
            flops=10 * EXP_DEV * total * D * FF,
            bytes_accessed=EXP_DEV * 6 * D * FF + 8 * total * D,
            transcendentals=EXP_DEV * total * FF,
        ),
        name="experts_forward",
    )(rows, gates, down, lift, lift, matrix_in, matrix_in, matrix_out)


def backward_kernel(
    parts,
    gates_ref,
    ranks_ref,
    down_ref,
    lift_gate_ref,
    lift_up_ref,
    in_gate_ref,
    in_up_ref,
    out_ref,
    gate_hbm,
    up_hbm,
    *refs,
):
    blocks, refs = refs[:parts], refs[parts:]
    sum_ref, rank_ref, lift_grad_ref, upstream, slot_acc, rank_acc, gate_acc, terms, gates, ups, load_sems, kept_sems = refs[:12]
    slot_up, slot_down, send_up, recv_up, send_down, recv_down = refs[12:]
    q, j, f = pl.program_id(0), pl.program_id(1), pl.program_id(2)
    tiles = FF // TILE
    me = lax.axis_index("expert")
    total = upstream.shape[0]
    piece, rows = total // parts, total // 2
    part = piece // 2
    own_half = jnp.where(me < parts // 2, 1 - q, q)
    begin = pl.multiple_of(own_half * rows, rows)
    here = pl.ds(begin, rows)
    inner = j * tiles + f
    step = q * EXP_DEV * tiles + inner
    slot_now = lax.rem(step, 2)

    def fetches(at):
        half = at // (EXP_DEV * tiles)
        first = pl.multiple_of(jnp.where(me < parts // 2, 1 - half, half) * rows, rows)
        source = (
            lax.rem(at // tiles, EXP_DEV),
            pl.ds(first, rows),
            pl.ds(pl.multiple_of(lax.rem(at, tiles) * TILE, TILE), TILE),
        )
        slot = lax.rem(at, 2)
        return (
            pltpu.make_async_copy(gate_hbm.at[source], gates.at[slot], kept_sems.at[slot, 0]),
            pltpu.make_async_copy(up_hbm.at[source], ups.at[slot], kept_sems.at[slot, 1]),
        )

    def hop(ref, slot, at, n, to, send, recv):
        return pltpu.make_async_remote_copy(
            src_ref=ref,
            dst_ref=slot.at[at, n * part : (n + 1) * part],
            send_sem=send.at[at, n],
            recv_sem=recv.at[at, n],
            device_id={"expert": to},
            device_id_type=MESH,
        )

    def landed(slot, at, n, send, recv):
        return hop(slot.at[at, n * part : (n + 1) * part], slot, at, n, me, send, recv)

    streams = ((True, slot_up, send_up, recv_up), (False, slot_down, send_down, recv_down))

    def where_to(up, at):
        line = me if up else parts - 1 - me
        dest_line = parts - 1 - at + line
        return line, (me + 1 if up else me - 1), (dest_line if up else parts - 1 - dest_line)

    def send_first(up, slot, send, recv, at):
        line, to, dest = where_to(up, at)

        @pl.when(line == 0)
        def _():
            for n in range(2):
                there = pl.ds(pl.multiple_of(dest * piece + n * part, part), part)
                hop(terms.at[there], slot, at, n, to, send, recv).start()

    def pass_on(up, slot, send, recv, at, n):
        _, to, dest = where_to(up, at)
        landed(slot, at - 1, n, send, recv).wait_recv()
        chunk = 16

        @pl.loop(0, part // chunk)
        def _(r):
            local = pl.ds(pl.multiple_of(n * part + r * chunk, chunk), chunk)
            there = pl.ds(pl.multiple_of(dest * piece + n * part + r * chunk, chunk), chunk)
            both = slot[at - 1, local, :].astype(jnp.float32) + terms[there, :].astype(jnp.float32)
            slot[at - 1, local, :] = both.astype(jnp.bfloat16)

        hop(slot.at[at - 1, n * part : (n + 1) * part], slot, at, n, to, send, recv).start()

    @pl.when(step == 0)
    def _():
        greet_line(me, parts)
        copies = []
        for shift in range(parts):
            there = row_chunk(lax.rem(me + parts - shift, parts), piece)
            copies.append(pltpu.make_async_copy(blocks[shift], upstream.at[there], load_sems.at[shift]))
        for copy in copies:
            copy.start()
        for copy in fetches(step):
            copy.start()
        lift_grad_ref[...] = jnp.zeros_like(lift_grad_ref)
        for copy in copies:
            copy.wait()

    @pl.when(step + 1 < 2 * EXP_DEV * tiles)
    def _():
        for copy in fetches(step + 1):
            copy.start()

    @pl.when(inner == 0)
    def _():
        slot_acc[...] = jnp.zeros_like(slot_acc)
        rank_acc[...] = jnp.zeros_like(rank_acc)
        gate_acc[...] = jnp.zeros_like(gate_acc)

    lift_gate, lift_up = own_lift(lift_gate_ref, j), own_lift(lift_up_ref, j)
    for copy in fetches(step):
        copy.wait()
    mine = lax.broadcasted_iota(jnp.int32, (rows, LANES), 1) == me * EXP_DEV + j
    column = jnp.sum(jnp.where(mine, gates_ref[here, :].astype(jnp.float32), 0.0), axis=1, keepdims=True)
    raw = dot_right(upstream[here, :], out_ref[0])
    gate = gates[slot_now].astype(jnp.float32)
    up_part = ups[slot_now].astype(jnp.float32)
    sigma = jax.nn.sigmoid(gate)
    silu = gate * sigma
    gate_grad = jnp.sum(raw * (silu * up_part), axis=1, keepdims=True)
    back = raw * column
    to_gate = (back * up_part * (sigma + silu * (1.0 - sigma))).astype(jnp.bfloat16)
    to_up = (back * silu).astype(jnp.bfloat16)
    slot_acc[...] += dot_right(to_gate, in_gate_ref[0]) + dot_right(to_up, in_up_ref[0])
    rank_acc[...] += dot_right(to_gate, lift_gate) + dot_right(to_up, lift_up)
    gate_acc[...] += jnp.where(mine, gate_grad, 0.0)
    ranks = ranks_ref[here, :]
    for side, grad in enumerate((to_gate, to_up)):
        lanes = pl.ds(pl.multiple_of(side * FF + f * TILE, TILE), TILE)
        lift_grad_ref[:, lanes] += jnp.where(
            lax.broadcasted_iota(jnp.int32, (LANES, TILE), 0) // RANK == j, dot_left(ranks, grad), 0.0
        )

    @pl.when(inner == EXP_DEV * tiles - 1)
    def _():
        size = rows // 4

        @pl.loop(0, 4)
        def _(b):
            local = row_chunk(b, size)
            there = pl.ds(pl.multiple_of(begin + b * size, size), size)
            rank_low = rank_acc[local, :].astype(jnp.bfloat16)
            rank_ref[there, :] = rank_low
            slot = slot_acc[local, :] + dot_plain(rank_low, down_ref[...])
            terms[there, :D] = slot.astype(jnp.bfloat16)
            wide = gate_acc[local, :]
            high = wide.astype(jnp.bfloat16).astype(jnp.float32)
            both = high + pltpu.roll(wide - high, LANES // 2, 1)
            terms[there, D:] = both.astype(jnp.bfloat16)

    @pl.when((q == 0) & (inner == EXP_DEV * tiles - 1))
    def _():
        for at in range(parts // 2):
            for stream in streams:
                send_first(*stream, at)

    @pl.when((q == 1) & (inner == EXP_DEV * tiles - 3))
    def _():
        for stream in streams:
            line, _, _ = where_to(stream[0], 1)

            @pl.when(line == 1)
            def _(stream=stream):
                for n in range(2):
                    pass_on(*stream, 1, n)

    @pl.when((q == 1) & (inner == EXP_DEV * tiles - 1))
    def _():
        for at in range(1, parts - 1):
            if at >= parts // 2:
                for stream in streams:
                    send_first(*stream, at)
            for n in range(2):
                for stream in streams:
                    line, _, _ = where_to(stream[0], at)
                    early = (line == 1) & (at == 1)

                    @pl.when((line > 0) & (at >= line) & (line < parts - 1) & jnp.logical_not(early))
                    def _(stream=stream, at=at, n=n):
                        pass_on(*stream, at, n)

        chunk = 16
        last = parts - 2

        @pl.loop(0, piece // chunk)
        def _(r):
            local = row_chunk(r, chunk)
            there = pl.ds(pl.multiple_of(me * piece + r * chunk, chunk), chunk)
            sum_ref[local, :] = terms[there, :].astype(jnp.float32)

        for n in range(2):
            for up, slot, send, recv in streams:
                line, _, _ = where_to(up, 0)

                @pl.when(line > 0)
                def _(slot=slot, n=n, send=send, recv=recv):
                    landed(slot, last, n, send, recv).wait_recv()

                    @pl.loop(0, part // chunk)
                    def _(r):
                        local = pl.ds(pl.multiple_of(n * part + r * chunk, chunk), chunk)
                        sum_ref[local, :] = sum_ref[local, :] + slot[last, local, :].astype(jnp.float32)

        for up, slot, send, recv in streams:
            line, _, _ = where_to(up, 0)
            for at in range(parts - 1):
                for n in range(2):

                    @pl.when((at >= line) & (line < parts - 1))
                    def _(slot=slot, at=at, n=n, send=send, recv=recv):
                        landed(slot, at, n, send, recv).wait_send()


def experts_backward(blocks, gates, ranks, down, lift, matrix_in, matrix_out, gate, up, cid):
    total, parts = gates.shape[0], len(blocks)
    rows, piece, tiles = total // 2, total // parts, FF // TILE
    once = dict(pipeline_mode=pl.Buffered(1))
    sem = pltpu.SemaphoreType.DMA
    weights = [
        pl.BlockSpec((LANES, TILE), lambda q, j, f: (0, f)),
        pl.BlockSpec((LANES, TILE), lambda q, j, f: (0, f + tiles)),
        pl.BlockSpec((1, D, TILE), lambda q, j, f: (j, 0, f)),
        pl.BlockSpec((1, D, TILE), lambda q, j, f: (j, 0, f + tiles)),
        pl.BlockSpec((1, TILE, D), lambda q, j, f: (j, f, 0)),
    ]
    whole = lambda q, j, f: (0, 0)
    return pl.pallas_call(
        functools.partial(backward_kernel, parts),
        grid=(2, EXP_DEV, tiles),
        in_specs=[VMEM] * 3 + weights + [ANY] * (2 + parts),
        out_specs=[
            pl.BlockSpec((piece, D + LANES), whole, **once),
            pl.BlockSpec((total, LANES), whole, **once),
            pl.BlockSpec((LANES, 2 * FF), whole, **once),
        ],
        out_shape=[
            jax.ShapeDtypeStruct((piece, D + LANES), jnp.float32),
            jax.ShapeDtypeStruct((total, LANES), jnp.bfloat16),
            jax.ShapeDtypeStruct((LANES, 2 * FF), jnp.float32),
        ],
        scratch_shapes=[
            pltpu.VMEM((total, D), jnp.bfloat16),
            pltpu.VMEM((rows, D), jnp.float32),
            pltpu.VMEM((rows, LANES), jnp.float32),
            pltpu.VMEM((rows, LANES), jnp.float32),
            pltpu.VMEM((total, D + LANES), jnp.bfloat16),
            pltpu.VMEM((2, rows, TILE), jnp.bfloat16),
            pltpu.VMEM((2, rows, TILE), jnp.bfloat16),
            sem((parts,)),
            sem((2, 2)),
            pltpu.VMEM((parts - 1, piece, D + LANES), jnp.bfloat16),
            pltpu.VMEM((parts - 1, piece, D + LANES), jnp.bfloat16),
        ]
        + [sem((parts - 1, 2))] * 4,
        compiler_params=pltpu.CompilerParams(
            dimension_semantics=("arbitrary",) * 3,
            vmem_limit_bytes=60 * 1024 * 1024,
            collective_id=cid,
            has_side_effects=True,
        ),
        cost_estimate=pl.CostEstimate(
            flops=32 * EXP_DEV * total * D * FF,
            bytes_accessed=EXP_DEV * 6 * D * FF + 8 * total * D,
            transcendentals=EXP_DEV * total * FF,
        ),
        name="experts_backward",
    )(gates, ranks, down, lift, lift, matrix_in, matrix_in, matrix_out, gate, up, *blocks)


def pick_kernel(experts, chosen_ref, small_ref, picked_ref, router_ref, gain_ref):
    row = lax.broadcasted_iota(jnp.int32, (LANES, LANES), 0)
    same = row == lax.broadcasted_iota(jnp.int32, (LANES, LANES), 1)
    every = same.astype(jnp.float32).astype(jnp.bfloat16)
    router = (same & (row < experts)).astype(jnp.float32).astype(jnp.bfloat16)
    gain_row = lax.broadcasted_iota(jnp.int32, (8, LANES), 0) + 64
    gain = gain_row == lax.broadcasted_iota(jnp.int32, (8, LANES), 1)
    picked_ref[...] = dot_right(every, chosen_ref[...]).astype(jnp.bfloat16)
    router_ref[...] = dot_right(router, small_ref[...]).astype(jnp.bfloat16)
    gain_ref[...] = dot_right(gain.astype(jnp.float32).astype(jnp.bfloat16), small_ref[...])


def pick_rows(chosen, dense, at, experts):
    return pl.pallas_call(
        functools.partial(pick_kernel, experts),
        grid=(1,),
        in_specs=[VMEM, pl.BlockSpec((D, LANES), lambda i: (0, at // LANES))],
        out_specs=[all_of(LANES, D), all_of(LANES, D), all_of(8, D)],
        out_shape=[
            jax.ShapeDtypeStruct((LANES, D), jnp.bfloat16),
            jax.ShapeDtypeStruct((LANES, D), jnp.bfloat16),
            jax.ShapeDtypeStruct((8, D), jnp.float32),
        ],
        name="pick_rows",
    )(chosen, dense)


def first_kernel(query_ref, key_ref, value_ref, rank_ref, down_ref, *refs):
    weights, out_ref = refs[:3], refs[3]
    total = dot_right(query_ref[...], weights[0][...]) + dot_right(key_ref[...], weights[1][...])
    total = total + dot_right(value_ref[...], weights[2][...]) + dot_plain(rank_ref[...], down_ref[...])
    out_ref[...] = total.astype(jnp.bfloat16)


def first_products(backs, ranks, down, dense):
    total, width = backs[0].shape
    tile = 512
    weights = [
        pl.BlockSpec((tile, width), lambda i, part=part: (i, D // width + part)) for part in range(3)
    ]
    return pl.pallas_call(
        first_kernel,
        grid=(D // tile,),
        in_specs=[VMEM] * 4 + [pl.BlockSpec((RANK, tile), lambda i: (0, i))] + weights,
        out_specs=pl.BlockSpec((total, tile), lambda i: (0, i)),
        out_shape=jax.ShapeDtypeStruct((total, D), jnp.bfloat16),
        compiler_params=pltpu.CompilerParams(vmem_limit_bytes=48 * 1024 * 1024),
        cost_estimate=pl.CostEstimate(
            flops=6 * total * width * D, bytes_accessed=6 * width * D + 2 * total * D, transcendentals=0
        ),
        name="first_products",
    )(*backs, ranks, down, dense, dense, dense)


def sublayer_params():
    return pltpu.CompilerParams(
        dimension_semantics=("arbitrary",), vmem_limit_bytes=56 * 1024 * 1024
    )


def all_of(*shape):
    return pl.BlockSpec(shape, lambda i: (0,) * len(shape))


def qkv_kernel(tokens_ref, gain_ref, down_ref, lift_ref, weight_ref, normed_ref, rank_ref, qkv_ref):
    @pl.when(pl.program_id(0) == 0)
    def _():
        rows = tokens_ref.shape[0] // 4

        @pl.loop(0, 4)
        def _(b):
            here = row_chunk(b, rows)
            values = tokens_ref[here, :].astype(jnp.float32)
            normed = (values * norm_inverse(values) * gain_ref[...]).astype(jnp.bfloat16)
            normed_ref[here, :] = normed
            rank_ref[here, :] = dot_right(normed, down_ref[...]).astype(jnp.bfloat16)

    total = dot_plain(normed_ref[...], weight_ref[...]) + dot_plain(rank_ref[...], lift_ref[...])
    qkv_ref[...] = total.astype(jnp.bfloat16)


def project_qkv(tokens, gain, down, lift, dense):
    total, width = tokens.shape[0], lift.shape[1] // 3
    return pl.pallas_call(
        qkv_kernel,
        grid=(3,),
        in_specs=[
            VMEM,
            VMEM,
            VMEM,
            pl.BlockSpec((RANK, width), lambda i: (0, i)),
            pl.BlockSpec((D, width), lambda i: (0, D // width + i)),
        ],
        out_specs=[
            all_of(total, D),
            all_of(total, RANK),
            pl.BlockSpec((total, width), lambda i: (0, i)),
        ],
        out_shape=[
            jax.ShapeDtypeStruct((total, D), jnp.bfloat16),
            jax.ShapeDtypeStruct((total, RANK), jnp.bfloat16),
            jax.ShapeDtypeStruct((total, 3 * width), jnp.bfloat16),
        ],
        compiler_params=sublayer_params(),
        cost_estimate=pl.CostEstimate(
            flops=6 * total * D * width, bytes_accessed=6 * D * width + 8 * total * D, transcendentals=0
        ),
        name="project_qkv",
    )(tokens, gain, down, lift, dense)


def middle_kernel(
    experts,
    mixed_ref,
    tokens_ref,
    down_mix_ref,
    lift_mix_ref,
    gain_ref,
    down_route_ref,
    router_ref,
    lift_route_ref,
    routed_ref,
    out_ref,
    middle_ref,
    rank_mix_ref,
    inverse_ref,
    second_ref,
    rank_route_ref,
    probs_ref,
    gates_ref,
):
    i = pl.program_id(0)
    tile = out_ref.shape[1]

    @pl.when(i == 0)
    def _():
        rank_mix_ref[...] = dot_right(mixed_ref[...], down_mix_ref[...]).astype(jnp.bfloat16)

    here = pl.ds(pl.multiple_of(i * tile, tile), tile)
    branch = dot_plain(mixed_ref[...], out_ref[...]) + dot_plain(rank_mix_ref[...], lift_mix_ref[...])
    middle_ref[:, here] = tokens_ref[...].astype(jnp.float32) + branch

    @pl.when(i == D // tile - 1)
    def _():
        middle = middle_ref[...]
        inverse = norm_inverse(middle)
        inverse_ref[...] = inverse
        second = (middle * inverse * gain_ref[...]).astype(jnp.bfloat16)
        second_ref[...] = second
        rank_route = dot_right(second, down_route_ref[...]).astype(jnp.bfloat16)
        rank_route_ref[...] = rank_route
        logits = dot_right(second, router_ref[...]) + dot_plain(rank_route, lift_route_ref[...])
        lane = lax.broadcasted_iota(jnp.int32, logits.shape, 1)
        logits = jnp.where(lane < experts, logits, MASKED)
        exped = jnp.exp(logits - jnp.max(logits, axis=1, keepdims=True))
        probs = exped / jnp.sum(exped, axis=1, keepdims=True)
        probs_ref[...] = probs
        gates_ref[...] = (probs * routed_ref[...]).astype(jnp.bfloat16)


def finish_attention(experts, mixed, tokens, down_mix, lift_mix, gain, down_route, router, lift_route, routed, out_matrix):
    piece, tile = tokens.shape[0], 512
    column = lambda i: (0, i)
    return pl.pallas_call(
        functools.partial(middle_kernel, experts),
        grid=(D // tile,),
        in_specs=[
            VMEM,
            pl.BlockSpec((piece, tile), column),
            VMEM,
            pl.BlockSpec((RANK, tile), column),
            VMEM,
            VMEM,
            VMEM,
            VMEM,
            VMEM,
            pl.BlockSpec((D, tile), column),
        ],
        out_specs=[
            all_of(piece, D),
            all_of(piece, RANK),
            all_of(piece, 1),
            all_of(piece, D),
            all_of(piece, RANK),
            all_of(piece, LANES),
            all_of(piece, LANES),
        ],
        out_shape=[
            jax.ShapeDtypeStruct((piece, D), jnp.float32),
            jax.ShapeDtypeStruct((piece, RANK), jnp.bfloat16),
            jax.ShapeDtypeStruct((piece, 1), jnp.float32),
            jax.ShapeDtypeStruct((piece, D), jnp.bfloat16),
            jax.ShapeDtypeStruct((piece, RANK), jnp.bfloat16),
            jax.ShapeDtypeStruct((piece, LANES), jnp.float32),
            jax.ShapeDtypeStruct((piece, LANES), jnp.bfloat16),
        ],
        compiler_params=sublayer_params(),
        cost_estimate=pl.CostEstimate(
            flops=2 * piece * D * D, bytes_accessed=2 * D * D + 12 * piece * D, transcendentals=piece * LANES
        ),
        name="finish_attention",
    )(mixed, tokens, down_mix, lift_mix, gain, down_route, router, lift_route, routed, out_matrix)


def middle_back_kernel(
    slot_ref,
    probs_ref,
    routed_ref,
    middle_ref,
    inverse_ref,
    cotangent_ref,
    gain_ref,
    router_ref,
    lift_route_ref,
    down_route_ref,
    lift_mix_ref,
    down_mix_ref,
    out_ref,
    mixed_ref,
    grad_ref,
    branch_ref,
    logit_ref,
    rank_route_ref,
    rank_mix_ref,
):
    @pl.when(pl.program_id(0) == 0)
    def _():
        parts = slot_ref[:, D:]
        prob_grad = (parts + pltpu.roll(parts, LANES // 2, 1)) * routed_ref[...]
        probs = probs_ref[...]
        logit_grad = probs * (prob_grad - jnp.sum(probs * prob_grad, axis=1, keepdims=True))
        logit_grad = logit_grad.astype(jnp.bfloat16)
        logit_ref[...] = logit_grad
        rank_route_grad = dot_right(logit_grad, lift_route_ref[...]).astype(jnp.bfloat16)
        rank_route_ref[...] = rank_route_grad
        upstream = slot_ref[:, :D] + dot_plain(logit_grad, router_ref[...])
        upstream = upstream + dot_plain(rank_route_grad, down_route_ref[...])
        middle_grad = cotangent_ref[...].astype(jnp.float32) + norm_backward(
            middle_ref[...], inverse_ref[...], gain_ref[...], upstream
        )
        grad_ref[...] = middle_grad
        branch_ref[...] = middle_grad.astype(jnp.bfloat16)
        rank_mix_ref[...] = dot_right(branch_ref[...], lift_mix_ref[...]).astype(jnp.bfloat16)

    mixed = dot_right(branch_ref[...], out_ref[...]) + dot_plain(rank_mix_ref[...], down_mix_ref[...])
    mixed_ref[...] = mixed.astype(jnp.bfloat16)


def middle_backward(
    width, slot, probs, routed, middle, inverse, cotangent, gain, router, lift_route, down_route, lift_mix, down_mix, out_matrix
):
    piece = middle.shape[0]
    return pl.pallas_call(
        middle_back_kernel,
        grid=(D // width,),
        in_specs=[VMEM] * 11
        + [
            pl.BlockSpec((RANK, width), lambda i: (0, i)),
            pl.BlockSpec((width, D), lambda i: (i, 0)),
        ],
        out_specs=[
            pl.BlockSpec((piece, width), lambda i: (i, 0)),
            all_of(piece, D),
            all_of(piece, D),
            all_of(piece, LANES),
            all_of(piece, RANK),
            all_of(piece, RANK),
        ],
        out_shape=[
            jax.ShapeDtypeStruct((piece * D // width, width), jnp.bfloat16),
            jax.ShapeDtypeStruct((piece, D), jnp.float32),
            jax.ShapeDtypeStruct((piece, D), jnp.bfloat16),
            jax.ShapeDtypeStruct((piece, LANES), jnp.bfloat16),
            jax.ShapeDtypeStruct((piece, RANK), jnp.bfloat16),
            jax.ShapeDtypeStruct((piece, RANK), jnp.bfloat16),
        ],
        compiler_params=sublayer_params(),
        cost_estimate=pl.CostEstimate(
            flops=2 * piece * D * D, bytes_accessed=2 * D * D + 24 * piece * D, transcendentals=0
        ),
        name="middle_backward",
    )(slot, probs, routed, middle, inverse, cotangent, gain, router, lift_route, down_route, lift_mix, down_mix, out_matrix)


def norm_inverse(values):
    return lax.rsqrt(jnp.mean(values * values, axis=-1, keepdims=True) + EPSILON)


def norm_backward(values, inverse, gain_row, upstream):
    scaled = upstream * gain_row
    return inverse * scaled - values * inverse**3 * jnp.mean(
        scaled * values, axis=-1, keepdims=True
    )


def segments_of(lengths, places):
    upto = jnp.arange(lengths.shape[0])
    limits = PROMPT + jnp.sum(
        jnp.where(upto[:, None] <= upto[None, :], lengths[:, None], 0), axis=0
    )
    passed = jnp.sum((places[:, None] >= limits[None, :]).astype(jnp.int32), axis=1)
    return jnp.where(places < PROMPT, 0, 1 + passed)


def body(
    tokens,
    cotangent,
    norm_gains,
    qkv_weight,
    out_weight,
    router_weight,
    adapter_down,
    adapter_qkv,
    adapter_out,
    adapter_router,
    expert_input,
    expert_output,
    expert_down,
    expert_lift,
    routes,
    adapter_ids,
    cont_lengths,
):
    low = jnp.bfloat16
    piece = tokens.shape[0]
    parts = lax.axis_size("expert")
    groups = lax.axis_size("dp")
    ways = parts * groups
    me = lax.axis_index("expert")
    total = parts * piece
    experts = EXP_DEV * parts
    width = D // parts
    share = D // ways
    route_rows = ADAPTERS * RANK // ways
    adapter = adapter_ids[0]

    matrix_out = lax.all_gather(expert_output, "dp", axis=1, tiled=True)

    group_ids = lax.all_gather(adapter_ids, "dp", axis=0, tiled=True)
    hot = group_ids[:, None] == jnp.arange(ADAPTERS, dtype=jnp.int32)
    group_hot = hot.astype(jnp.float32)
    adapter_cols = expert_lift.shape[3]
    pairs = jnp.stack([expert_down.transpose(0, 2, 3, 1), expert_lift])
    pairs = pairs.transpose(2, 0, 1, 3, 4).reshape(ADAPTERS, 2 * EXP_DEV * RANK * adapter_cols)
    pairs = dot_plain(hot.astype(low), pairs).astype(low)
    pairs = lax.all_to_all(
        pairs.reshape(groups, 2 * EXP_DEV * RANK, adapter_cols), "dp", split_axis=0, concat_axis=0, tiled=True
    )
    pairs = pairs.reshape(groups, 2, EXP_DEV * RANK, adapter_cols).transpose(1, 2, 0, 3)
    pairs = pairs.reshape(2, EXP_DEV * RANK, D)
    pairs = jnp.pad(pairs, ((0, 0), (0, LANES - EXP_DEV * RANK), (0, 0)))

    def columns(array, upto):
        return jnp.pad(array, ((0, share - array.shape[0]), (0, upto - array.shape[1])))

    adapters = jnp.concatenate(
        [
            adapter_down.reshape(share, ADAPTERS * 3 * RANK),
            adapter_out.reshape(ADAPTERS * RANK, share).T,
            adapter_qkv.reshape(ADAPTERS * RANK, 3, share).transpose(2, 1, 0).reshape(share, 3 * LANES),
        ],
        axis=1,
    )
    row = jnp.arange(LANES, dtype=jnp.int32)[None, :]
    ids = group_ids[:, None]
    wanted = jnp.where(
        row < 48,
        ids * 48 + row,
        jnp.where(
            row < 64,
            384 + ids * RANK + row - 48,
            jnp.where(row < 112, 512 + LANES * ((row - 64) // RANK) + ids * RANK + (row - 64) % RANK, -1),
        ),
    ).reshape(1, groups * LANES)
    chosen = jnp.arange(adapters.shape[1], dtype=jnp.int32)[:, None] == wanted
    chosen = dot_plain(adapters, chosen.astype(low)).astype(low)

    qkv_blocks = (
        qkv_weight.reshape(share, 3, parts, width).transpose(2, 0, 1, 3).reshape(parts * share, 3 * width)
    )
    small = jnp.concatenate(
        [columns(router_weight, 32), columns(adapter_router, 32), columns(norm_gains.T, 64)], axis=1
    )
    dense_line, chosen_line = gather_weights(qkv_blocks, out_weight, small, chosen, 0)
    chosen_all = lax.all_to_all(
        chosen_line.reshape(parts * share, groups, LANES).transpose(1, 0, 2),
        "dp",
        split_axis=0,
        concat_axis=0,
        tiled=True,
    ).reshape(D, LANES)
    def shifted(array, by):
        return lax.ppermute(array, "expert", [(i, (i + by) % parts) for i in range(parts)])

    there = chosen_line[0, 0]
    late_shifts = list(range(2, parts))
    moved = {1: shifted(jnp.where(there == there, cotangent, 0), 1)}
    dense_line, expert_input, matrix_out, chosen_all, pairs, moved[1] = lax.optimization_barrier(
        (dense_line, expert_input, matrix_out, chosen_all, pairs, moved[1])
    )
    dense_all = lax.all_gather(dense_line, "dp", axis=0, tiled=True)
    (tokens_all,) = line_gather([tokens], 1, 2)
    matrix_in = lax.all_gather(expert_input, "dp", axis=1, tiled=True)
    small_at = D + 3 * width

    picked, router_rows, gain_rows = pick_rows(chosen_all, dense_all, small_at, experts)
    down_query, down_mix, down_route = picked[:16], picked[16:32], picked[32:48]
    lift_mix = picked[48:64]
    lift_query = (
        picked[64:112].reshape(3, RANK, ways, share).transpose(1, 2, 0, 3).reshape(RANK, 3, parts, width)
    )
    lift_query = lax.dynamic_index_in_dim(lift_query, me, 2, keepdims=False).reshape(RANK, 3 * width)
    by_owner = dense_all[:, small_at : small_at + LANES].reshape(ways, share, LANES)
    lift_route = lax.dynamic_slice_in_dim(
        by_owner[:, :route_rows, 32 : 32 + experts].reshape(ADAPTERS * RANK, experts),
        adapter * RANK,
        RANK,
        0,
    )
    lift_route = jnp.pad(lift_route, ((0, 0), (0, LANES - experts)))
    routed = jnp.any(routes[:, :, None] == jnp.arange(LANES, dtype=jnp.int32), axis=1).astype(jnp.float32)
    normed_low, rank_query, qkv_low = project_qkv(
        tokens_all, gain_rows[0:1], down_query, lift_query, dense_all
    )
    segments = segments_of(cont_lengths[0], jnp.arange(total, dtype=jnp.int32))
    segment_column, segment_row = segments[:, None], segments[None, :]
    mixed_low, log_mass = run_attention(segment_column, segment_row, qkv_low, 3)

    middle, rank_mix, inverse_second, second_low, rank_route, router_probs, gates = finish_attention(
        experts,
        mixed_low,
        tokens,
        down_mix,
        lift_mix,
        gain_rows[1:2],
        down_route,
        router_rows,
        lift_route,
        routed,
        dense_all,
    )
    second_all, gates_all = line_gather([second_low, gates], 4, 2)

    late, second_all = lax.optimization_barrier((cotangent, second_all))
    moved.update({s: shifted(late, s) for s in late_shifts})
    cotangents = [cotangent] + [moved[s] for s in range(1, parts)]
    output_left, output_right, ranks, gate, up = experts_forward(
        second_all, gates_all, pairs[0], pairs[1], matrix_in, matrix_out
    )
    output_left = lax.psum_scatter(output_left, "expert", scatter_dimension=0, tiled=True)
    slot_sum, rank_expert_grad, lift_expert_grad = experts_backward(
        cotangents, gates_all, ranks, pairs[0], pairs[1], matrix_in, matrix_out, gate, up, 5
    )
    output_left, output_right, slot_sum = lax.optimization_barrier(
        (output_left, output_right, slot_sum)
    )
    output_right = lax.psum_scatter(output_right, "expert", scatter_dimension=0, tiled=True)
    output_sum = jnp.concatenate([output_left, output_right], axis=1)
    layer_output = (middle + output_sum.astype(jnp.float32)).astype(low)

    lift_sent = lift_expert_grad[: EXP_DEV * RANK]
    down_sent = dot_left(rank_expert_grad[:, : EXP_DEV * RANK], second_all)
    expert_sent = (
        jnp.concatenate([lift_sent, down_sent], axis=0)
        .astype(low)
        .reshape(2 * EXP_DEV * RANK, groups, -1)
        .transpose(1, 0, 2)
    )
    expert_got = lax.all_to_all(expert_sent, "dp", split_axis=0, concat_axis=0, tiled=True)
    by_adapter = jnp.einsum(
        "ga,gkc->akc", group_hot, expert_got.astype(jnp.float32), precision=lax.Precision.HIGHEST
    ).reshape(ADAPTERS, 2, EXP_DEV, RANK, -1)
    explift_grad = by_adapter[:, 0].transpose(1, 0, 2, 3)
    expdown_grad = by_adapter[:, 1].transpose(1, 3, 0, 2)

    mixed_grad, middle_grad, branch_grad, logit_grad, rank_route_grad, rank_mix_grad = middle_backward(
        width,
        slot_sum,
        router_probs,
        routed,
        middle,
        inverse_second,
        cotangent,
        gain_rows[1:2],
        router_rows,
        lift_route,
        down_route,
        lift_mix,
        down_mix,
        dense_all,
    )

    back_query, back_key, back_value = run_attention_back(
        segment_column, segment_row, qkv_low, mixed_grad, log_mass, 6
    )
    qkv_back = jnp.concatenate([back_query, back_key, back_value], axis=1)
    rank_query_grad = dot_right(qkv_back, lift_query).astype(low)
    first_terms = first_products([back_query, back_key, back_value], rank_query_grad, down_query, dense_all)
    lift_query_grad = lax.dynamic_update_slice(
        jnp.zeros((RANK, 3, parts, width), jnp.float32),
        dot_left(rank_query, qkv_back).reshape(RANK, 3, 1, width),
        (0, 0, me, 0),
    )
    downs = jnp.concatenate(
        [
            dot_left(rank_query_grad, normed_low),
            dot_left(rank_mix_grad, mixed_low),
            dot_left(rank_route_grad, second_low),
            dot_left(rank_mix, branch_grad),
        ]
    )
    owned = jnp.concatenate(
        [
            downs.reshape(4 * RANK, ways, share).transpose(1, 0, 2).reshape(ways, -1),
            lift_query_grad.reshape(RANK, ways, 3 * share).transpose(1, 0, 2).reshape(ways, -1),
            jnp.broadcast_to(dot_left(rank_route, logit_grad)[:, :experts].reshape(1, -1), (ways, RANK * experts)),
        ],
        axis=1,
    ).astype(low)
    first_grad = lax.psum_scatter(first_terms, "expert", scatter_dimension=0, tiled=True).astype(jnp.float32)
    got = lax.all_to_all(owned, ("dp", "expert"), split_axis=0, concat_axis=0, tiled=True)
    inputs = tokens.astype(jnp.float32)
    inverse_first = norm_inverse(inputs)
    input_grad = (
        middle_grad + norm_backward(inputs, inverse_first, gain_rows[0:1], first_grad)
    ).astype(low)
    summed = jnp.einsum(
        "ga,gek->ak",
        group_hot,
        got.astype(jnp.float32).reshape(groups, parts, -1),
        precision=lax.Precision.HIGHEST,
    )
    n_down, n_qkv = 4 * RANK * share, 3 * RANK * share
    downs = summed[:, :n_down].reshape(ADAPTERS, 4, RANK, share)
    down_grad = downs[:, :3].transpose(3, 0, 1, 2)
    proj_grad = downs[:, 3]
    qkv_grad = summed[:, n_down : n_down + n_qkv].reshape(ADAPTERS, RANK, 3 * share)
    router_grad = lax.dynamic_slice_in_dim(
        summed[:, n_down + n_qkv :].reshape(ADAPTERS * RANK, experts),
        (lax.axis_index("dp") * parts + me) * route_rows,
        route_rows,
        0,
    )
    return (
        layer_output,
        input_grad,
        down_grad,
        qkv_grad,
        proj_grad,
        router_grad,
        expdown_grad,
        explift_grad,
    )


def solution(mesh):
    placed = (
        P(("dp", "expert"), None),
        P(("dp", "expert"), None),
        P(None, ("dp", "expert")),
        P(("dp", "expert"), None),
        P(("dp", "expert"), None),
        P(("dp", "expert"), None),
        P(("dp", "expert"), None, None, None),
        P(None, None, ("dp", "expert")),
        P(None, None, ("dp", "expert")),
        P(("dp", "expert"), None),
        P("expert", "dp", None),
        P("expert", "dp", None),
        P("expert", "dp", None, None),
        P("expert", None, None, "dp"),
        P(("dp", "expert"), None),
        P("dp"),
        P("dp", None),
    )
    return jax.shard_map(
        body,
        mesh=mesh,
        in_specs=placed,
        out_specs=(
            P(("dp", "expert"), None),
            P(("dp", "expert"), None),
            P(("dp", "expert"), None, None, None),
            P(None, None, ("dp", "expert")),
            P(None, None, ("dp", "expert")),
            P(("dp", "expert"), None),
            P("expert", "dp", None, None),
            P("expert", None, None, "dp"),
        ),
        check_vma=False,
    )
```
